128 devices in a mesh: along: 32 (over x, y, z_lo), cross: 4 (over z_hi, core).
Axes of the slice: x: 4, y: 4, z: 4 (z_hi: 2, z_lo: 2; z = z_hi * 2 + z_lo), core: 2. Of those that a mesh axis runs over, the one named last changes fastest.
Arguments:
- adjoint: float32 [32, 4, 64, 8192], P(None, None, 'cross', 'along'), may hold values from -6 to 6
- flow: float32 [32, 2, 64, 8192], P(None, None, 'cross', 'along'), may hold values from -0.4 to 0.4
- land_mask: int32 [32, 64, 8192], P(None, 'cross', 'along'), may hold values 0 or 1
- mixing: float32 [31, 64, 8192], P(None, 'cross', 'along'), may hold values from 0.05 to 2
- seam_code: int32 [32], replicated, may hold values from 0 to 3
- obs_misfit: bfloat16 [524288, 128], P(('along', 'cross')), may hold values from -6 to 6
- obs_owner: int32 [524288, 1], P(('along', 'cross')), may hold values from 0 to 127; in each aligned block of 4096 rows (0 to 4095, 4096 to 8191, ...) at most 64 rows name the same one
- obs_cell: int32 [524288], P(('along', 'cross')), may hold values from 0 to 4095
Outputs:
- adjoint_next: float32 [32, 4, 64, 8192], P(None, None, 'cross', 'along')
The draws below stay inside these ranges and needn't reach their ends.
Inputs may be any that keep to these rules, and one draw needn't show every extreme that they name: `obs_owner`: each row names its owning tile as i * 4 + j for the tile at index i along and j across. Among the rows of one device no tile is named by more than 64 rows, a bound that some block reaches of them. `obs_cell`: the cell within the owning tile, as c * 256 + e for row c and column e of that tile. `seam_code`: A code k stands for the rotation R_k.
All inputs are finite; a program needn't handle non-finite values. No bound on the sum of `land_mask` on one device may be relied on, other than what follows from the above.
Results may differ from the reference program's by a relative error of at most 0.0025.
Values may be sent and summed in bfloat16 or wider, within the bound.
No kernel may reach another device: no remote copies, remote signals or barrier semaphores. Data moves between devices by JAX's collectives and lax.ppermute only.
A program may use at most 128 MiB of HBM per device.

```python
import math
import jax
import jax.numpy as jnp
import numpy as np
from jax import lax

ALONG_DEV = 256
CROSS_DEV = 16
LEVELS = 32
OBS_DEV = 4096
TILES_ALONG = 32
TILES_CROSS = 4
ALONG_ALL = 8192
CROSS_ALL = 64
OBS_ALL = 524288
CAPACITY = 64
DEVICES = 128


def plant(values, stream_key, least, high):
    index_at = [jax.random.randint(jax.random.fold_in(stream_key, axis), (), 0, length) for axis, length in enumerate(values.shape)]
    main_axis = values.shape.index(max(values.shape))
    next_to = index_at[:main_axis] + [(index_at[main_axis] + 1) % values.shape[main_axis]] + index_at[main_axis + 1:]
    return values.at[tuple(index_at)].set(least).at[tuple(next_to)].set(high)


def shard_levels(stream_key, dims, cuts, low, top_value):
    level, own = 1.0, jax.random.fold_in(stream_key, 6)
    for position, blocks in cuts:
        draws = jnp.exp(jax.random.uniform(jax.random.fold_in(own, position), (blocks,), jnp.float32, low / len(cuts), top_value / len(cuts)))
        level = level * jnp.repeat(draws, dims[position] // blocks).reshape([-1 if axis == position else 1 for axis in range(len(dims))])
    return level


def shared_out(own_key, own, number, rows, number_of, top, reach, lean):
    sequence = jax.random.permutation(own_key, number_of)
    packed, ordinary = load_shares(number_of, rows * top, reach, lean, True), load_shares(number_of, rows * top, reach, lean, False)
    places = jnp.arange(number_of)

    def named(lengths, offset_by):
        used = int((lengths > 0).sum())
        fixed = max(1, used // 4)
        moved = fixed + (places - fixed + offset_by * (used - fixed)) % max(1, number_of - fixed)
        return jnp.zeros((number_of,), jnp.int32).at[sequence[jnp.where(places < fixed, places, moved)]].set(jnp.asarray(lengths, jnp.int32))

    lengths = jnp.where(number % 4 == 0, named(packed, number // 4), named(ordinary, number - number // 4 - 1))
    mixed = jax.random.permutation(jax.random.fold_in(own, 3), number_of)
    giver, receiver = mixed[0:number_of // 2 * 2:2], mixed[1:number_of // 2 * 2:2]
    margin = jnp.minimum(lengths[giver] - 1, reach - lengths[receiver]) // 2
    margin = jnp.where((giver == sequence[0]) | (receiver == sequence[0]) | (lengths[receiver] == 0), 0, jnp.maximum(margin, 0))
    moved = jax.random.randint(jax.random.fold_in(own, 4), (number_of // 2,), 0, 1 << 20) % (margin + 1)
    lengths = lengths.at[giver].add(-moved).at[receiver].add(moved)
    labels = jnp.searchsorted(jnp.cumsum(lengths), jnp.arange(rows * top), side="right").astype(jnp.int32)
    table = labels.reshape(top, rows).T
    table = table[jax.random.permutation(jax.random.fold_in(own, 1), rows)]
    offset_by = jax.random.randint(jax.random.fold_in(own, 2), (rows, 1), 0, top)
    return jnp.take_along_axis(table, (jnp.arange(top)[None, :] + offset_by) % top, axis=1)


def load_shares(number_of, total, reach, slope, full):
    loads = [(1 << 20) // math.isqrt(standing ** slope) + 1 for standing in range(1, number_of + 1)]
    largest = reach if full else min(reach, max(-(-total // number_of), total * loads[0] // sum(loads)))
    least = 1 if total - largest >= number_of - 1 else 0
    counts, surplus = [largest] + [least] * (number_of - 1), total - largest - least * (number_of - 1)
    while surplus > 0:
        candidates = [i for i in range(1, number_of) if counts[i] < largest] or [i for i in range(1, number_of) if counts[i] < reach]
        mass, left = sum([loads[i] for i in candidates]), surplus
        for i in candidates:
            more = min(reach - counts[i], max(1, left * loads[i] // mass), surplus)
            counts[i] = counts[i] + more
            surplus = surplus - more
    return np.array(counts)


def noise(own_key, dims, spread, bound, cuts=(), kind=jnp.bfloat16):
    array = jax.random.normal(own_key, dims, jnp.float32) * spread
    if len(cuts) > 0:
        array = shard_levels(own_key, dims, cuts, -0.22, 0.18) * array
    return jnp.clip(array, min=-bound, max=bound).astype(kind)


def setup_inputs(seed: int = 0) -> dict:
    key_of = jax.random.split(jax.random.key(seed), 9)
    adjoint = noise(key_of[0], (LEVELS, 4, CROSS_ALL, ALONG_ALL), 1.0, 6.0, ((2, 4), (3, 32)), jnp.float32)
    flow = jnp.clip(jax.random.uniform(key_of[1], (LEVELS, 2, CROSS_ALL, ALONG_ALL), jnp.float32, -0.4, 0.4) * shard_levels(key_of[1], (LEVELS, 2, CROSS_ALL, ALONG_ALL), ((2, 4), (3, 32)), -0.4, 0.0), -0.4, 0.4)
    land_mask = plant((jax.random.randint(key_of[2], (LEVELS, CROSS_ALL, ALONG_ALL), 0, 10) < 9).astype(jnp.int32), jax.random.fold_in(key_of[2], 1), 0, 1)
    mixing = jnp.clip(jnp.exp(math.log(2.0) - 3.6888794 * jax.random.uniform(key_of[3], (LEVELS - 1, CROSS_ALL, ALONG_ALL), jnp.float32) ** shard_levels(key_of[3], (LEVELS - 1, CROSS_ALL, ALONG_ALL), ((1, 4), (2, 32)), -0.2, 0.2)), 0.05, 2.0)
    seam_code = plant(jax.random.randint(key_of[4], (TILES_ALONG,), 0, 4), jax.random.fold_in(key_of[4], 1), 0, 3).astype(jnp.int32)
    obs_misfit = noise(key_of[5], (OBS_ALL, 4 * LEVELS), 1.0, 6.0, ((0, 128),))
    obs_owner_keys = jax.random.split(jax.random.fold_in(key_of[6], 1), OBS_ALL // OBS_DEV)
    obs_owner_turns = jax.random.permutation(jax.random.fold_in(key_of[6], 3), OBS_ALL // OBS_DEV)
    obs_owner = jax.vmap(lambda own, number: shared_out(jax.random.fold_in(key_of[6], 2), own, number, OBS_DEV, DEVICES, 1, CAPACITY, 2))(obs_owner_keys, obs_owner_turns).reshape((OBS_ALL, 1))
    obs_cell = plant(jax.random.randint(key_of[7], (OBS_ALL,), 0, CROSS_DEV * ALONG_DEV), jax.random.fold_in(key_of[7], 1), 0, (CROSS_DEV * ALONG_DEV) - 1).astype(jnp.int32)
    return dict(adjoint=adjoint, flow=flow, land_mask=land_mask, mixing=mixing, seam_code=seam_code, obs_misfit=obs_misfit, obs_owner=obs_owner, obs_cell=obs_cell)


diffusion_rate = 0.15
coriolis = 0.3
couple_rate = 0.3
thermal_coef = 0.8
haline_coef = 0.6


def turn_vectors(field_stack, turn_code):
    cosine = (turn_code == 0).astype(jnp.float32) - (turn_code == 2).astype(jnp.float32)
    sine = (turn_code == 1).astype(jnp.float32) - (turn_code == 3).astype(jnp.float32)
    zonal = cosine * field_stack[:, 2] - sine * field_stack[:, 3]
    meridional = sine * field_stack[:, 2] + cosine * field_stack[:, 3]
    return jnp.stack([field_stack[:, 0], field_stack[:, 1], zonal, meridional], axis=1)


def transport(center, east_side, west_side, north_side, south_side, flow, mask_float):
    laplace = east_side + west_side + north_side + south_side - 4.0 * center
    along_diff = 0.5 * (east_side - west_side)
    cross_diff = 0.5 * (north_side - south_side)
    advect = center + diffusion_rate * laplace + flow[:, 0:1] * along_diff + flow[:, 1:2] * cross_diff
    buoy_along = thermal_coef * along_diff[:, 0] - haline_coef * along_diff[:, 1]
    buoy_cross = thermal_coef * cross_diff[:, 0] - haline_coef * cross_diff[:, 1]
    diverge = along_diff[:, 2] + cross_diff[:, 3]
    temper = advect[:, 0] - thermal_coef * couple_rate * diverge
    saline = advect[:, 1] + haline_coef * couple_rate * diverge
    zonal = advect[:, 2] + coriolis * center[:, 3] + couple_rate * buoy_along
    meridional = advect[:, 3] - coriolis * center[:, 2] + couple_rate * buoy_cross
    return jnp.stack([temper, saline, zonal, meridional], axis=1) * mask_float[:, None]


def vertical_solve(right_side, coupling):
    empty = jnp.zeros_like(coupling[:1])
    upper = jnp.concatenate([coupling, empty], axis=0)
    lower = jnp.concatenate([empty, coupling], axis=0)
    diagonal = 1.0 + lower + upper
    first_ratio = -upper[0] / diagonal[0]
    first_value = right_side[0] / diagonal[0]

    def forward(state_pair, inputs):
        ratio_prev, value_prev = state_pair
        below_coef, diag_here, above_coef, right_here = inputs
        denominator = diag_here + below_coef * ratio_prev
        ratio_here = -above_coef / denominator
        value_here = (right_here + below_coef * value_prev) / denominator
        return (ratio_here, value_here), (ratio_here, value_here)

    final_state, stacked = lax.scan(forward, (first_ratio, first_value), (lower[1:], diagonal[1:], upper[1:], right_side[1:]))
    ratios = jnp.concatenate([first_ratio[None], stacked[0]], axis=0)
    values = jnp.concatenate([first_value[None], stacked[1]], axis=0)

    def backward(below_solution, inputs):
        ratio_here, value_here = inputs
        solution = value_here - ratio_here * below_solution
        return solution, solution

    last_solution, upper_solutions = lax.scan(backward, values[-1], (ratios[:-1], values[:-1]), reverse=True)
    return jnp.concatenate([upper_solutions, values[-1:]], axis=0)


def reference(adjoint, flow, land_mask, mixing, seam_code, obs_misfit, obs_owner, obs_cell):
    mask_float = land_mask.astype(jnp.float32)
    column = jnp.arange(ALONG_ALL, dtype=jnp.int32)
    tile_index = column // ALONG_DEV
    east_code = jnp.where(column % ALONG_DEV == ALONG_DEV - 1, (4 - seam_code[(tile_index + 1) % TILES_ALONG]) % 4, 0)
    west_code = jnp.where(column % ALONG_DEV == 0, seam_code[tile_index], 0)
    east_side = turn_vectors(jnp.roll(adjoint, -1, axis=3), east_code)
    west_side = turn_vectors(jnp.roll(adjoint, 1, axis=3), west_code)
    empty_row = jnp.zeros_like(adjoint[:, :, :1])
    north_side = jnp.concatenate([adjoint[:, :, 1:], empty_row], axis=2)
    south_side = jnp.concatenate([empty_row, adjoint[:, :, :-1]], axis=2)
    horizontal = transport(adjoint, east_side, west_side, north_side, south_side, flow, mask_float)
    owner_id = obs_owner[:, 0]
    along_tile = owner_id // TILES_CROSS
    cross_tile = owner_id % TILES_CROSS
    cross_global = cross_tile * CROSS_DEV + obs_cell // ALONG_DEV
    along_global = along_tile * ALONG_DEV + obs_cell % ALONG_DEV
    flat_index = cross_global * ALONG_ALL + along_global
    forcing = jnp.zeros((CROSS_ALL * ALONG_ALL, 4 * LEVELS), jnp.float32).at[flat_index].add(obs_misfit.astype(jnp.float32))
    forcing = forcing.reshape(CROSS_ALL, ALONG_ALL, LEVELS, 4).transpose(2, 3, 0, 1)
    right_side = mask_float[:, None] * (horizontal + forcing)
    coupling = mixing * mask_float[:-1] * mask_float[1:]
    return vertical_solve(right_side, coupling)
```

```python
import jax
import jax.numpy as jnp
from jax import lax
from jax.experimental import pallas as pl
from jax.experimental.pallas import tpu as pltpu
from jax.sharding import PartitionSpec as P

diffusion_rate = 0.15
coriolis = 0.3
couple_rate = 0.3
thermal_coef = 0.8
haline_coef = 0.6

LANES = 128
HEAD_ROWS = 8
VMEM_BYTES = 56 * 1024 * 1024


def pack_kernel(owner_ref, cell_ref, rows_ref, out_ref, stage, rows_f, meta, slot_v, slot_s):
    tiles, block_rows, _ = out_ref.shape
    capacity = block_rows - HEAD_ROWS
    blocks = owner_ref.shape[0]
    rows_f[...] = rows_ref[...].astype(jnp.float32)
    tile_id = lax.broadcasted_iota(jnp.int32, (tiles, LANES), 0)
    low = lax.broadcasted_iota(jnp.int32, (LANES, 2 * LANES), 0)
    high = lax.broadcasted_iota(jnp.int32, (LANES, 2 * LANES), 1)
    count_with = ((low <= high) | (high >= LANES)).astype(jnp.float32).astype(jnp.bfloat16)
    place = (lax.broadcasted_iota(jnp.int32, (LANES, LANES), 0) % capacity).astype(jnp.float32)
    carry = jnp.zeros((tiles, LANES), jnp.float32)
    total = jnp.zeros((tiles, 2 * LANES), jnp.float32)
    for b in range(blocks):
        owner = owner_ref[b : b + 1, :]
        cell = cell_ref[b : b + 1, :]
        hit = (tile_id == owner).astype(jnp.float32)
        hit_narrow = hit.astype(jnp.bfloat16)
        counts = jnp.dot(hit_narrow, count_with, preferred_element_type=jnp.float32)
        rank = jnp.sum((counts[:, :LANES] + carry) * hit, axis=0, keepdims=True) - 1.0
        carry = carry + counts[:, LANES:]
        slot_v[b : b + 1, :] = owner * capacity + rank.astype(jnp.int32)
        row_part = ((cell >> 8) + 1).astype(jnp.float32)
        column_part = (cell & 255).astype(jnp.float32)
        here = place == rank
        values = jnp.concatenate(
            [jnp.where(here, row_part, 0.0), jnp.where(here, column_part, 0.0)], axis=0
        ).astype(jnp.bfloat16)
        total = total + lax.dot_general(
            hit_narrow, values, (((1,), (1,)), ((), ())), preferred_element_type=jnp.float32
        )
    meta[0] = total[:, :LANES]
    meta[1] = total[:, LANES:]
    pltpu.sync_copy(slot_v, slot_s)

    def scatter(b, carried):
        base = pl.multiple_of(b * LANES, LANES)
        for j in range(LANES):
            stage[pl.ds(slot_s[b, j], 1), :] = rows_f[pl.ds(base + j, 1), :]
        return carried

    lax.fori_loop(0, blocks, scatter, 0)
    first = lax.broadcasted_iota(jnp.int32, (HEAD_ROWS, LANES), 0) == 0

    def narrow(d, carried):
        base = pl.multiple_of(d * capacity, capacity)
        out_ref[d, 0:capacity, :] = stage[pl.ds(base, capacity), :].astype(jnp.bfloat16)
        head = jnp.where(
            first,
            jnp.broadcast_to(meta[0, pl.ds(d, 1), :], (HEAD_ROWS, LANES)),
            jnp.broadcast_to(meta[1, pl.ds(d, 1), :], (HEAD_ROWS, LANES)),
        )
        out_ref[d, capacity:block_rows, :] = head.astype(jnp.bfloat16)
        return carried

    lax.fori_loop(0, tiles, narrow, 0, unroll=4)


def pack_rows(obs_owner, obs_cell, obs_misfit, tiles, capacity):
    obs_rows, width = obs_misfit.shape
    blocks = obs_rows // LANES
    vmem = pl.BlockSpec(memory_space=pltpu.VMEM)
    return pl.pallas_call(
        pack_kernel,
        out_shape=jax.ShapeDtypeStruct((tiles, capacity + HEAD_ROWS, width), jnp.bfloat16),
        in_specs=[vmem] * 3,
        out_specs=vmem,
        scratch_shapes=[
            pltpu.VMEM((tiles * capacity, width), jnp.float32),
            pltpu.VMEM((obs_rows, width), jnp.float32),
            pltpu.VMEM((2, tiles, LANES), jnp.float32),
            pltpu.VMEM((blocks, LANES), jnp.int32),
            pltpu.SMEM((blocks, LANES), jnp.int32),
        ],
        compiler_params=pltpu.CompilerParams(vmem_limit_bytes=VMEM_BYTES),
        name="pack_rows",
    )(obs_owner.reshape(blocks, LANES), obs_cell.reshape(blocks, LANES), obs_misfit)


def local_kernel(
    adj_ref, flow_ref, mask_ref, mix_ref, north_ref, south_ref, east_ref, west_ref,
    hor_ref, mask_inv_ref, lower_inv_ref, ratio_ref, north_f, south_f,
):
    levels, fields, rows, columns = adj_ref.shape
    north_f[...] = north_ref[...].astype(jnp.float32)
    south_f[...] = south_ref[...].astype(jnp.float32)
    shape = (rows, columns)
    lane = lax.broadcasted_iota(jnp.int32, shape, 1)
    sub = lax.broadcasted_iota(jnp.int32, shape, 0)
    last_column, first_column = lane == columns - 1, lane == 0
    last_row, first_row = sub == rows - 1, sub == 0

    def level(k, state):
        lower, ratio_prev = state
        mask = mask_ref[k].astype(jnp.float32)
        below = jnp.minimum(k + 1, levels - 1)
        mask_below = mask_ref[below].astype(jnp.float32)
        mix = mix_ref[jnp.minimum(k, levels - 2)]
        upper = jnp.where(k < levels - 1, mix * mask * mask_below, 0.0)
        inverse = 1.0 / (1.0 + lower + upper + lower * ratio_prev)
        ratio = -upper * inverse
        mask_inv = mask * inverse
        mask_inv_ref[k] = mask_inv
        lower_inv_ref[k] = lower * inverse
        ratio_ref[k] = ratio
        flow_along, flow_cross = flow_ref[k, 0], flow_ref[k, 1]
        centers, advects, alongs, crosses = [], [], [], []
        for f in range(fields):
            x = adj_ref[k, f]
            halo_east = jnp.concatenate([east_ref[k, f]] * (columns // LANES), axis=1)
            halo_west = jnp.concatenate([west_ref[k, f]] * (columns // LANES), axis=1)
            east = jnp.where(last_column, halo_east, pltpu.roll(x, columns - 1, 1))
            west = jnp.where(first_column, halo_west, pltpu.roll(x, 1, 1))
            at = k * fields + f
            halo_north = jnp.broadcast_to(north_f[pl.ds(at, 1), :], shape)
            halo_south = jnp.broadcast_to(south_f[pl.ds(at, 1), :], shape)
            north = jnp.where(last_row, halo_north, pltpu.roll(x, rows - 1, 0))
            south = jnp.where(first_row, halo_south, pltpu.roll(x, 1, 0))
            along = 0.5 * (east - west)
            cross = 0.5 * (north - south)
            advect = (
                x
                + diffusion_rate * (east + west + north + south - 4.0 * x)
                + flow_along * along
                + flow_cross * cross
            )
            centers.append(x)
            advects.append(advect)
            alongs.append(along)
            crosses.append(cross)
        diverge = alongs[2] + crosses[3]
        buoy_along = thermal_coef * alongs[0] - haline_coef * alongs[1]
        buoy_cross = thermal_coef * crosses[0] - haline_coef * crosses[1]
        hor_ref[k, 0] = mask_inv * (advects[0] - thermal_coef * couple_rate * diverge)
        hor_ref[k, 1] = mask_inv * (advects[1] + haline_coef * couple_rate * diverge)
        hor_ref[k, 2] = mask_inv * (advects[2] + coriolis * centers[3] + couple_rate * buoy_along)
        hor_ref[k, 3] = mask_inv * (advects[3] - coriolis * centers[2] + couple_rate * buoy_cross)
        return upper, ratio

    zero = jnp.zeros(shape, jnp.float32)
    lax.fori_loop(0, levels, level, (zero, zero))


def local_part(adjoint, flow, land_mask, mixing, north, south, east, west):
    levels, fields, rows, columns = adjoint.shape
    vmem = pl.BlockSpec(memory_space=pltpu.VMEM)
    plane = jax.ShapeDtypeStruct((levels, rows, columns), jnp.float32)
    return pl.pallas_call(
        local_kernel,
        out_shape=(jax.ShapeDtypeStruct(adjoint.shape, jnp.float32), plane, plane, plane),
        in_specs=[vmem] * 8,
        out_specs=(vmem,) * 4,
        scratch_shapes=[pltpu.VMEM((levels * fields, columns), jnp.float32)] * 2,
        compiler_params=pltpu.CompilerParams(vmem_limit_bytes=VMEM_BYTES),
        cost_estimate=pl.CostEstimate(flops=1000, bytes_accessed=100000, transcendentals=0),
        name="local_part",
    )(adjoint, flow, land_mask, mixing, north, south, east, west)


GROUP = 8


def finish_kernel(got_ref, hor_ref, mask_inv_ref, lower_inv_ref, ratio_ref, out_ref, acc):
    tiles, block_rows, width = got_ref.shape
    capacity = block_rows - HEAD_ROWS
    levels, fields, rows, columns = out_ref.shape
    depth = GROUP * capacity
    column_id = lax.broadcasted_iota(jnp.int32, (columns, depth), 0).astype(jnp.float32)
    left = lax.broadcasted_iota(jnp.int32, (1, LANES), 1) < capacity
    acc[...] = jnp.zeros_like(acc)

    def gather(g, carried):
        payload = got_ref[pl.ds(g * GROUP, GROUP), 0:capacity, :].reshape(depth, width)
        turned = jnp.transpose(payload)
        row_of, column_of = [], []
        for i in range(0, GROUP, 2):
            one = got_ref[g * GROUP + i, capacity:block_rows, :].astype(jnp.float32)
            two = got_ref[g * GROUP + i + 1, capacity:block_rows, :].astype(jnp.float32)
            row_of.append(jnp.where(left, one[0:1], two[0:1]))
            column_of.append(jnp.where(left, one[1:2], two[1:2]))
        row_of = jnp.concatenate(row_of, axis=1)
        column_of = jnp.concatenate(column_of, axis=1)
        onehot = (column_id == column_of).astype(jnp.float32).astype(jnp.bfloat16)
        row_wide = jnp.broadcast_to(row_of, (width, depth)).astype(jnp.bfloat16)
        zero = jnp.zeros((width, depth), jnp.bfloat16)
        masked = jnp.concatenate(
            [jnp.where(row_wide == (c + 1), turned, zero) for c in range(rows)], axis=0
        )
        part = lax.dot_general(
            masked, onehot, (((1,), (1,)), ((), ())), preferred_element_type=jnp.float32
        )
        acc[...] += part.reshape(rows, width, columns)
        return carried

    lax.fori_loop(0, tiles // GROUP, gather, 0)

    def forward(q, previous):
        forcing = jnp.swapaxes(acc[:, pl.ds(pl.multiple_of(q * 8, 8), 8), :], 0, 1)
        state = list(previous)
        for i in range(8 // fields):
            k = q * (8 // fields) + i
            mask_inv, lower_inv = mask_inv_ref[k], lower_inv_ref[k]
            for f in range(fields):
                state[f] = (
                    hor_ref[k, f] + mask_inv * forcing[i * fields + f] + lower_inv * state[f]
                )
                out_ref[k, f] = state[f]
        return tuple(state)

    zero = jnp.zeros((rows, columns), jnp.float32)
    last = lax.fori_loop(0, levels * fields // 8, forward, (zero,) * fields)

    def backward(step, below):
        k = levels - 2 - step
        ratio = ratio_ref[k]
        here = []
        for f in range(fields):
            here.append(out_ref[k, f] - ratio * below[f])
            out_ref[k, f] = here[f]
        return tuple(here)

    lax.fori_loop(0, levels - 1, backward, last)


def finish(got, hor, mask_inv, lower_inv, ratio):
    levels, fields, rows, columns = hor.shape
    vmem = pl.BlockSpec(memory_space=pltpu.VMEM)
    return pl.pallas_call(
        finish_kernel,
        out_shape=jax.ShapeDtypeStruct(hor.shape, jnp.float32),
        in_specs=[vmem] * 5,
        out_specs=vmem,
        scratch_shapes=[pltpu.VMEM((rows, levels * fields, columns), jnp.float32)],
        compiler_params=pltpu.CompilerParams(vmem_limit_bytes=VMEM_BYTES),
        name="finish",
    )(got, hor, mask_inv, lower_inv, ratio)


def turn(edge, code):
    cosine = (code == 0).astype(jnp.float32) - (code == 2).astype(jnp.float32)
    sine = (code == 1).astype(jnp.float32) - (code == 3).astype(jnp.float32)
    zonal = cosine * edge[:, 2] - sine * edge[:, 3]
    meridional = sine * edge[:, 2] + cosine * edge[:, 3]
    return jnp.stack([edge[:, 0], edge[:, 1], zonal, meridional], axis=1)


def per_device(adjoint, flow, land_mask, mixing, seam_code, obs_misfit, obs_owner, obs_cell):
    levels, fields, rows, columns = adjoint.shape
    along_count = lax.axis_size("along")
    cross_count = lax.axis_size("cross")
    devices = along_count * cross_count
    along_rank = lax.axis_index("along")
    capacity = 2 * obs_misfit.shape[0] // devices
    packed = pack_rows(obs_owner, obs_cell, obs_misfit, devices, capacity)
    packed, adjoint = lax.optimization_barrier((packed, adjoint))
    got = lax.all_to_all(packed, ("along", "cross"), split_axis=0, concat_axis=0, tiled=True)

    ring_up = [(i, (i + 1) % along_count) for i in range(along_count)]
    ring_down = [(target, source) for source, target in ring_up]
    line_up = [(i, i + 1) for i in range(cross_count - 1)]
    line_down = [(target, source) for source, target in line_up]
    narrow = lambda a: a.astype(jnp.bfloat16)
    west = lax.ppermute(narrow(adjoint[:, :, :, columns - 1]), "along", ring_up)
    east = lax.ppermute(narrow(adjoint[:, :, :, 0]), "along", ring_down)
    south = lax.ppermute(
        narrow(adjoint[:, :, rows - 1, :]).reshape(levels * fields, columns), "cross", line_up
    )
    north = lax.ppermute(
        narrow(adjoint[:, :, 0, :]).reshape(levels * fields, columns), "cross", line_down
    )
    tile_ids = jnp.arange(seam_code.shape[0], dtype=jnp.int32)
    own_code = jnp.sum(jnp.where(tile_ids == along_rank, seam_code, 0))
    next_code = jnp.sum(jnp.where(tile_ids == (along_rank + 1) % along_count, seam_code, 0))
    west = turn(west.astype(jnp.float32), own_code)
    east = turn(east.astype(jnp.float32), (4 - next_code) % 4)
    spread = lambda edge: jnp.broadcast_to(edge[..., None], edge.shape + (LANES,))
    hor, mask_inv, lower_inv, ratio = local_part(
        adjoint, flow, land_mask, mixing, north, south, spread(east), spread(west)
    )
    return finish(got, hor, mask_inv, lower_inv, ratio)


def solution(mesh):
    return jax.shard_map(
        per_device,
        mesh=mesh,
        in_specs=(
            P(None, None, "cross", "along"),
            P(None, None, "cross", "along"),
            P(None, "cross", "along"),
            P(None, "cross", "along"),
            P(),
            P(("along", "cross"), None),
            P(("along", "cross"), None),
            P(("along", "cross")),
        ),
        out_specs=P(None, None, "cross", "along"),
        check_vma=False,
    )
```

```python
import jax
import jax.numpy as jnp
from jax import lax
from jax.experimental import pallas as pl
from jax.experimental.pallas import tpu as pltpu
from jax.sharding import PartitionSpec as P

diffusion_rate = 0.15
coriolis = 0.3
couple_rate = 0.3
thermal_coef = 0.8
haline_coef = 0.6

LANES = 128
HEAD_ROWS = 8
VMEM_BYTES = 20 * 1024 * 1024


def pack_kernel(owner_ref, cell_ref, rows_ref, out_ref, stage, rows_f, meta, slot_v, slot_s):
    tiles, block_rows, _ = out_ref.shape
    capacity = block_rows - HEAD_ROWS
    blocks = owner_ref.shape[0]
    rows_f[...] = rows_ref[...].astype(jnp.float32)
    tile_id = lax.broadcasted_iota(jnp.int32, (tiles, LANES), 0)
    low = lax.broadcasted_iota(jnp.int32, (LANES, 2 * LANES), 0)
    high = lax.broadcasted_iota(jnp.int32, (LANES, 2 * LANES), 1)
    count_with = ((low <= high) | (high >= LANES)).astype(jnp.float32).astype(jnp.bfloat16)
    place = (lax.broadcasted_iota(jnp.int32, (LANES, LANES), 0) % capacity).astype(jnp.float32)
    carry = jnp.zeros((tiles, LANES), jnp.float32)
    total = jnp.zeros((tiles, 2 * LANES), jnp.float32)
    for b in range(blocks):
        owner = owner_ref[b : b + 1, :]
        cell = cell_ref[b : b + 1, :]
        hit = (tile_id == owner).astype(jnp.float32)
        hit_narrow = hit.astype(jnp.bfloat16)
        counts = jnp.dot(hit_narrow, count_with, preferred_element_type=jnp.float32)
        rank = jnp.sum((counts[:, :LANES] + carry) * hit, axis=0, keepdims=True) - 1.0
        carry = carry + counts[:, LANES:]
        slot_v[b : b + 1, :] = owner * capacity + rank.astype(jnp.int32)
        row_part = ((cell >> 8) + 1).astype(jnp.float32)
        column_part = (cell & 255).astype(jnp.float32)
        here = place == rank
        values = jnp.concatenate(
            [jnp.where(here, row_part, 0.0), jnp.where(here, column_part, 0.0)], axis=0
        ).astype(jnp.bfloat16)
        total = total + lax.dot_general(
            hit_narrow, values, (((1,), (1,)), ((), ())), preferred_element_type=jnp.float32
        )
    meta[0] = total[:, :LANES]
    meta[1] = total[:, LANES:]
    pltpu.sync_copy(slot_v, slot_s)

    def scatter(b, carried):
        base = pl.multiple_of(b * LANES, LANES)
        for j in range(LANES):
            stage[pl.ds(slot_s[b, j], 1), :] = rows_f[pl.ds(base + j, 1), :]
        return carried

    lax.fori_loop(0, blocks, scatter, 0)
    first = lax.broadcasted_iota(jnp.int32, (HEAD_ROWS, LANES), 0) == 0

    def narrow(d, carried):
        base = pl.multiple_of(d * capacity, capacity)
        out_ref[d, 0:capacity, :] = stage[pl.ds(base, capacity), :].astype(jnp.bfloat16)
        head = jnp.where(
            first,
            jnp.broadcast_to(meta[0, pl.ds(d, 1), :], (HEAD_ROWS, LANES)),
            jnp.broadcast_to(meta[1, pl.ds(d, 1), :], (HEAD_ROWS, LANES)),
        )
        out_ref[d, capacity:block_rows, :] = head.astype(jnp.bfloat16)
        return carried

    lax.fori_loop(0, tiles, narrow, 0, unroll=4)


def pack_rows(obs_owner, obs_cell, obs_misfit, tiles, capacity):
    obs_rows, width = obs_misfit.shape
    blocks = obs_rows // LANES
    vmem = pl.BlockSpec(memory_space=pltpu.VMEM)
    return pl.pallas_call(
        pack_kernel,
        out_shape=jax.ShapeDtypeStruct((tiles, capacity + HEAD_ROWS, width), jnp.bfloat16),
        in_specs=[vmem] * 3,
        out_specs=vmem,
        scratch_shapes=[
            pltpu.VMEM((tiles * capacity, width), jnp.float32),
            pltpu.VMEM((obs_rows, width), jnp.float32),
            pltpu.VMEM((2, tiles, LANES), jnp.float32),
            pltpu.VMEM((blocks, LANES), jnp.int32),
            pltpu.SMEM((blocks, LANES), jnp.int32),
        ],
        compiler_params=pltpu.CompilerParams(vmem_limit_bytes=VMEM_BYTES),
        name="pack_rows",
    )(obs_owner.reshape(blocks, LANES), obs_cell.reshape(blocks, LANES), obs_misfit)


def edge_kernel(adj_ref, north_ref, south_ref, east_ref, west_ref):
    planes, rows, columns = adj_ref.shape
    north_ref[...] = adj_ref[:, 0, :].astype(jnp.bfloat16)
    south_ref[...] = adj_ref[:, rows - 1, :].astype(jnp.bfloat16)
    lane = lax.broadcasted_iota(jnp.int32, (8, LANES), 1)
    for ref, start, at in ((east_ref, 0, 0), (west_ref, columns - LANES, LANES - 1)):
        pick = (lane == at).astype(jnp.float32).astype(jnp.bfloat16)
        side = adj_ref[:, :, start : start + LANES].reshape(planes * rows, LANES)
        line = lax.dot_general(
            pick,
            side.astype(jnp.bfloat16),
            (((1,), (1,)), ((), ())),
            preferred_element_type=jnp.float32,
        )
        for i in range(planes * rows // LANES):
            ref[i : i + 1, :] = line[0:1, i * LANES : (i + 1) * LANES]


def edges(adjoint):
    levels, fields, rows, columns = adjoint.shape
    planes = levels * fields
    vmem = pl.BlockSpec(memory_space=pltpu.VMEM)
    line = jax.ShapeDtypeStruct((planes * rows // LANES, LANES), jnp.float32)
    row = jax.ShapeDtypeStruct((planes, columns), jnp.bfloat16)
    return pl.pallas_call(
        edge_kernel,
        out_shape=(row, row, line, line),
        in_specs=[vmem],
        out_specs=(vmem,) * 4,
        compiler_params=pltpu.CompilerParams(vmem_limit_bytes=VMEM_BYTES),
        cost_estimate=pl.CostEstimate(flops=1000, bytes_accessed=100000, transcendentals=0),
        name="edges",
    )(adjoint.reshape(planes, rows, columns))


def turned_edge(edge, code, rows):
    cosine = jnp.where(code == 0, 1.0, 0.0) - jnp.where(code == 2, 1.0, 0.0)
    sine = jnp.where(code == 1, 1.0, 0.0) - jnp.where(code == 3, 1.0, 0.0)
    field = (lax.broadcasted_iota(jnp.int32, edge.shape, 1) // rows) % 4
    zonal = cosine * edge - sine * pltpu.roll(edge, LANES - rows, 1)
    meridional = sine * pltpu.roll(edge, rows, 1) + cosine * edge
    return jnp.where(field == 2, zonal, jnp.where(field == 3, meridional, edge))


def spread_edge(edge, spread_ref):
    shape = (LANES, LANES)
    diagonal = lax.broadcasted_iota(jnp.int32, shape, 0) == lax.broadcasted_iota(jnp.int32, shape, 1)
    ones = jnp.ones(shape, jnp.bfloat16)
    for i in range(edge.shape[0]):
        line = jnp.where(diagonal, jnp.broadcast_to(edge[i : i + 1, :], shape), 0.0)
        spread_ref[i * LANES : (i + 1) * LANES, :] = jnp.dot(
            line.astype(jnp.bfloat16), ones, preferred_element_type=jnp.float32
        )


def local_kernel(
    seam_ref, adj_ref, flow_ref, mask_ref, mix_ref, north_ref, south_ref, east_ref, west_ref,
    hor_ref, mask_inv_ref, lower_inv_ref, ratio_ref, north_f, south_f, east_f, west_f,
):
    levels, fields, rows, columns = adj_ref.shape
    along_rank = lax.axis_index("along")
    own_code = seam_ref[along_rank]
    next_code = seam_ref[lax.rem(along_rank + 1, seam_ref.shape[0])]
    spread_edge(turned_edge(west_ref[...].astype(jnp.float32), own_code, rows), west_f)
    spread_edge(turned_edge(east_ref[...].astype(jnp.float32), (4 - next_code) & 3, rows), east_f)
    north_f[...] = north_ref[...].astype(jnp.float32)
    south_f[...] = south_ref[...].astype(jnp.float32)
    shape = (rows, columns)
    lane = lax.broadcasted_iota(jnp.int32, shape, 1)
    sub = lax.broadcasted_iota(jnp.int32, shape, 0)
    last_column, first_column = lane == columns - 1, lane == 0
    last_row, first_row = sub == rows - 1, sub == 0

    def level(k, state):
        lower, ratio_prev = state
        mask = mask_ref[k].astype(jnp.float32)
        below = jnp.minimum(k + 1, levels - 1)
        mask_below = mask_ref[below].astype(jnp.float32)
        mix = mix_ref[jnp.minimum(k, levels - 2)]
        upper = jnp.where(k < levels - 1, mix * mask * mask_below, 0.0)
        inverse = 1.0 / (1.0 + lower + upper + lower * ratio_prev)
        ratio = -upper * inverse
        mask_inv = mask * inverse
        mask_inv_ref[k] = mask_inv
        lower_inv_ref[k] = lower * inverse
        ratio_ref[k] = ratio
        flow_along, flow_cross = flow_ref[k, 0], flow_ref[k, 1]
        centers, advects, alongs, crosses = [], [], [], []
        for f in range(fields):
            x = adj_ref[k, f]
            at = k * fields + f
            tall = pl.ds(pl.multiple_of(at * rows, rows), rows)
            halo_east = jnp.concatenate([east_f[tall, :]] * (columns // LANES), axis=1)
            halo_west = jnp.concatenate([west_f[tall, :]] * (columns // LANES), axis=1)
            east = jnp.where(last_column, halo_east, pltpu.roll(x, columns - 1, 1))
            west = jnp.where(first_column, halo_west, pltpu.roll(x, 1, 1))
            halo_north = jnp.broadcast_to(north_f[pl.ds(at, 1), :], shape)
            halo_south = jnp.broadcast_to(south_f[pl.ds(at, 1), :], shape)
            north = jnp.where(last_row, halo_north, pltpu.roll(x, rows - 1, 0))
            south = jnp.where(first_row, halo_south, pltpu.roll(x, 1, 0))
            along = 0.5 * (east - west)
            cross = 0.5 * (north - south)
            advect = (
                x
                + diffusion_rate * (east + west + north + south - 4.0 * x)
                + flow_along * along
                + flow_cross * cross
            )
            centers.append(x)
            advects.append(advect)
            alongs.append(along)
            crosses.append(cross)
        diverge = alongs[2] + crosses[3]
        buoy_along = thermal_coef * alongs[0] - haline_coef * alongs[1]
        buoy_cross = thermal_coef * crosses[0] - haline_coef * crosses[1]
        hor_ref[k, 0] = mask_inv * (advects[0] - thermal_coef * couple_rate * diverge)
        hor_ref[k, 1] = mask_inv * (advects[1] + haline_coef * couple_rate * diverge)
        hor_ref[k, 2] = mask_inv * (advects[2] + coriolis * centers[3] + couple_rate * buoy_along)
        hor_ref[k, 3] = mask_inv * (advects[3] - coriolis * centers[2] + couple_rate * buoy_cross)
        return upper, ratio

    zero = jnp.zeros(shape, jnp.float32)
    lax.fori_loop(0, levels, level, (zero, zero))


def local_part(seam_code, adjoint, flow, land_mask, mixing, north, south, east, west):
    levels, fields, rows, columns = adjoint.shape
    planes = levels * fields
    vmem = pl.BlockSpec(memory_space=pltpu.VMEM)
    plane = jax.ShapeDtypeStruct((levels, rows, columns), jnp.float32)
    return pl.pallas_call(
        local_kernel,
        out_shape=(jax.ShapeDtypeStruct(adjoint.shape, jnp.float32), plane, plane, plane),
        in_specs=[pl.BlockSpec(memory_space=pltpu.SMEM)] + [vmem] * 8,
        out_specs=(vmem,) * 4,
        scratch_shapes=[pltpu.VMEM((planes, columns), jnp.float32)] * 2
        + [pltpu.VMEM((planes * rows, LANES), jnp.float32)] * 2,
        compiler_params=pltpu.CompilerParams(vmem_limit_bytes=VMEM_BYTES),
        cost_estimate=pl.CostEstimate(flops=1000, bytes_accessed=100000, transcendentals=0),
        name="local_part",
    )(seam_code, adjoint, flow, land_mask, mixing, north, south, east, west)


GROUP = 8


def finish_kernel(got_ref, hor_ref, mask_inv_ref, lower_inv_ref, ratio_ref, out_ref, acc):
    tiles, block_rows, width = got_ref.shape
    capacity = block_rows - HEAD_ROWS
    levels, fields, rows, columns = out_ref.shape
    depth = GROUP * capacity
    column_id = lax.broadcasted_iota(jnp.int32, (columns, depth), 0).astype(jnp.float32)
    left = lax.broadcasted_iota(jnp.int32, (1, LANES), 1) < capacity
    acc[...] = jnp.zeros_like(acc)

    def gather(g, carried):
        payload = got_ref[pl.ds(g * GROUP, GROUP), 0:capacity, :].reshape(depth, width)
        turned = jnp.transpose(payload)
        row_of, column_of = [], []
        for i in range(0, GROUP, 2):
            one = got_ref[g * GROUP + i, capacity:block_rows, :].astype(jnp.float32)
            two = got_ref[g * GROUP + i + 1, capacity:block_rows, :].astype(jnp.float32)
            row_of.append(jnp.where(left, one[0:1], two[0:1]))
            column_of.append(jnp.where(left, one[1:2], two[1:2]))
        row_of = jnp.concatenate(row_of, axis=1)
        column_of = jnp.concatenate(column_of, axis=1)
        onehot = (column_id == column_of).astype(jnp.float32).astype(jnp.bfloat16)
        row_wide = jnp.broadcast_to(row_of, (width, depth)).astype(jnp.bfloat16)
        zero = jnp.zeros((width, depth), jnp.bfloat16)
        masked = jnp.concatenate(
            [jnp.where(row_wide == (c + 1), turned, zero) for c in range(rows)], axis=0
        )
        part = lax.dot_general(
            masked, onehot, (((1,), (1,)), ((), ())), preferred_element_type=jnp.float32
        )
        acc[...] += part.reshape(rows, width, columns)
        return carried

    lax.fori_loop(0, tiles // GROUP, gather, 0)

    def forward(q, previous):
        forcing = jnp.swapaxes(acc[:, pl.ds(pl.multiple_of(q * 8, 8), 8), :], 0, 1)
        state = list(previous)
        for i in range(8 // fields):
            k = q * (8 // fields) + i
            mask_inv, lower_inv = mask_inv_ref[k], lower_inv_ref[k]
            for f in range(fields):
                state[f] = (
                    hor_ref[k, f] + mask_inv * forcing[i * fields + f] + lower_inv * state[f]
                )
                out_ref[k, f] = state[f]
        return tuple(state)

    zero = jnp.zeros((rows, columns), jnp.float32)
    last = lax.fori_loop(0, levels * fields // 8, forward, (zero,) * fields)

    def backward(step, below):
        k = levels - 2 - step
        ratio = ratio_ref[k]
        here = []
        for f in range(fields):
            here.append(out_ref[k, f] - ratio * below[f])
            out_ref[k, f] = here[f]
        return tuple(here)

    lax.fori_loop(0, levels - 1, backward, last)


def finish(got, hor, mask_inv, lower_inv, ratio):
    levels, fields, rows, columns = hor.shape
    vmem = pl.BlockSpec(memory_space=pltpu.VMEM)
    return pl.pallas_call(
        finish_kernel,
        out_shape=jax.ShapeDtypeStruct(hor.shape, jnp.float32),
        in_specs=[vmem] * 5,
        out_specs=vmem,
        scratch_shapes=[pltpu.VMEM((rows, levels * fields, columns), jnp.float32)],
        compiler_params=pltpu.CompilerParams(vmem_limit_bytes=VMEM_BYTES),
        name="finish",
    )(got, hor, mask_inv, lower_inv, ratio)


def per_device(adjoint, flow, land_mask, mixing, seam_code, obs_misfit, obs_owner, obs_cell):
    levels, fields, rows, columns = adjoint.shape
    along_count = lax.axis_size("along")
    cross_count = lax.axis_size("cross")
    devices = along_count * cross_count
    capacity = 2 * obs_misfit.shape[0] // devices
    packed = pack_rows(obs_owner, obs_cell, obs_misfit, devices, capacity)
    packed, adjoint = lax.optimization_barrier((packed, adjoint))
    got = lax.all_to_all(packed, ("along", "cross"), split_axis=0, concat_axis=0, tiled=True)

    ring_up = [(i, (i + 1) % along_count) for i in range(along_count)]
    ring_down = [(target, source) for source, target in ring_up]
    line_up = [(i, i + 1) for i in range(cross_count - 1)]
    line_down = [(target, source) for source, target in line_up]
    first_row, last_row, first_column, last_column = edges(adjoint)
    west = lax.ppermute(last_column.astype(jnp.bfloat16), "along", ring_up)
    east = lax.ppermute(first_column.astype(jnp.bfloat16), "along", ring_down)
    south = lax.ppermute(last_row, "cross", line_up)
    north = lax.ppermute(first_row, "cross", line_down)
    hor, mask_inv, lower_inv, ratio = local_part(
        seam_code, adjoint, flow, land_mask, mixing, north, south, east, west
    )
    return finish(got, hor, mask_inv, lower_inv, ratio)


def solution(mesh):
    return jax.shard_map(
        per_device,
        mesh=mesh,
        in_specs=(
            P(None, None, "cross", "along"),
            P(None, None, "cross", "along"),
            P(None, "cross", "along"),
            P(None, "cross", "along"),
            P(),
            P(("along", "cross"), None),
            P(("along", "cross"), None),
            P(("along", "cross")),
        ),
        out_specs=P(None, None, "cross", "along"),
        check_vma=False,
    )
```

```python
import jax
import jax.numpy as jnp
from jax import lax
from jax.experimental import pallas as pl
from jax.experimental.pallas import tpu as pltpu
from jax.sharding import PartitionSpec as P

diffusion_rate = 0.15
coriolis = 0.3
couple_rate = 0.3
thermal_coef = 0.8
haline_coef = 0.6

LANES = 128
HEAD_ROWS = 8
VMEM_BYTES = 20 * 1024 * 1024
WIDE_VMEM_BYTES = 61 * 1024 * 1024


def pack_kernel(
    owner_hbm, cell_hbm, rows_hbm, out_ref,
    owner_ref, cell_ref, rows_ref, stage, rows_f, meta, slot_v, slot_s, sems,
):
    tiles, block_rows, _ = out_ref.shape
    capacity = block_rows - HEAD_ROWS
    blocks = owner_ref.shape[0]
    owner_copy = pltpu.make_async_copy(owner_hbm, owner_ref, sems.at[0])
    cell_copy = pltpu.make_async_copy(cell_hbm, cell_ref, sems.at[1])
    rows_copy = pltpu.make_async_copy(rows_hbm, rows_ref, sems.at[2])
    owner_copy.start()
    cell_copy.start()
    rows_copy.start()
    owner_copy.wait()
    cell_copy.wait()
    tile_id = lax.broadcasted_iota(jnp.int32, (tiles, LANES), 0)
    low = lax.broadcasted_iota(jnp.int32, (LANES, 2 * LANES), 0)
    high = lax.broadcasted_iota(jnp.int32, (LANES, 2 * LANES), 1)
    count_with = ((low <= high) | (high >= LANES)).astype(jnp.float32).astype(jnp.bfloat16)
    place = (lax.broadcasted_iota(jnp.int32, (LANES, LANES), 0) % capacity).astype(jnp.float32)
    carry = jnp.zeros((tiles, LANES), jnp.float32)
    total = jnp.zeros((tiles, 2 * LANES), jnp.float32)
    for b in range(blocks):
        owner = owner_ref[b : b + 1, :]
        cell = cell_ref[b : b + 1, :]
        hit = (tile_id == owner).astype(jnp.float32)
        hit_narrow = hit.astype(jnp.bfloat16)
        counts = jnp.dot(hit_narrow, count_with, preferred_element_type=jnp.float32)
        rank = jnp.sum((counts[:, :LANES] + carry) * hit, axis=0, keepdims=True) - 1.0
        carry = carry + counts[:, LANES:]
        slot_v[b : b + 1, :] = owner * capacity + rank.astype(jnp.int32)
        row_part = ((cell >> 8) + 1).astype(jnp.float32)
        column_part = (cell & 255).astype(jnp.float32)
        here = place == rank
        values = jnp.concatenate(
            [jnp.where(here, row_part, 0.0), jnp.where(here, column_part, 0.0)], axis=0
        ).astype(jnp.bfloat16)
        total = total + lax.dot_general(
            hit_narrow, values, (((1,), (1,)), ((), ())), preferred_element_type=jnp.float32
        )
    meta[0] = total[:, :LANES]
    meta[1] = total[:, LANES:]
    slot_copy = pltpu.make_async_copy(slot_v, slot_s, sems.at[3])
    slot_copy.start()
    rows_copy.wait()
    rows_f[...] = rows_ref[...].astype(jnp.float32)
    slot_copy.wait()

    def scatter(b, carried):
        base = pl.multiple_of(b * LANES, LANES)
        for j in range(LANES):
            stage[pl.ds(slot_s[b, j], 1), :] = rows_f[pl.ds(base + j, 1), :]
        return carried

    lax.fori_loop(0, blocks, scatter, 0)
    first = lax.broadcasted_iota(jnp.int32, (HEAD_ROWS, LANES), 0) == 0

    def narrow(d, carried):
        base = pl.multiple_of(d * capacity, capacity)
        out_ref[d, 0:capacity, :] = stage[pl.ds(base, capacity), :].astype(jnp.bfloat16)
        head = jnp.where(
            first,
            jnp.broadcast_to(meta[0, pl.ds(d, 1), :], (HEAD_ROWS, LANES)),
            jnp.broadcast_to(meta[1, pl.ds(d, 1), :], (HEAD_ROWS, LANES)),
        )
        out_ref[d, capacity:block_rows, :] = head.astype(jnp.bfloat16)
        return carried

    lax.fori_loop(0, tiles, narrow, 0, unroll=4)


def pack_rows(obs_owner, obs_cell, obs_misfit, tiles, capacity):
    obs_rows, width = obs_misfit.shape
    blocks = obs_rows // LANES
    vmem = pl.BlockSpec(memory_space=pltpu.VMEM)
    return pl.pallas_call(
        pack_kernel,
        out_shape=jax.ShapeDtypeStruct((tiles, capacity + HEAD_ROWS, width), jnp.bfloat16),
        in_specs=[pl.BlockSpec(memory_space=pltpu.HBM)] * 3,
        out_specs=vmem,
        scratch_shapes=[
            pltpu.VMEM((blocks, LANES), jnp.int32),
            pltpu.VMEM((blocks, LANES), jnp.int32),
            pltpu.VMEM((obs_rows, width), jnp.bfloat16),
            pltpu.VMEM((tiles * capacity, width), jnp.float32),
            pltpu.VMEM((obs_rows, width), jnp.float32),
            pltpu.VMEM((2, tiles, LANES), jnp.float32),
            pltpu.VMEM((blocks, LANES), jnp.int32),
            pltpu.SMEM((blocks, LANES), jnp.int32),
            pltpu.SemaphoreType.DMA((4,)),
        ],
        compiler_params=pltpu.CompilerParams(vmem_limit_bytes=WIDE_VMEM_BYTES),
        name="pack_rows",
    )(obs_owner.reshape(blocks, LANES), obs_cell.reshape(blocks, LANES), obs_misfit)


def edge_kernel(adj_ref, north_ref, south_ref, east_ref, west_ref):
    planes, rows, columns = adj_ref.shape
    north_ref[...] = adj_ref[:, 0, :].astype(jnp.bfloat16)
    south_ref[...] = adj_ref[:, rows - 1, :].astype(jnp.bfloat16)
    row = lax.broadcasted_iota(jnp.int32, (rows, LANES), 0)
    lane = lax.broadcasted_iota(jnp.int32, (rows, LANES), 1)
    for ref, start, at in ((east_ref, 0, 0), (west_ref, columns - LANES, LANES - 1)):
        line = jnp.zeros((rows, planes), jnp.float32)
        for r in range(rows):
            pick = ((lane == at) & (row == r)).astype(jnp.float32).astype(jnp.bfloat16)
            side = adj_ref[:, r, start : start + LANES].astype(jnp.bfloat16)
            line = line + lax.dot_general(
                pick, side, (((1,), (1,)), ((), ())), preferred_element_type=jnp.float32
            )
        ref[...] = line.astype(jnp.bfloat16)


def edges(adjoint):
    levels, fields, rows, columns = adjoint.shape
    planes = levels * fields
    vmem = pl.BlockSpec(memory_space=pltpu.VMEM)
    side = jax.ShapeDtypeStruct((rows, planes), jnp.bfloat16)
    row = jax.ShapeDtypeStruct((planes, columns), jnp.bfloat16)
    return pl.pallas_call(
        edge_kernel,
        out_shape=(row, row, side, side),
        in_specs=[vmem],
        out_specs=(vmem,) * 4,
        compiler_params=pltpu.CompilerParams(vmem_limit_bytes=VMEM_BYTES),
        cost_estimate=pl.CostEstimate(flops=1000, bytes_accessed=100000, transcendentals=0),
        name="edges",
    )(adjoint.reshape(planes, rows, columns))


def local_kernel(
    adj_ref, flow_ref, mask_ref, mix_ref,
    hor_ref, coef_ref, weight_north_ref, weight_south_ref, weight_east_ref, weight_west_ref,
):
    levels, fields, rows, columns = adj_ref.shape
    planes = levels * fields
    shape = (rows, columns)
    lane = lax.broadcasted_iota(jnp.int32, shape, 1)
    sub = lax.broadcasted_iota(jnp.int32, shape, 0)
    last_column, first_column = lane == columns - 1, lane == 0
    last_row, first_row = sub == rows - 1, sub == 0

    row = lax.broadcasted_iota(jnp.int32, (rows, LANES), 0)
    short_lane = lax.broadcasted_iota(jnp.int32, (rows, LANES), 1)
    repeat = (
        lax.broadcasted_iota(jnp.int32, (levels, planes), 1) // fields
        == lax.broadcasted_iota(jnp.int32, (levels, planes), 0)
    ).astype(jnp.float32)
    for ref, start, at, half in (
        (weight_east_ref, columns - LANES, LANES - 1, 0.5),
        (weight_west_ref, 0, 0, -0.5),
    ):
        line = jnp.zeros((rows, levels), jnp.float32)
        for r in range(rows):
            pick = ((short_lane == at) & (row == r)).astype(jnp.float32)
            line = line + lax.dot_general(
                pick,
                flow_ref[:, 0, r, start : start + LANES],
                (((1,), (1,)), ((), ())),
                precision=lax.Precision.HIGHEST,
                preferred_element_type=jnp.float32,
            )
        line = jnp.dot(
            line, repeat, precision=lax.Precision.HIGHEST, preferred_element_type=jnp.float32
        )
        ref[...] = diffusion_rate + half * line

    def level(k, state):
        lower, ratio_prev = state
        mask = mask_ref[k].astype(jnp.float32)
        below = jnp.minimum(k + 1, levels - 1)
        mask_below = mask_ref[below].astype(jnp.float32)
        mix = mix_ref[jnp.minimum(k, levels - 2)]
        upper = jnp.where(k < levels - 1, mix * mask * mask_below, 0.0)
        inverse = 1.0 / (1.0 + lower + upper + lower * ratio_prev)
        ratio = -upper * inverse
        mask_inv = mask * inverse
        coef_ref[0, k] = mask_inv
        coef_ref[1, k] = lower * inverse
        coef_ref[2, k] = ratio
        flow_along, flow_cross = flow_ref[k, 0], flow_ref[k, 1]
        north_weight = diffusion_rate + 0.5 * flow_cross[rows - 1 : rows, :]
        south_weight = diffusion_rate - 0.5 * flow_cross[0:1, :]
        centers, advects, alongs, crosses = [], [], [], []
        for f in range(fields):
            weight_north_ref[pl.ds(k * fields + f, 1), :] = north_weight
            weight_south_ref[pl.ds(k * fields + f, 1), :] = south_weight
            x = adj_ref[k, f]
            east = jnp.where(last_column, 0.0, pltpu.roll(x, columns - 1, 1))
            west = jnp.where(first_column, 0.0, pltpu.roll(x, 1, 1))
            north = jnp.where(last_row, 0.0, pltpu.roll(x, rows - 1, 0))
            south = jnp.where(first_row, 0.0, pltpu.roll(x, 1, 0))
            along = 0.5 * (east - west)
            cross = 0.5 * (north - south)
            advect = (
                x
                + diffusion_rate * (east + west + north + south - 4.0 * x)
                + flow_along * along
                + flow_cross * cross
            )
            centers.append(x)
            advects.append(advect)
            alongs.append(along)
            crosses.append(cross)
        diverge = alongs[2] + crosses[3]
        buoy_along = thermal_coef * alongs[0] - haline_coef * alongs[1]
        buoy_cross = thermal_coef * crosses[0] - haline_coef * crosses[1]
        hor_ref[k, 0] = mask_inv * (advects[0] - thermal_coef * couple_rate * diverge)
        hor_ref[k, 1] = mask_inv * (advects[1] + haline_coef * couple_rate * diverge)
        hor_ref[k, 2] = mask_inv * (advects[2] + coriolis * centers[3] + couple_rate * buoy_along)
        hor_ref[k, 3] = mask_inv * (advects[3] - coriolis * centers[2] + couple_rate * buoy_cross)
        return upper, ratio

    zero = jnp.zeros(shape, jnp.float32)
    lax.fori_loop(0, levels, level, (zero, zero))


def local_part(adjoint, flow, land_mask, mixing):
    levels, fields, rows, columns = adjoint.shape
    planes = levels * fields
    vmem = pl.BlockSpec(memory_space=pltpu.VMEM)
    shape = lambda *dims: jax.ShapeDtypeStruct(dims, jnp.float32)
    return pl.pallas_call(
        local_kernel,
        out_shape=(
            shape(*adjoint.shape),
            shape(3, levels, rows, columns),
            shape(planes, columns),
            shape(planes, columns),
            shape(rows, planes),
            shape(rows, planes),
        ),
        in_specs=[vmem] * 4,
        out_specs=(vmem,) * 6,
        compiler_params=pltpu.CompilerParams(vmem_limit_bytes=VMEM_BYTES),
        cost_estimate=pl.CostEstimate(flops=1000, bytes_accessed=100000, transcendentals=0),
        name="local_part",
    )(adjoint, flow, land_mask, mixing)


def turned_edge(edge, code):
    planes = edge.shape[1]
    cosine = jnp.where(code == 0, 1.0, 0.0) - jnp.where(code == 2, 1.0, 0.0)
    sine = jnp.where(code == 1, 1.0, 0.0) - jnp.where(code == 3, 1.0, 0.0)
    field = lax.broadcasted_iota(jnp.int32, edge.shape, 1) & 3
    zonal = cosine * edge - sine * pltpu.roll(edge, planes - 1, 1)
    meridional = sine * pltpu.roll(edge, 1, 1) + cosine * edge
    return jnp.where(field == 2, zonal, jnp.where(field == 3, meridional, edge))


def edge_term(edge, weight, sign, axis, vector):
    planes = edge.shape[axis]
    field = lax.broadcasted_iota(jnp.int32, edge.shape, axis) & 3
    ahead = lambda n: pltpu.roll(edge, planes - n, axis)
    behind = lambda n: pltpu.roll(edge, n, axis)
    thermal = sign * 0.5 * thermal_coef * couple_rate
    haline = sign * 0.5 * haline_coef * couple_rate
    other = thermal * behind(vector) - haline * behind(vector - 1)
    mixed = jnp.where(field == 0, -thermal * ahead(vector), 0.0)
    mixed = jnp.where(field == 1, haline * ahead(vector - 1), mixed)
    mixed = jnp.where(field == vector, other, mixed)
    return weight * edge + mixed


def start_with_edges(
    acc, own_code, next_code, north_ref, south_ref, east_ref, west_ref,
    weight_north, weight_south, weight_east, weight_west,
):
    rows, planes, columns = acc.shape
    east = turned_edge(east_ref[...].astype(jnp.float32), (4 - next_code) & 3)
    west = turned_edge(west_ref[...].astype(jnp.float32), own_code)
    fill = jnp.zeros((LANES - rows, planes), jnp.float32)
    tall = lambda line: jnp.transpose(jnp.concatenate([line, fill], axis=0))
    east = tall(edge_term(east, weight_east[...], 1.0, 1, 2))
    west = tall(edge_term(west, weight_west[...], -1.0, 1, 2))
    north = edge_term(north_ref[...].astype(jnp.float32), weight_north[...], 1.0, 0, 3)
    south = edge_term(south_ref[...].astype(jnp.float32), weight_south[...], -1.0, 0, 3)
    lane = lax.broadcasted_iota(jnp.int32, (planes, LANES), 1)
    blank = jnp.zeros((planes, columns - 2 * LANES), jnp.float32)
    for c in range(rows):
        first = jnp.where(lane == 0, jnp.broadcast_to(west[:, c : c + 1], lane.shape), 0.0)
        last = jnp.where(lane == LANES - 1, jnp.broadcast_to(east[:, c : c + 1], lane.shape), 0.0)
        line = jnp.concatenate([first, blank, last], axis=1) if blank.shape[1] else (
            jnp.concatenate([first, last], axis=1)
        )
        if c == 0:
            line = line + south
        if c == rows - 1:
            line = line + north
        acc[c] = line


GROUP = 8


def finish_kernel(
    seam_ref, got_ref, north_ref, south_ref, east_ref, west_ref, hor_hbm, coef_hbm,
    weight_north_hbm, weight_south_hbm, weight_east_hbm, weight_west_hbm,
    out_hbm, acc, out_ref, hor_ref, coef_ref,
    weight_north, weight_south, weight_east, weight_west, sems, out_sems,
):
    tiles, block_rows, width = got_ref.shape
    capacity = block_rows - HEAD_ROWS
    levels, fields, rows, columns = out_ref.shape
    depth = GROUP * capacity
    weight_copies = [
        pltpu.make_async_copy(source, target, sems.at[i])
        for i, (source, target) in enumerate(
            (
                (weight_north_hbm, weight_north),
                (weight_south_hbm, weight_south),
                (weight_east_hbm, weight_east),
                (weight_west_hbm, weight_west),
            )
        )
    ]
    solve_copies = [
        pltpu.make_async_copy(hor_hbm, hor_ref, sems.at[4]),
        pltpu.make_async_copy(coef_hbm, coef_ref, sems.at[5]),
    ]
    for copy in weight_copies + solve_copies:
        copy.start()
    column_id = lax.broadcasted_iota(jnp.int32, (columns, depth), 0).astype(jnp.float32)
    left = lax.broadcasted_iota(jnp.int32, (1, LANES), 1) < capacity
    along_rank = lax.axis_index("along")
    own_code = seam_ref[along_rank]
    next_code = seam_ref[lax.rem(along_rank + 1, seam_ref.shape[0])]
    for copy in weight_copies:
        copy.wait()
    start_with_edges(
        acc, own_code, next_code, north_ref, south_ref, east_ref, west_ref,
        weight_north, weight_south, weight_east, weight_west,
    )

    def gather(g, carried):
        payload = got_ref[pl.ds(g * GROUP, GROUP), 0:capacity, :].reshape(depth, width)
        turned = jnp.transpose(payload)
        row_of, column_of = [], []
        for i in range(0, GROUP, 2):
            one = got_ref[g * GROUP + i, capacity:block_rows, :].astype(jnp.float32)
            two = got_ref[g * GROUP + i + 1, capacity:block_rows, :].astype(jnp.float32)
            row_of.append(jnp.where(left, one[0:1], two[0:1]))
            column_of.append(jnp.where(left, one[1:2], two[1:2]))
        row_of = jnp.concatenate(row_of, axis=1)
        column_of = jnp.concatenate(column_of, axis=1)
        onehot = (column_id == column_of).astype(jnp.float32).astype(jnp.bfloat16)
        row_wide = jnp.broadcast_to(row_of, (width, depth)).astype(jnp.bfloat16)
        zero = jnp.zeros((width, depth), jnp.bfloat16)
        masked = jnp.concatenate(
            [jnp.where(row_wide == (c + 1), turned, zero) for c in range(rows)], axis=0
        )
        part = lax.dot_general(
            masked, onehot, (((1,), (1,)), ((), ())), preferred_element_type=jnp.float32
        )
        acc[...] += part.reshape(rows, width, columns)
        return carried

    lax.fori_loop(0, tiles // GROUP, gather, 0)

    for copy in solve_copies:
        copy.wait()

    def forward(q, previous):
        forcing = jnp.swapaxes(acc[:, pl.ds(pl.multiple_of(q * 8, 8), 8), :], 0, 1)
        state = list(previous)
        for i in range(8 // fields):
            k = q * (8 // fields) + i
            mask_inv, lower_inv = coef_ref[0, k], coef_ref[1, k]
            for f in range(fields):
                state[f] = (
                    hor_ref[k, f] + mask_inv * forcing[i * fields + f] + lower_inv * state[f]
                )
                out_ref[k, f] = state[f]
        return tuple(state)

    zero = jnp.zeros((rows, columns), jnp.float32)
    last = lax.fori_loop(0, levels * fields // 8, forward, (zero,) * fields)

    def backward(step, below):
        k = levels - 2 - step
        ratio = coef_ref[2, k]
        here = []
        for f in range(fields):
            here.append(out_ref[k, f] - ratio * below[f])
            out_ref[k, f] = here[f]
        return tuple(here)

    below = last
    out_copies = []
    part = levels // 4
    done = 0
    for i in range(4):
        steps = part - 1 if i == 0 else part
        below = lax.fori_loop(done, done + steps, backward, below)
        done += steps
        span = pl.ds(levels - (i + 1) * part, part)
        copy = pltpu.make_async_copy(out_ref.at[span], out_hbm.at[span], out_sems.at[i])
        copy.start()
        out_copies.append(copy)
    for copy in out_copies:
        copy.wait()


def finish(seam_code, got, halos, local):
    hor, coef, weights = local[0], local[1], local[2:]
    levels, fields, rows, columns = hor.shape
    planes = levels * fields
    vmem = pl.BlockSpec(memory_space=pltpu.VMEM)
    hbm = pl.BlockSpec(memory_space=pltpu.HBM)
    return pl.pallas_call(
        finish_kernel,
        out_shape=jax.ShapeDtypeStruct(hor.shape, jnp.float32),
        in_specs=[pl.BlockSpec(memory_space=pltpu.SMEM)] + [vmem] * 5 + [hbm] * 6,
        out_specs=hbm,
        scratch_shapes=[
            pltpu.VMEM((rows, planes, columns), jnp.float32),
            pltpu.VMEM(hor.shape, jnp.float32),
            pltpu.VMEM(hor.shape, jnp.float32),
            pltpu.VMEM(coef.shape, jnp.float32),
        ]
        + [pltpu.VMEM(w.shape, jnp.float32) for w in weights]
        + [pltpu.SemaphoreType.DMA((6,)), pltpu.SemaphoreType.DMA((4,))],
        compiler_params=pltpu.CompilerParams(vmem_limit_bytes=WIDE_VMEM_BYTES),
        name="finish",
    )(seam_code, got, *halos, hor, coef, *weights)


def per_device(adjoint, flow, land_mask, mixing, seam_code, obs_misfit, obs_owner, obs_cell):
    levels, fields, rows, columns = adjoint.shape
    along_count = lax.axis_size("along")
    cross_count = lax.axis_size("cross")
    devices = along_count * cross_count
    capacity = 2 * obs_misfit.shape[0] // devices
    packed = pack_rows(obs_owner, obs_cell, obs_misfit, devices, capacity)
    packed, adjoint = lax.optimization_barrier((packed, adjoint))
    got = lax.all_to_all(packed, ("along", "cross"), split_axis=0, concat_axis=0, tiled=True)

    ring_up = [(i, (i + 1) % along_count) for i in range(along_count)]
    ring_down = [(target, source) for source, target in ring_up]
    line_up = [(i, i + 1) for i in range(cross_count - 1)]
    line_down = [(target, source) for source, target in line_up]
    first_row, last_row, first_column, last_column = edges(adjoint)
    west = lax.ppermute(last_column, "along", ring_up)
    east = lax.ppermute(first_column, "along", ring_down)
    south = lax.ppermute(last_row, "cross", line_up)
    north = lax.ppermute(first_row, "cross", line_down)
    local = local_part(adjoint, flow, land_mask, mixing)
    return finish(seam_code, got, (north, south, east, west), local)


def solution(mesh):
    return jax.shard_map(
        per_device,
        mesh=mesh,
        in_specs=(
            P(None, None, "cross", "along"),
            P(None, None, "cross", "along"),
            P(None, "cross", "along"),
            P(None, "cross", "along"),
            P(),
            P(("along", "cross"), None),
            P(("along", "cross"), None),
            P(("along", "cross")),
        ),
        out_specs=P(None, None, "cross", "along"),
        check_vma=False,
    )
```

```python
import functools

import jax
import jax.numpy as jnp
from jax import lax
from jax.experimental import pallas as pl
from jax.experimental.pallas import tpu as pltpu
from jax.sharding import PartitionSpec as P

diffusion_rate = 0.15
coriolis = 0.3
couple_rate = 0.3
thermal_coef = 0.8
haline_coef = 0.6

LANES = 128
HEAD_ROWS = 2
PARTS = 4
VMEM_BYTES = 20 * 1024 * 1024
WIDE_VMEM_BYTES = 61 * 1024 * 1024


def pack_kernel(
    owner_hbm, cell_hbm, rows_hbm, out_hbm,
    owner_ref, cell_ref, rows_ref, out_ref, stage, rows_f, slot_v, slot_s, sems, out_sems,
    *, tiles,
):
    block_rows = out_ref.shape[0] // tiles
    capacity = block_rows - HEAD_ROWS
    blocks = owner_ref.shape[0]
    half = blocks // 2
    owner_copy = pltpu.make_async_copy(owner_hbm, owner_ref, sems.at[0])
    cell_copy = pltpu.make_async_copy(cell_hbm, cell_ref, sems.at[1])
    rows_copy = pltpu.make_async_copy(rows_hbm, rows_ref, sems.at[2])
    owner_copy.start()
    cell_copy.start()
    rows_copy.start()
    tile_id = lax.broadcasted_iota(jnp.int32, (tiles, LANES), 0)
    low = lax.broadcasted_iota(jnp.int32, (LANES, 2 * LANES), 0)
    high = lax.broadcasted_iota(jnp.int32, (LANES, 2 * LANES), 1)
    count_with = ((low <= high) | (high >= LANES)).astype(jnp.float32).astype(jnp.bfloat16)
    device = lax.axis_index("along") * lax.axis_size("cross") + lax.axis_index("cross")
    place = lax.broadcasted_iota(jnp.int32, (LANES, LANES), 0) - device * block_rows
    place = (place & (LANES - 1)).astype(jnp.float32)
    carry = jnp.zeros((tiles, LANES), jnp.float32)
    total = jnp.zeros((tiles, 2 * LANES), jnp.float32)
    owner_copy.wait()
    cell_copy.wait()
    slot_copies = []
    for b in range(blocks):
        owner = owner_ref[b : b + 1, :]
        cell = cell_ref[b : b + 1, :]
        hit = (tile_id == owner).astype(jnp.float32)
        hit_narrow = hit.astype(jnp.bfloat16)
        counts = jnp.dot(hit_narrow, count_with, preferred_element_type=jnp.float32)
        rank = jnp.sum((counts[:, :LANES] + carry) * hit, axis=0, keepdims=True) - 1.0
        carry = carry + counts[:, LANES:]
        slot_v[b : b + 1, :] = owner * block_rows + rank.astype(jnp.int32)
        row_part = ((cell >> 8) + 1).astype(jnp.float32)
        column_part = (cell & 255).astype(jnp.float32)
        here = place == rank
        values = jnp.concatenate(
            [jnp.where(here, row_part, 0.0), jnp.where(here, column_part, 0.0)], axis=0
        ).astype(jnp.bfloat16)
        total = total + lax.dot_general(
            hit_narrow, values, (((1,), (1,)), ((), ())), preferred_element_type=jnp.float32
        )
        if (b + 1) % half == 0:
            span = pl.ds(b + 1 - half, half)
            copy = pltpu.make_async_copy(
                slot_v.at[span], slot_s.at[span], sems.at[3 + len(slot_copies)]
            )
            copy.start()
            slot_copies.append(copy)
    stage[pl.ds(capacity, tiles, stride=block_rows), :] = total[:, :LANES]
    stage[pl.ds(capacity + 1, tiles, stride=block_rows), :] = total[:, LANES:]
    rows_copy.wait()
    rows_f[...] = rows_ref[...].astype(jnp.float32)

    def scatter(b, carried):
        base = pl.multiple_of(b * LANES, LANES)
        for j in range(LANES):
            stage[pl.ds(slot_s[b, j], 1), :] = rows_f[pl.ds(base + j, 1), :]
        return carried

    for i, copy in enumerate(slot_copies):
        copy.wait()
        lax.fori_loop(i * half, (i + 1) * half, scatter, 0)

    step = out_ref.shape[0] // PARTS
    piece = capacity

    def narrow(i, carried):
        span = pl.ds(pl.multiple_of(i * piece, piece), piece)
        out_ref[span, :] = stage[span, :].astype(jnp.bfloat16)
        return carried

    out_copies = []
    for i in range(PARTS):
        lax.fori_loop(i * step // piece, (i + 1) * step // piece, narrow, 0, unroll=3)
        span = pl.ds(i * step, step)
        copy = pltpu.make_async_copy(out_ref.at[span], out_hbm.at[span], out_sems.at[i])
        copy.start()
        out_copies.append(copy)
    for copy in out_copies:
        copy.wait()


def pack_rows(obs_owner, obs_cell, obs_misfit, tiles, capacity):
    obs_rows, width = obs_misfit.shape
    blocks = obs_rows // LANES
    slots = tiles * (capacity + HEAD_ROWS)
    hbm = pl.BlockSpec(memory_space=pltpu.HBM)
    return pl.pallas_call(
        functools.partial(pack_kernel, tiles=tiles),
        out_shape=jax.ShapeDtypeStruct((slots, width), jnp.bfloat16),
        in_specs=[hbm] * 3,
        out_specs=hbm,
        scratch_shapes=[
            pltpu.VMEM((blocks, LANES), jnp.int32),
            pltpu.VMEM((blocks, LANES), jnp.int32),
            pltpu.VMEM((obs_rows, width), jnp.bfloat16),
            pltpu.VMEM((slots, width), jnp.bfloat16),
            pltpu.VMEM((slots, width), jnp.float32),
            pltpu.VMEM((obs_rows, width), jnp.float32),
            pltpu.VMEM((blocks, LANES), jnp.int32),
            pltpu.SMEM((blocks, LANES), jnp.int32),
            pltpu.SemaphoreType.DMA((5,)),
            pltpu.SemaphoreType.DMA((PARTS,)),
        ],
        compiler_params=pltpu.CompilerParams(vmem_limit_bytes=WIDE_VMEM_BYTES),
        name="pack_rows",
    )(obs_owner.reshape(blocks, LANES), obs_cell.reshape(blocks, LANES), obs_misfit)


def edge_kernel(adj_ref, north_ref, south_ref, east_ref, west_ref):
    planes, rows, columns = adj_ref.shape
    north_ref[...] = adj_ref[:, 0, :].astype(jnp.bfloat16)
    south_ref[...] = adj_ref[:, rows - 1, :].astype(jnp.bfloat16)
    row = lax.broadcasted_iota(jnp.int32, (rows, LANES), 0)
    lane = lax.broadcasted_iota(jnp.int32, (rows, LANES), 1)
    for ref, start, at in ((east_ref, 0, 0), (west_ref, columns - LANES, LANES - 1)):
        line = jnp.zeros((rows, planes), jnp.float32)
        for r in range(rows):
            pick = ((lane == at) & (row == r)).astype(jnp.float32).astype(jnp.bfloat16)
            side = adj_ref[:, r, start : start + LANES].astype(jnp.bfloat16)
            line = line + lax.dot_general(
                pick, side, (((1,), (1,)), ((), ())), preferred_element_type=jnp.float32
            )
        ref[...] = line.astype(jnp.bfloat16)


def edges(adjoint):
    levels, fields, rows, columns = adjoint.shape
    planes = levels * fields
    vmem = pl.BlockSpec(memory_space=pltpu.VMEM)
    side = jax.ShapeDtypeStruct((rows, planes), jnp.bfloat16)
    row = jax.ShapeDtypeStruct((planes, columns), jnp.bfloat16)
    return pl.pallas_call(
        edge_kernel,
        out_shape=(row, row, side, side),
        in_specs=[vmem],
        out_specs=(vmem,) * 4,
        compiler_params=pltpu.CompilerParams(vmem_limit_bytes=VMEM_BYTES),
        cost_estimate=pl.CostEstimate(flops=1000, bytes_accessed=100000, transcendentals=0),
        name="edges",
    )(adjoint.reshape(planes, rows, columns))


def local_kernel(
    adj_ref, flow_ref, mask_ref, mix_ref,
    hor_ref, coef_ref, weight_north_ref, weight_south_ref, weight_east_ref, weight_west_ref,
):
    levels, fields, rows, columns = adj_ref.shape
    planes = levels * fields
    shape = (rows, columns)
    lane = lax.broadcasted_iota(jnp.int32, shape, 1)
    sub = lax.broadcasted_iota(jnp.int32, shape, 0)
    last_column, first_column = lane == columns - 1, lane == 0
    last_row, first_row = sub == rows - 1, sub == 0

    row = lax.broadcasted_iota(jnp.int32, (rows, LANES), 0)
    short_lane = lax.broadcasted_iota(jnp.int32, (rows, LANES), 1)
    repeat = (
        lax.broadcasted_iota(jnp.int32, (levels, planes), 1) // fields
        == lax.broadcasted_iota(jnp.int32, (levels, planes), 0)
    ).astype(jnp.float32)
    for ref, start, at, half in (
        (weight_east_ref, columns - LANES, LANES - 1, 0.5),
        (weight_west_ref, 0, 0, -0.5),
    ):
        line = jnp.zeros((rows, levels), jnp.float32)
        for r in range(rows):
            pick = ((short_lane == at) & (row == r)).astype(jnp.float32)
            line = line + lax.dot_general(
                pick,
                flow_ref[:, 0, r, start : start + LANES],
                (((1,), (1,)), ((), ())),
                precision=lax.Precision.HIGHEST,
                preferred_element_type=jnp.float32,
            )
        line = jnp.dot(
            line, repeat, precision=lax.Precision.HIGHEST, preferred_element_type=jnp.float32
        )
        ref[...] = diffusion_rate + half * line

    def level(k, state):
        lower, ratio_prev = state
        mask = mask_ref[k].astype(jnp.float32)
        below = jnp.minimum(k + 1, levels - 1)
        mask_below = mask_ref[below].astype(jnp.float32)
        mix = mix_ref[jnp.minimum(k, levels - 2)]
        upper = jnp.where(k < levels - 1, mix * mask * mask_below, 0.0)
        inverse = 1.0 / (1.0 + lower + upper + lower * ratio_prev)
        ratio = -upper * inverse
        mask_inv = mask * inverse
        coef_ref[0, k] = mask_inv
        coef_ref[1, k] = lower * inverse
        coef_ref[2, k] = ratio
        flow_along, flow_cross = flow_ref[k, 0], flow_ref[k, 1]
        north_weight = diffusion_rate + 0.5 * flow_cross[rows - 1 : rows, :]
        south_weight = diffusion_rate - 0.5 * flow_cross[0:1, :]
        centers, advects, alongs, crosses = [], [], [], []
        for f in range(fields):
            weight_north_ref[pl.ds(k * fields + f, 1), :] = north_weight
            weight_south_ref[pl.ds(k * fields + f, 1), :] = south_weight
            x = adj_ref[k, f]
            east = jnp.where(last_column, 0.0, pltpu.roll(x, columns - 1, 1))
            west = jnp.where(first_column, 0.0, pltpu.roll(x, 1, 1))
            north = jnp.where(last_row, 0.0, pltpu.roll(x, rows - 1, 0))
            south = jnp.where(first_row, 0.0, pltpu.roll(x, 1, 0))
            along = 0.5 * (east - west)
            cross = 0.5 * (north - south)
            advect = (
                x
                + diffusion_rate * (east + west + north + south - 4.0 * x)
                + flow_along * along
                + flow_cross * cross
            )
            centers.append(x)
            advects.append(advect)
            alongs.append(along)
            crosses.append(cross)
        diverge = alongs[2] + crosses[3]
        buoy_along = thermal_coef * alongs[0] - haline_coef * alongs[1]
        buoy_cross = thermal_coef * crosses[0] - haline_coef * crosses[1]
        hor_ref[k, 0] = mask_inv * (advects[0] - thermal_coef * couple_rate * diverge)
        hor_ref[k, 1] = mask_inv * (advects[1] + haline_coef * couple_rate * diverge)
        hor_ref[k, 2] = mask_inv * (advects[2] + coriolis * centers[3] + couple_rate * buoy_along)
        hor_ref[k, 3] = mask_inv * (advects[3] - coriolis * centers[2] + couple_rate * buoy_cross)
        return upper, ratio

    zero = jnp.zeros(shape, jnp.float32)
    lax.fori_loop(0, levels, level, (zero, zero))


def local_part(adjoint, flow, land_mask, mixing):
    levels, fields, rows, columns = adjoint.shape
    planes = levels * fields
    vmem = pl.BlockSpec(memory_space=pltpu.VMEM)
    shape = lambda *dims: jax.ShapeDtypeStruct(dims, jnp.float32)
    return pl.pallas_call(
        local_kernel,
        out_shape=(
            shape(*adjoint.shape),
            shape(3, levels, rows, columns),
            shape(planes, columns),
            shape(planes, columns),
            shape(rows, planes),
            shape(rows, planes),
        ),
        in_specs=[vmem] * 4,
        out_specs=(vmem,) * 6,
        compiler_params=pltpu.CompilerParams(vmem_limit_bytes=VMEM_BYTES),
        cost_estimate=pl.CostEstimate(flops=1000, bytes_accessed=100000, transcendentals=0),
        name="local_part",
    )(adjoint, flow, land_mask, mixing)


def turned_edge(edge, code):
    planes = edge.shape[1]
    cosine = jnp.where(code == 0, 1.0, 0.0) - jnp.where(code == 2, 1.0, 0.0)
    sine = jnp.where(code == 1, 1.0, 0.0) - jnp.where(code == 3, 1.0, 0.0)
    field = lax.broadcasted_iota(jnp.int32, edge.shape, 1) & 3
    zonal = cosine * edge - sine * pltpu.roll(edge, planes - 1, 1)
    meridional = sine * pltpu.roll(edge, 1, 1) + cosine * edge
    return jnp.where(field == 2, zonal, jnp.where(field == 3, meridional, edge))


def edge_term(edge, weight, sign, axis, vector):
    planes = edge.shape[axis]
    field = lax.broadcasted_iota(jnp.int32, edge.shape, axis) & 3
    ahead = lambda n: pltpu.roll(edge, planes - n, axis)
    behind = lambda n: pltpu.roll(edge, n, axis)
    thermal = sign * 0.5 * thermal_coef * couple_rate
    haline = sign * 0.5 * haline_coef * couple_rate
    other = thermal * behind(vector) - haline * behind(vector - 1)
    mixed = jnp.where(field == 0, -thermal * ahead(vector), 0.0)
    mixed = jnp.where(field == 1, haline * ahead(vector - 1), mixed)
    mixed = jnp.where(field == vector, other, mixed)
    return weight * edge + mixed


def start_with_edges(
    acc, own_code, next_code, north_ref, south_ref, east_ref, west_ref,
    weight_north, weight_south, weight_east, weight_west,
):
    rows, planes, columns = acc.shape
    east = turned_edge(east_ref[...].astype(jnp.float32), (4 - next_code) & 3)
    west = turned_edge(west_ref[...].astype(jnp.float32), own_code)
    fill = jnp.zeros((LANES - rows, planes), jnp.float32)
    tall = lambda line: jnp.transpose(jnp.concatenate([line, fill], axis=0))
    east = tall(edge_term(east, weight_east[...], 1.0, 1, 2))
    west = tall(edge_term(west, weight_west[...], -1.0, 1, 2))
    north = edge_term(north_ref[...].astype(jnp.float32), weight_north[...], 1.0, 0, 3)
    south = edge_term(south_ref[...].astype(jnp.float32), weight_south[...], -1.0, 0, 3)
    lane = lax.broadcasted_iota(jnp.int32, (planes, LANES), 1)
    blank = jnp.zeros((planes, columns - 2 * LANES), jnp.float32)
    for c in range(rows):
        first = jnp.where(lane == 0, jnp.broadcast_to(west[:, c : c + 1], lane.shape), 0.0)
        last = jnp.where(lane == LANES - 1, jnp.broadcast_to(east[:, c : c + 1], lane.shape), 0.0)
        line = jnp.concatenate([first, blank, last], axis=1) if blank.shape[1] else (
            jnp.concatenate([first, last], axis=1)
        )
        if c == 0:
            line = line + south
        if c == rows - 1:
            line = line + north
        acc[c] = line


GATHER_BLOCKS = 3


def lane_order(head_f, line_ref, capacity):
    tiles = head_f.shape[0]
    pitch = capacity + HEAD_ROWS
    lane = lax.broadcasted_iota(jnp.int32, (1, LANES), 1)
    for t in range(tiles * pitch // LANES):
        line = jnp.zeros((1, LANES), jnp.float32)
        for source in range(tiles):
            start = source * pitch - t * LANES
            if start < LANES and start + capacity > 0:
                inside = (lane >= start) & (lane < start + capacity)
                line = jnp.where(inside, head_f[source : source + 1, :], line)
        line_ref[:, t * LANES : (t + 1) * LANES] = line


def finish_kernel(
    seam_ref, got_hbm, heads_hbm, north_ref, south_ref, east_ref, west_ref, hor_hbm, coef_hbm,
    weight_north_hbm, weight_south_hbm, weight_east_hbm, weight_west_hbm,
    out_hbm, acc, out_ref, hor_ref, coef_ref,
    weight_north, weight_south, weight_east, weight_west,
    got_ref, heads_ref, head_f, row_line, column_line, sems, got_sems, out_sems,
):
    slots, width = got_ref.shape
    tiles = heads_ref.shape[0]
    capacity = slots // tiles - HEAD_ROWS
    levels, fields, rows, columns = out_ref.shape
    depth = slots // GATHER_BLOCKS
    heads_copy = pltpu.make_async_copy(
        heads_hbm.at[:, capacity // HEAD_ROWS], heads_ref, sems.at[6]
    )
    heads_copy.start()
    got_copies = []
    for i in range(GATHER_BLOCKS):
        span = pl.ds(i * depth, depth)
        copy = pltpu.make_async_copy(got_hbm.at[span], got_ref.at[span], got_sems.at[i])
        copy.start()
        got_copies.append(copy)
    weight_copies = [
        pltpu.make_async_copy(source, target, sems.at[i])
        for i, (source, target) in enumerate(
            (
                (weight_north_hbm, weight_north),
                (weight_south_hbm, weight_south),
                (weight_east_hbm, weight_east),
                (weight_west_hbm, weight_west),
            )
        )
    ]
    solve_copies = [
        pltpu.make_async_copy(hor_hbm, hor_ref, sems.at[4]),
        pltpu.make_async_copy(coef_hbm, coef_ref, sems.at[5]),
    ]
    for copy in weight_copies + solve_copies:
        copy.start()
    along_rank = lax.axis_index("along")
    own_code = seam_ref[along_rank]
    next_code = seam_ref[lax.rem(along_rank + 1, seam_ref.shape[0])]
    for copy in weight_copies:
        copy.wait()
    start_with_edges(
        acc, own_code, next_code, north_ref, south_ref, east_ref, west_ref,
        weight_north, weight_south, weight_east, weight_west,
    )

    heads_copy.wait()
    heads = heads_ref[...].astype(jnp.float32)
    for i, line_ref in enumerate((row_line, column_line)):
        head_f[i] = heads[:, i, :]
        lane_order(head_f.at[i], line_ref, capacity)
    column_id = lax.broadcasted_iota(jnp.int32, (columns, depth), 0).astype(jnp.float32)
    zero = jnp.zeros((width, depth), jnp.bfloat16)
    for i in range(GATHER_BLOCKS):
        got_copies[i].wait()
        turned = jnp.transpose(got_ref[i * depth : (i + 1) * depth, :])
        row_of = row_line[:, i * depth : (i + 1) * depth]
        column_of = column_line[:, i * depth : (i + 1) * depth]
        onehot = (column_id == column_of).astype(jnp.float32).astype(jnp.bfloat16)
        row_wide = jnp.broadcast_to(row_of, (width, depth)).astype(jnp.bfloat16)
        masked = jnp.concatenate(
            [jnp.where(row_wide == (c + 1), turned, zero) for c in range(rows)], axis=0
        )
        part = lax.dot_general(
            masked, onehot, (((1,), (1,)), ((), ())), preferred_element_type=jnp.float32
        )
        acc[...] += part.reshape(rows, width, columns)

    for copy in solve_copies:
        copy.wait()

    def forward(q, previous):
        forcing = jnp.swapaxes(acc[:, pl.ds(pl.multiple_of(q * 8, 8), 8), :], 0, 1)
        state = list(previous)
        for i in range(8 // fields):
            k = q * (8 // fields) + i
            mask_inv, lower_inv = coef_ref[0, k], coef_ref[1, k]
            for f in range(fields):
                state[f] = (
                    hor_ref[k, f] + mask_inv * forcing[i * fields + f] + lower_inv * state[f]
                )
                out_ref[k, f] = state[f]
        return tuple(state)

    zero = jnp.zeros((rows, columns), jnp.float32)
    last = lax.fori_loop(0, levels * fields // 8, forward, (zero,) * fields)

    def backward(step, below):
        k = levels - 2 - step
        ratio = coef_ref[2, k]
        here = []
        for f in range(fields):
            here.append(out_ref[k, f] - ratio * below[f])
            out_ref[k, f] = here[f]
        return tuple(here)

    below = last
    out_copies = []
    part = levels // PARTS
    done = 0
    for i in range(PARTS):
        steps = part - 1 if i == 0 else part
        below = lax.fori_loop(done, done + steps, backward, below)
        done += steps
        span = pl.ds(levels - (i + 1) * part, part)
        copy = pltpu.make_async_copy(out_ref.at[span], out_hbm.at[span], out_sems.at[i])
        copy.start()
        out_copies.append(copy)
    for copy in out_copies:
        copy.wait()


def finish(seam_code, got, halos, local, tiles):
    hor, coef, weights = local[0], local[1], local[2:]
    slots, width = got.shape
    heads = got.reshape(tiles, slots // tiles // HEAD_ROWS, HEAD_ROWS, width)
    levels, fields, rows, columns = hor.shape
    planes = levels * fields
    vmem = pl.BlockSpec(memory_space=pltpu.VMEM)
    hbm = pl.BlockSpec(memory_space=pltpu.HBM)
    return pl.pallas_call(
        finish_kernel,
        out_shape=jax.ShapeDtypeStruct(hor.shape, jnp.float32),
        in_specs=[pl.BlockSpec(memory_space=pltpu.SMEM)] + [hbm] * 2 + [vmem] * 4 + [hbm] * 6,
        out_specs=hbm,
        scratch_shapes=[
            pltpu.VMEM((rows, planes, columns), jnp.float32),
            pltpu.VMEM(hor.shape, jnp.float32),
            pltpu.VMEM(hor.shape, jnp.float32),
            pltpu.VMEM(coef.shape, jnp.float32),
        ]
        + [pltpu.VMEM(w.shape, jnp.float32) for w in weights]
        + [
            pltpu.VMEM((slots, width), jnp.bfloat16),
            pltpu.VMEM((tiles, HEAD_ROWS, width), jnp.bfloat16),
            pltpu.VMEM((2, tiles, LANES), jnp.float32),
            pltpu.VMEM((1, slots), jnp.float32),
            pltpu.VMEM((1, slots), jnp.float32),
            pltpu.SemaphoreType.DMA((7,)),
            pltpu.SemaphoreType.DMA((GATHER_BLOCKS,)),
            pltpu.SemaphoreType.DMA((PARTS,)),
        ],
        compiler_params=pltpu.CompilerParams(vmem_limit_bytes=WIDE_VMEM_BYTES),
        name="finish",
    )(seam_code, got, heads, *halos, hor, coef, *weights)


def per_device(adjoint, flow, land_mask, mixing, seam_code, obs_misfit, obs_owner, obs_cell):
    levels, fields, rows, columns = adjoint.shape
    along_count = lax.axis_size("along")
    cross_count = lax.axis_size("cross")
    devices = along_count * cross_count
    capacity = 2 * obs_misfit.shape[0] // devices
    packed = pack_rows(obs_owner, obs_cell, obs_misfit, devices, capacity)
    packed, adjoint = lax.optimization_barrier((packed, adjoint))
    slots, width = packed.shape
    pairs = packed.reshape(slots // HEAD_ROWS, HEAD_ROWS, width)
    got = lax.all_to_all(pairs, ("along", "cross"), split_axis=0, concat_axis=0, tiled=True)
    got = got.reshape(slots, width)

    ring_up = [(i, (i + 1) % along_count) for i in range(along_count)]
    ring_down = [(target, source) for source, target in ring_up]
    line_up = [(i, i + 1) for i in range(cross_count - 1)]
    line_down = [(target, source) for source, target in line_up]
    first_row, last_row, first_column, last_column = edges(adjoint)
    west = lax.ppermute(last_column, "along", ring_up)
    east = lax.ppermute(first_column, "along", ring_down)
    south = lax.ppermute(last_row, "cross", line_up)
    north = lax.ppermute(first_row, "cross", line_down)
    local = local_part(adjoint, flow, land_mask, mixing)
    return finish(seam_code, got, (north, south, east, west), local, devices)


def solution(mesh):
    return jax.shard_map(
        per_device,
        mesh=mesh,
        in_specs=(
            P(None, None, "cross", "along"),
            P(None, None, "cross", "along"),
            P(None, "cross", "along"),
            P(None, "cross", "along"),
            P(),
            P(("along", "cross"), None),
            P(("along", "cross"), None),
            P(("along", "cross")),
        ),
        out_specs=P(None, None, "cross", "along"),
        check_vma=False,
    )
```

```python
import functools

import jax
import jax.numpy as jnp
from jax import lax
from jax.experimental import pallas as pl
from jax.experimental.pallas import tpu as pltpu
from jax.sharding import PartitionSpec as P

diffusion_rate = 0.15
coriolis = 0.3
couple_rate = 0.3
thermal_coef = 0.8
haline_coef = 0.6

LANES = 128
HEAD_ROWS = 2
PARTS = 4
VMEM_BYTES = 20 * 1024 * 1024
WIDE_VMEM_BYTES = 61 * 1024 * 1024


def pack_kernel(
    owner_hbm, cell_hbm, rows_hbm, out_hbm,
    owner_ref, cell_ref, rows_ref, out_ref, stage, rows_f, slot_v, slot_s, sems, out_sems,
    *, tiles,
):
    block_rows = out_ref.shape[0] // tiles
    capacity = block_rows - HEAD_ROWS
    blocks = owner_ref.shape[0]
    half = blocks // 2
    owner_copy = pltpu.make_async_copy(owner_hbm, owner_ref, sems.at[0])
    cell_copy = pltpu.make_async_copy(cell_hbm, cell_ref, sems.at[1])
    rows_copy = pltpu.make_async_copy(rows_hbm, rows_ref, sems.at[2])
    owner_copy.start()
    cell_copy.start()
    rows_copy.start()
    tile_id = lax.broadcasted_iota(jnp.int32, (tiles, LANES), 0)
    low = lax.broadcasted_iota(jnp.int32, (LANES, 2 * LANES), 0)
    high = lax.broadcasted_iota(jnp.int32, (LANES, 2 * LANES), 1)
    count_with = ((low <= high) | (high >= LANES)).astype(jnp.float32).astype(jnp.bfloat16)
    device = lax.axis_index("along") * lax.axis_size("cross") + lax.axis_index("cross")
    place = lax.broadcasted_iota(jnp.int32, (LANES, LANES), 0) - device * block_rows
    place = (place & (LANES - 1)).astype(jnp.float32)
    carry = jnp.zeros((tiles, LANES), jnp.float32)
    total = jnp.zeros((tiles, 2 * LANES), jnp.float32)
    owner_copy.wait()
    cell_copy.wait()
    slot_copies = []
    for b in range(blocks):
        owner = owner_ref[b : b + 1, :]
        cell = cell_ref[b : b + 1, :]
        hit = (tile_id == owner).astype(jnp.float32)
        hit_narrow = hit.astype(jnp.bfloat16)
        counts = jnp.dot(hit_narrow, count_with, preferred_element_type=jnp.float32)
        rank = jnp.sum((counts[:, :LANES] + carry) * hit, axis=0, keepdims=True) - 1.0
        carry = carry + counts[:, LANES:]
        slot_v[b : b + 1, :] = owner * block_rows + rank.astype(jnp.int32)
        row_part = ((cell >> 8) + 1).astype(jnp.float32)
        column_part = (cell & 255).astype(jnp.float32)
        here = place == rank
        values = jnp.concatenate(
            [jnp.where(here, row_part, 0.0), jnp.where(here, column_part, 0.0)], axis=0
        ).astype(jnp.bfloat16)
        total = total + lax.dot_general(
            hit_narrow, values, (((1,), (1,)), ((), ())), preferred_element_type=jnp.float32
        )
        if (b + 1) % half == 0:
            span = pl.ds(b + 1 - half, half)
            copy = pltpu.make_async_copy(
                slot_v.at[span], slot_s.at[span], sems.at[3 + len(slot_copies)]
            )
            copy.start()
            slot_copies.append(copy)
    stage[pl.ds(capacity, tiles, stride=block_rows), :] = total[:, :LANES]
    stage[pl.ds(capacity + 1, tiles, stride=block_rows), :] = total[:, LANES:]
    rows_copy.wait()
    rows_f[...] = rows_ref[...].astype(jnp.float32)

    def scatter(b, carried):
        base = pl.multiple_of(b * LANES, LANES)
        for j in range(LANES):
            stage[pl.ds(slot_s[b, j], 1), :] = rows_f[pl.ds(base + j, 1), :]
        return carried

    for i, copy in enumerate(slot_copies):
        copy.wait()
        lax.fori_loop(i * half, (i + 1) * half, scatter, 0)

    step = out_ref.shape[0] // PARTS
    piece = capacity

    def narrow(i, carried):
        span = pl.ds(pl.multiple_of(i * piece, piece), piece)
        out_ref[span, :] = stage[span, :].astype(jnp.bfloat16)
        return carried

    out_copies = []
    for i in range(PARTS):
        lax.fori_loop(i * step // piece, (i + 1) * step // piece, narrow, 0, unroll=3)
        span = pl.ds(i * step, step)
        copy = pltpu.make_async_copy(out_ref.at[span], out_hbm.at[span], out_sems.at[i])
        copy.start()
        out_copies.append(copy)
    for copy in out_copies:
        copy.wait()


def pack_rows(obs_owner, obs_cell, obs_misfit, tiles, capacity):
    obs_rows, width = obs_misfit.shape
    blocks = obs_rows // LANES
    slots = tiles * (capacity + HEAD_ROWS)
    hbm = pl.BlockSpec(memory_space=pltpu.HBM)
    return pl.pallas_call(
        functools.partial(pack_kernel, tiles=tiles),
        out_shape=jax.ShapeDtypeStruct((slots, width), jnp.bfloat16),
        in_specs=[hbm] * 3,
        out_specs=hbm,
        scratch_shapes=[
            pltpu.VMEM((blocks, LANES), jnp.int32),
            pltpu.VMEM((blocks, LANES), jnp.int32),
            pltpu.VMEM((obs_rows, width), jnp.bfloat16),
            pltpu.VMEM((slots, width), jnp.bfloat16),
            pltpu.VMEM((slots, width), jnp.float32),
            pltpu.VMEM((obs_rows, width), jnp.float32),
            pltpu.VMEM((blocks, LANES), jnp.int32),
            pltpu.SMEM((blocks, LANES), jnp.int32),
            pltpu.SemaphoreType.DMA((5,)),
            pltpu.SemaphoreType.DMA((PARTS,)),
        ],
        compiler_params=pltpu.CompilerParams(vmem_limit_bytes=WIDE_VMEM_BYTES),
        name="pack_rows",
    )(obs_owner.reshape(blocks, LANES), obs_cell.reshape(blocks, LANES), obs_misfit)


def edge_kernel(adj_ref, north_ref, south_ref, east_ref, west_ref):
    planes, rows, columns = adj_ref.shape
    north_ref[...] = adj_ref[:, 0, :].astype(jnp.bfloat16)
    south_ref[...] = adj_ref[:, rows - 1, :].astype(jnp.bfloat16)
    row = lax.broadcasted_iota(jnp.int32, (rows, LANES), 0)
    lane = lax.broadcasted_iota(jnp.int32, (rows, LANES), 1)
    for ref, start, at in ((east_ref, 0, 0), (west_ref, columns - LANES, LANES - 1)):
        line = jnp.zeros((rows, planes), jnp.float32)
        for r in range(rows):
            pick = ((lane == at) & (row == r)).astype(jnp.float32).astype(jnp.bfloat16)
            side = adj_ref[:, r, start : start + LANES].astype(jnp.bfloat16)
            line = line + lax.dot_general(
                pick, side, (((1,), (1,)), ((), ())), preferred_element_type=jnp.float32
            )
        ref[...] = line.astype(jnp.bfloat16)


def edges(adjoint):
    levels, fields, rows, columns = adjoint.shape
    planes = levels * fields
    vmem = pl.BlockSpec(memory_space=pltpu.VMEM)
    side = jax.ShapeDtypeStruct((rows, planes), jnp.bfloat16)
    row = jax.ShapeDtypeStruct((planes, columns), jnp.bfloat16)
    return pl.pallas_call(
        edge_kernel,
        out_shape=(row, row, side, side),
        in_specs=[vmem],
        out_specs=(vmem,) * 4,
        compiler_params=pltpu.CompilerParams(vmem_limit_bytes=VMEM_BYTES),
        cost_estimate=pl.CostEstimate(flops=1000, bytes_accessed=100000, transcendentals=0),
        name="edges",
    )(adjoint.reshape(planes, rows, columns))


def local_kernel(
    adj_ref, flow_ref, mask_ref, mix_ref,
    hor_ref, coef_ref, weight_north_ref, weight_south_ref, weight_east_ref, weight_west_ref,
):
    levels, fields, rows, columns = adj_ref.shape
    planes = levels * fields
    shape = (rows, columns)
    lane = lax.broadcasted_iota(jnp.int32, shape, 1)
    sub = lax.broadcasted_iota(jnp.int32, shape, 0)
    last_column, first_column = lane == columns - 1, lane == 0
    last_row, first_row = sub == rows - 1, sub == 0

    row = lax.broadcasted_iota(jnp.int32, (rows, LANES), 0)
    short_lane = lax.broadcasted_iota(jnp.int32, (rows, LANES), 1)
    repeat = (
        lax.broadcasted_iota(jnp.int32, (levels, planes), 1) // fields
        == lax.broadcasted_iota(jnp.int32, (levels, planes), 0)
    ).astype(jnp.float32)
    for ref, start, at, half in (
        (weight_east_ref, columns - LANES, LANES - 1, 0.5),
        (weight_west_ref, 0, 0, -0.5),
    ):
        line = jnp.zeros((rows, levels), jnp.float32)
        for r in range(rows):
            pick = ((short_lane == at) & (row == r)).astype(jnp.float32)
            line = line + lax.dot_general(
                pick,
                flow_ref[:, 0, r, start : start + LANES],
                (((1,), (1,)), ((), ())),
                precision=lax.Precision.HIGHEST,
                preferred_element_type=jnp.float32,
            )
        line = jnp.dot(
            line, repeat, precision=lax.Precision.HIGHEST, preferred_element_type=jnp.float32
        )
        ref[...] = diffusion_rate + half * line

    def level(k, state):
        lower, ratio_prev = state
        mask = mask_ref[k].astype(jnp.float32)
        below = jnp.minimum(k + 1, levels - 1)
        mask_below = mask_ref[below].astype(jnp.float32)
        mix = mix_ref[jnp.minimum(k, levels - 2)]
        upper = jnp.where(k < levels - 1, mix * mask * mask_below, 0.0)
        inverse = 1.0 / (1.0 + lower + upper + lower * ratio_prev)
        ratio = -upper * inverse
        mask_inv = mask * inverse
        coef_ref[0, k] = mask_inv
        coef_ref[1, k] = lower * inverse
        coef_ref[2, k] = ratio
        flow_along, flow_cross = flow_ref[k, 0], flow_ref[k, 1]
        north_weight = diffusion_rate + 0.5 * flow_cross[rows - 1 : rows, :]
        south_weight = diffusion_rate - 0.5 * flow_cross[0:1, :]
        centers, advects, alongs, crosses = [], [], [], []
        for f in range(fields):
            weight_north_ref[pl.ds(k * fields + f, 1), :] = north_weight
            weight_south_ref[pl.ds(k * fields + f, 1), :] = south_weight
            x = adj_ref[k, f]
            east = jnp.where(last_column, 0.0, pltpu.roll(x, columns - 1, 1))
            west = jnp.where(first_column, 0.0, pltpu.roll(x, 1, 1))
            north = jnp.where(last_row, 0.0, pltpu.roll(x, rows - 1, 0))
            south = jnp.where(first_row, 0.0, pltpu.roll(x, 1, 0))
            along = 0.5 * (east - west)
            cross = 0.5 * (north - south)
            advect = (
                x
                + diffusion_rate * (east + west + north + south - 4.0 * x)
                + flow_along * along
                + flow_cross * cross
            )
            centers.append(x)
            advects.append(advect)
            alongs.append(along)
            crosses.append(cross)
        diverge = alongs[2] + crosses[3]
        buoy_along = thermal_coef * alongs[0] - haline_coef * alongs[1]
        buoy_cross = thermal_coef * crosses[0] - haline_coef * crosses[1]
        hor_ref[k, 0] = mask_inv * (advects[0] - thermal_coef * couple_rate * diverge)
        hor_ref[k, 1] = mask_inv * (advects[1] + haline_coef * couple_rate * diverge)
        hor_ref[k, 2] = mask_inv * (advects[2] + coriolis * centers[3] + couple_rate * buoy_along)
        hor_ref[k, 3] = mask_inv * (advects[3] - coriolis * centers[2] + couple_rate * buoy_cross)
        return upper, ratio

    zero = jnp.zeros(shape, jnp.float32)
    lax.fori_loop(0, levels, level, (zero, zero))


def local_part(adjoint, flow, land_mask, mixing):
    levels, fields, rows, columns = adjoint.shape
    planes = levels * fields
    vmem = pl.BlockSpec(memory_space=pltpu.VMEM)
    shape = lambda *dims: jax.ShapeDtypeStruct(dims, jnp.float32)
    return pl.pallas_call(
        local_kernel,
        out_shape=(
            shape(*adjoint.shape),
            shape(3, levels, rows, columns),
            shape(planes, columns),
            shape(planes, columns),
            shape(rows, planes),
            shape(rows, planes),
        ),
        in_specs=[vmem] * 4,
        out_specs=(vmem,) * 6,
        compiler_params=pltpu.CompilerParams(vmem_limit_bytes=VMEM_BYTES),
        cost_estimate=pl.CostEstimate(flops=1000, bytes_accessed=100000, transcendentals=0),
        name="local_part",
    )(adjoint, flow, land_mask, mixing)


def turned_edge(edge, code):
    planes = edge.shape[1]
    cosine = jnp.where(code == 0, 1.0, 0.0) - jnp.where(code == 2, 1.0, 0.0)
    sine = jnp.where(code == 1, 1.0, 0.0) - jnp.where(code == 3, 1.0, 0.0)
    field = lax.broadcasted_iota(jnp.int32, edge.shape, 1) & 3
    zonal = cosine * edge - sine * pltpu.roll(edge, planes - 1, 1)
    meridional = sine * pltpu.roll(edge, 1, 1) + cosine * edge
    return jnp.where(field == 2, zonal, jnp.where(field == 3, meridional, edge))


def edge_term(edge, weight, sign, axis, vector):
    planes = edge.shape[axis]
    field = lax.broadcasted_iota(jnp.int32, edge.shape, axis) & 3
    ahead = lambda n: pltpu.roll(edge, planes - n, axis)
    behind = lambda n: pltpu.roll(edge, n, axis)
    thermal = sign * 0.5 * thermal_coef * couple_rate
    haline = sign * 0.5 * haline_coef * couple_rate
    other = thermal * behind(vector) - haline * behind(vector - 1)
    mixed = jnp.where(field == 0, -thermal * ahead(vector), 0.0)
    mixed = jnp.where(field == 1, haline * ahead(vector - 1), mixed)
    mixed = jnp.where(field == vector, other, mixed)
    return weight * edge + mixed


def start_with_edges(
    acc, own_code, next_code, north_ref, south_ref, east_ref, west_ref,
    weight_north, weight_south, weight_east, weight_west,
):
    rows, planes, columns = acc.shape
    east = turned_edge(east_ref[...].astype(jnp.float32), (4 - next_code) & 3)
    west = turned_edge(west_ref[...].astype(jnp.float32), own_code)
    fill = jnp.zeros((LANES - rows, planes), jnp.float32)
    tall = lambda line: jnp.transpose(jnp.concatenate([line, fill], axis=0))
    east = tall(edge_term(east, weight_east[...], 1.0, 1, 2))
    west = tall(edge_term(west, weight_west[...], -1.0, 1, 2))
    north = edge_term(north_ref[...].astype(jnp.float32), weight_north[...], 1.0, 0, 3)
    south = edge_term(south_ref[...].astype(jnp.float32), weight_south[...], -1.0, 0, 3)
    lane = lax.broadcasted_iota(jnp.int32, (planes, LANES), 1)
    blank = jnp.zeros((planes, columns - 2 * LANES), jnp.float32)
    for c in range(rows):
        first = jnp.where(lane == 0, jnp.broadcast_to(west[:, c : c + 1], lane.shape), 0.0)
        last = jnp.where(lane == LANES - 1, jnp.broadcast_to(east[:, c : c + 1], lane.shape), 0.0)
        line = jnp.concatenate([first, blank, last], axis=1) if blank.shape[1] else (
            jnp.concatenate([first, last], axis=1)
        )
        if c == 0:
            line = line + south
        if c == rows - 1:
            line = line + north
        acc[c] = line


GATHER_BLOCKS = 3


def lane_order(head_f, line_ref, capacity):
    tiles = head_f.shape[0]
    pitch = capacity + HEAD_ROWS
    lane = lax.broadcasted_iota(jnp.int32, (1, LANES), 1)
    for t in range(tiles * pitch // LANES):
        line = jnp.zeros((1, LANES), jnp.float32)
        for source in range(tiles):
            start = source * pitch - t * LANES
            if start < LANES and start + capacity > 0:
                inside = (lane >= start) & (lane < start + capacity)
                line = jnp.where(inside, head_f[source : source + 1, :], line)
        line_ref[:, t * LANES : (t + 1) * LANES] = line


def finish_kernel(
    seam_ref, got_hbm, heads_hbm, north_ref, south_ref, east_ref, west_ref, hor_hbm, coef_hbm,
    weight_north_hbm, weight_south_hbm, weight_east_hbm, weight_west_hbm,
    out_hbm, acc, out_ref, hor_ref, coef_ref,
    weight_north, weight_south, weight_east, weight_west,
    got_ref, heads_ref, head_f, row_line, column_line, sems, got_sems, out_sems,
):
    slots, width = got_ref.shape
    tiles = heads_ref.shape[0]
    capacity = slots // tiles - HEAD_ROWS
    levels, fields, rows, columns = out_ref.shape
    depth = slots // GATHER_BLOCKS
    heads_copy = pltpu.make_async_copy(
        heads_hbm.at[:, capacity // HEAD_ROWS], heads_ref, sems.at[6]
    )
    heads_copy.start()
    for i in range(GATHER_BLOCKS):
        span = pl.ds(i * depth, depth)
        pltpu.make_async_copy(got_hbm.at[span], got_ref.at[span], got_sems.at[i]).start()
    weight_copies = [
        pltpu.make_async_copy(source, target, sems.at[i])
        for i, (source, target) in enumerate(
            (
                (weight_north_hbm, weight_north),
                (weight_south_hbm, weight_south),
                (weight_east_hbm, weight_east),
                (weight_west_hbm, weight_west),
            )
        )
    ]
    solve_copies = [
        pltpu.make_async_copy(hor_hbm, hor_ref, sems.at[4]),
        pltpu.make_async_copy(coef_hbm, coef_ref, sems.at[5]),
    ]
    for copy in weight_copies + solve_copies:
        copy.start()
    along_rank = lax.axis_index("along")
    own_code = seam_ref[along_rank]
    next_code = seam_ref[lax.rem(along_rank + 1, seam_ref.shape[0])]
    for copy in weight_copies:
        copy.wait()
    start_with_edges(
        acc, own_code, next_code, north_ref, south_ref, east_ref, west_ref,
        weight_north, weight_south, weight_east, weight_west,
    )

    heads_copy.wait()
    heads = heads_ref[...].astype(jnp.float32)
    for i, line_ref in enumerate((row_line, column_line)):
        head_f[i] = heads[:, i, :]
        lane_order(head_f.at[i], line_ref, capacity)
    column_id = lax.broadcasted_iota(jnp.int32, (columns, depth), 0).astype(jnp.float32)
    zero = jnp.zeros((width, depth), jnp.bfloat16)

    def gather(i, carried):
        span = pl.ds(pl.multiple_of(i * depth, depth), depth)
        pltpu.make_async_copy(got_hbm.at[span], got_ref.at[span], got_sems.at[i]).wait()
        turned = jnp.transpose(got_ref[span, :])
        onehot = (column_id == column_line[:, span]).astype(jnp.float32).astype(jnp.bfloat16)
        row_wide = jnp.broadcast_to(row_line[:, span], (width, depth)).astype(jnp.bfloat16)
        masked = jnp.concatenate(
            [jnp.where(row_wide == (c + 1), turned, zero) for c in range(rows)], axis=0
        )
        part = lax.dot_general(
            masked, onehot, (((1,), (1,)), ((), ())), preferred_element_type=jnp.float32
        )
        acc[...] += part.reshape(rows, width, columns)
        return carried

    lax.fori_loop(0, GATHER_BLOCKS, gather, 0)

    for copy in solve_copies:
        copy.wait()

    def forward(q, previous):
        forcing = jnp.swapaxes(acc[:, pl.ds(pl.multiple_of(q * 8, 8), 8), :], 0, 1)
        state = list(previous)
        for i in range(8 // fields):
            k = q * (8 // fields) + i
            mask_inv, lower_inv = coef_ref[0, k], coef_ref[1, k]
            for f in range(fields):
                state[f] = (
                    hor_ref[k, f] + mask_inv * forcing[i * fields + f] + lower_inv * state[f]
                )
                out_ref[k, f] = state[f]
        return tuple(state)

    zero = jnp.zeros((rows, columns), jnp.float32)
    last = lax.fori_loop(0, levels * fields // 8, forward, (zero,) * fields)

    def backward(step, below):
        k = levels - 2 - step
        ratio = coef_ref[2, k]
        here = []
        for f in range(fields):
            here.append(out_ref[k, f] - ratio * below[f])
            out_ref[k, f] = here[f]
        return tuple(here)

    below = last
    out_copies = []
    part = levels // PARTS
    done = 0
    for i in range(PARTS):
        steps = part - 1 if i == 0 else part
        below = lax.fori_loop(done, done + steps, backward, below)
        done += steps
        span = pl.ds(levels - (i + 1) * part, part)
        copy = pltpu.make_async_copy(out_ref.at[span], out_hbm.at[span], out_sems.at[i])
        copy.start()
        out_copies.append(copy)
    for copy in out_copies:
        copy.wait()


def finish(seam_code, got, halos, local, tiles):
    hor, coef, weights = local[0], local[1], local[2:]
    slots, width = got.shape
    heads = got.reshape(tiles, slots // tiles // HEAD_ROWS, HEAD_ROWS, width)
    levels, fields, rows, columns = hor.shape
    planes = levels * fields
    vmem = pl.BlockSpec(memory_space=pltpu.VMEM)
    hbm = pl.BlockSpec(memory_space=pltpu.HBM)
    return pl.pallas_call(
        finish_kernel,
        out_shape=jax.ShapeDtypeStruct(hor.shape, jnp.float32),
        in_specs=[pl.BlockSpec(memory_space=pltpu.SMEM)] + [hbm] * 2 + [vmem] * 4 + [hbm] * 6,
        out_specs=hbm,
        scratch_shapes=[
            pltpu.VMEM((rows, planes, columns), jnp.float32),
            pltpu.VMEM(hor.shape, jnp.float32),
            pltpu.VMEM(hor.shape, jnp.float32),
            pltpu.VMEM(coef.shape, jnp.float32),
        ]
        + [pltpu.VMEM(w.shape, jnp.float32) for w in weights]
        + [
            pltpu.VMEM((slots, width), jnp.bfloat16),
            pltpu.VMEM((tiles, HEAD_ROWS, width), jnp.bfloat16),
            pltpu.VMEM((2, tiles, LANES), jnp.float32),
            pltpu.VMEM((1, slots), jnp.float32),
            pltpu.VMEM((1, slots), jnp.float32),
            pltpu.SemaphoreType.DMA((7,)),
            pltpu.SemaphoreType.DMA((GATHER_BLOCKS,)),
            pltpu.SemaphoreType.DMA((PARTS,)),
        ],
        compiler_params=pltpu.CompilerParams(vmem_limit_bytes=WIDE_VMEM_BYTES),
        name="finish",
    )(seam_code, got, heads, *halos, hor, coef, *weights)


def per_device(adjoint, flow, land_mask, mixing, seam_code, obs_misfit, obs_owner, obs_cell):
    levels, fields, rows, columns = adjoint.shape
    along_count = lax.axis_size("along")
    cross_count = lax.axis_size("cross")
    devices = along_count * cross_count
    capacity = 2 * obs_misfit.shape[0] // devices
    packed = pack_rows(obs_owner, obs_cell, obs_misfit, devices, capacity)
    packed, adjoint = lax.optimization_barrier((packed, adjoint))
    slots, width = packed.shape
    pairs = packed.reshape(slots // HEAD_ROWS, HEAD_ROWS, width)
    got = lax.all_to_all(pairs, ("along", "cross"), split_axis=0, concat_axis=0, tiled=True)
    got = got.reshape(slots, width)

    ring_up = [(i, (i + 1) % along_count) for i in range(along_count)]
    ring_down = [(target, source) for source, target in ring_up]
    line_up = [(i, i + 1) for i in range(cross_count - 1)]
    line_down = [(target, source) for source, target in line_up]
    first_row, last_row, first_column, last_column = edges(adjoint)
    west = lax.ppermute(last_column, "along", ring_up)
    east = lax.ppermute(first_column, "along", ring_down)
    south = lax.ppermute(last_row, "cross", line_up)
    north = lax.ppermute(first_row, "cross", line_down)
    local = local_part(adjoint, flow, land_mask, mixing)
    return finish(seam_code, got, (north, south, east, west), local, devices)


def solution(mesh):
    return jax.shard_map(
        per_device,
        mesh=mesh,
        in_specs=(
            P(None, None, "cross", "along"),
            P(None, None, "cross", "along"),
            P(None, "cross", "along"),
            P(None, "cross", "along"),
            P(),
            P(("along", "cross"), None),
            P(("along", "cross"), None),
            P(("along", "cross")),
        ),
        out_specs=P(None, None, "cross", "along"),
        check_vma=False,
    )
```

```python
import functools

import jax
import jax.numpy as jnp
from jax import lax
from jax.experimental import pallas as pl
from jax.experimental.pallas import tpu as pltpu
from jax.sharding import PartitionSpec as P

diffusion_rate = 0.15
coriolis = 0.3
couple_rate = 0.3
thermal_coef = 0.8
haline_coef = 0.6

LANES = 128
HEAD_ROWS = 2
PARTS = 4
CONVERT_AFTER = 16
LAST_VMEM_BYTES = 44 * 1024 * 1024
LOCAL_PLANES = 1536
WIDE_VMEM_BYTES = 61 * 1024 * 1024


def pack_kernel(
    owner_hbm, cell_hbm, rows_hbm, out_hbm,
    owner_ref, cell_ref, rows_ref, out_ref, stage, rows_f, slot_v, slot_s, sems, out_sems,
    *, tiles,
):
    block_rows = out_ref.shape[0] // tiles
    capacity = block_rows - HEAD_ROWS
    blocks = owner_ref.shape[0]
    half = blocks // 2
    owner_copy = pltpu.make_async_copy(owner_hbm, owner_ref, sems.at[0])
    cell_copy = pltpu.make_async_copy(cell_hbm, cell_ref, sems.at[1])
    rows_copy = pltpu.make_async_copy(rows_hbm, rows_ref, sems.at[2])
    owner_copy.start()
    cell_copy.start()
    rows_copy.start()
    tile_id = lax.broadcasted_iota(jnp.int32, (tiles, LANES), 0)
    low = lax.broadcasted_iota(jnp.int32, (LANES, 2 * LANES), 0)
    high = lax.broadcasted_iota(jnp.int32, (LANES, 2 * LANES), 1)
    count_with = ((low <= high) | (high >= LANES)).astype(jnp.float32).astype(jnp.bfloat16)
    device = lax.axis_index("along") * lax.axis_size("cross") + lax.axis_index("cross")
    place = lax.broadcasted_iota(jnp.int32, (LANES, LANES), 0) - device * block_rows
    place = (place & (LANES - 1)).astype(jnp.float32)
    carry = jnp.zeros((tiles, LANES), jnp.float32)
    total = jnp.zeros((tiles, 2 * LANES), jnp.float32)
    owner_copy.wait()
    cell_copy.wait()
    slot_copies = []
    for b in range(blocks):
        owner = owner_ref[b : b + 1, :]
        cell = cell_ref[b : b + 1, :]
        hit = (tile_id == owner).astype(jnp.float32)
        hit_narrow = hit.astype(jnp.bfloat16)
        counts = jnp.dot(hit_narrow, count_with, preferred_element_type=jnp.float32)
        rank = jnp.sum((counts[:, :LANES] + carry) * hit, axis=0, keepdims=True) - 1.0
        carry = carry + counts[:, LANES:]
        slot_v[b : b + 1, :] = owner * block_rows + rank.astype(jnp.int32)
        row_part = ((cell >> 8) + 1).astype(jnp.float32)
        column_part = (cell & 255).astype(jnp.float32)
        here = place == rank
        values = jnp.concatenate(
            [jnp.where(here, row_part, 0.0), jnp.where(here, column_part, 0.0)], axis=0
        ).astype(jnp.bfloat16)
        total = total + lax.dot_general(
            hit_narrow, values, (((1,), (1,)), ((), ())), preferred_element_type=jnp.float32
        )
        if b == CONVERT_AFTER:
            rows_copy.wait()
        if b >= CONVERT_AFTER:
            share = rows_ref.shape[0] // (blocks - CONVERT_AFTER)
            at = (b - CONVERT_AFTER) * share
            rows_f[at : at + share, :] = rows_ref[at : at + share, :].astype(jnp.float32)
        if (b + 1) % half == 0:
            span = pl.ds(b + 1 - half, half)
            copy = pltpu.make_async_copy(
                slot_v.at[span], slot_s.at[span], sems.at[3 + len(slot_copies)]
            )
            copy.start()
            slot_copies.append(copy)
    stage[pl.ds(capacity, tiles, stride=block_rows), :] = total[:, :LANES]
    stage[pl.ds(capacity + 1, tiles, stride=block_rows), :] = total[:, LANES:]

    def scatter(b, carried):
        base = pl.multiple_of(b * LANES, LANES)
        for j in range(LANES):
            stage[pl.ds(slot_s[b, j], 1), :] = rows_f[pl.ds(base + j, 1), :]
        return carried

    for i, copy in enumerate(slot_copies):
        copy.wait()
        lax.fori_loop(i * half, (i + 1) * half, scatter, 0)

    step = out_ref.shape[0] // PARTS
    piece = capacity

    def narrow(i, carried):
        span = pl.ds(pl.multiple_of(i * piece, piece), piece)
        out_ref[span, :] = stage[span, :].astype(jnp.bfloat16)
        return carried

    out_copies = []
    for i in range(PARTS):
        lax.fori_loop(i * step // piece, (i + 1) * step // piece, narrow, 0, unroll=3)
        span = pl.ds(i * step, step)
        copy = pltpu.make_async_copy(out_ref.at[span], out_hbm.at[span], out_sems.at[i])
        copy.start()
        out_copies.append(copy)
    for copy in out_copies:
        copy.wait()


def pack_rows(obs_owner, obs_cell, obs_misfit, tiles, capacity):
    obs_rows, width = obs_misfit.shape
    blocks = obs_rows // LANES
    slots = tiles * (capacity + HEAD_ROWS)
    hbm = pl.BlockSpec(memory_space=pltpu.HBM)
    return pl.pallas_call(
        functools.partial(pack_kernel, tiles=tiles),
        out_shape=jax.ShapeDtypeStruct((slots, width), jnp.bfloat16),
        in_specs=[hbm] * 3,
        out_specs=hbm,
        scratch_shapes=[
            pltpu.VMEM((blocks, LANES), jnp.int32),
            pltpu.VMEM((blocks, LANES), jnp.int32),
            pltpu.VMEM((obs_rows, width), jnp.bfloat16),
            pltpu.VMEM((slots, width), jnp.bfloat16),
            pltpu.VMEM((slots, width), jnp.float32),
            pltpu.VMEM((obs_rows, width), jnp.float32),
            pltpu.VMEM((blocks, LANES), jnp.int32),
            pltpu.SMEM((blocks, LANES), jnp.int32),
            pltpu.SemaphoreType.DMA((5,)),
            pltpu.SemaphoreType.DMA((PARTS,)),
        ],
        compiler_params=pltpu.CompilerParams(vmem_limit_bytes=WIDE_VMEM_BYTES),
        name="pack_rows",
    )(obs_owner.reshape(blocks, LANES), obs_cell.reshape(blocks, LANES), obs_misfit)


def edge_kernel(adj_ref, north_ref, south_ref, east_ref, west_ref):
    planes, rows, columns = adj_ref.shape
    north_ref[...] = adj_ref[:, 0, :].astype(jnp.bfloat16)
    south_ref[...] = adj_ref[:, rows - 1, :].astype(jnp.bfloat16)
    row = lax.broadcasted_iota(jnp.int32, (rows, LANES), 0)
    lane = lax.broadcasted_iota(jnp.int32, (rows, LANES), 1)
    for ref, start, at in ((east_ref, 0, 0), (west_ref, columns - LANES, LANES - 1)):
        line = jnp.zeros((rows, planes), jnp.float32)
        for r in range(rows):
            pick = ((lane == at) & (row == r)).astype(jnp.float32).astype(jnp.bfloat16)
            side = adj_ref[:, r, start : start + LANES].astype(jnp.bfloat16)
            line = line + lax.dot_general(
                pick, side, (((1,), (1,)), ((), ())), preferred_element_type=jnp.float32
            )
        ref[...] = line.astype(jnp.bfloat16)


def edges(adjoint):
    levels, fields, rows, columns = adjoint.shape
    planes = levels * fields
    vmem = pl.BlockSpec(memory_space=pltpu.VMEM)
    side = jax.ShapeDtypeStruct((rows, planes), jnp.bfloat16)
    row = jax.ShapeDtypeStruct((planes, columns), jnp.bfloat16)
    return pl.pallas_call(
        edge_kernel,
        out_shape=(row, row, side, side),
        in_specs=[vmem],
        out_specs=(vmem,) * 4,
        compiler_params=pltpu.CompilerParams(vmem_limit_bytes=WIDE_VMEM_BYTES),
        cost_estimate=pl.CostEstimate(flops=1000, bytes_accessed=100000, transcendentals=0),
        name="edges",
    )(adjoint.reshape(planes, rows, columns))


def local_kernel(
    adj_ref, flow_ref, mask_ref, mix_ref, local_hbm, hor_ref, coef_ref, weight_ref, sems,
):
    levels, fields, rows, columns = adj_ref.shape
    planes = levels * fields
    shape = (rows, columns)
    lane = lax.broadcasted_iota(jnp.int32, shape, 1)
    sub = lax.broadcasted_iota(jnp.int32, shape, 0)
    last_column, first_column = lane == columns - 1, lane == 0
    last_row, first_row = sub == rows - 1, sub == 0

    row = lax.broadcasted_iota(jnp.int32, (rows, LANES), 0)
    short_lane = lax.broadcasted_iota(jnp.int32, (rows, LANES), 1)
    repeat = (
        lax.broadcasted_iota(jnp.int32, (levels, planes), 1) // fields
        == lax.broadcasted_iota(jnp.int32, (levels, planes), 0)
    ).astype(jnp.float32)
    row_planes = planes // rows
    for place, start, at, half in ((0, columns - LANES, LANES - 1, 0.5), (planes, 0, 0, -0.5)):
        line = jnp.zeros((rows, levels), jnp.float32)
        for r in range(rows):
            pick = ((short_lane == at) & (row == r)).astype(jnp.float32)
            line = line + lax.dot_general(
                pick,
                flow_ref[:, 0, r, start : start + LANES],
                (((1,), (1,)), ((), ())),
                precision=lax.Precision.HIGHEST,
                preferred_element_type=jnp.float32,
            )
        line = jnp.dot(
            line, repeat, precision=lax.Precision.HIGHEST, preferred_element_type=jnp.float32
        )
        weight_ref[2 * row_planes, :, place : place + planes] = diffusion_rate + half * line

    def level(k, state):
        lower, ratio_prev = state
        mask = mask_ref[k].astype(jnp.float32)
        below = jnp.minimum(k + 1, levels - 1)
        mask_below = mask_ref[below].astype(jnp.float32)
        mix = mix_ref[jnp.minimum(k, levels - 2)]
        upper = jnp.where(k < levels - 1, mix * mask * mask_below, 0.0)
        inverse = 1.0 / (1.0 + lower + upper + lower * ratio_prev)
        ratio = -upper * inverse
        mask_inv = mask * inverse
        coef_ref[k] = mask_inv
        coef_ref[levels + k] = lower * inverse
        coef_ref[2 * levels + k] = ratio
        flow_along, flow_cross = flow_ref[k, 0], flow_ref[k, 1]
        north_weight = diffusion_rate + 0.5 * flow_cross[rows - 1 : rows, :]
        south_weight = diffusion_rate - 0.5 * flow_cross[0:1, :]
        centers, advects, alongs, crosses = [], [], [], []
        for f in range(fields):
            at = k * fields + f
            weight_ref[at // rows, pl.ds(at % rows, 1), :] = north_weight
            weight_ref[row_planes + at // rows, pl.ds(at % rows, 1), :] = south_weight
            x = adj_ref[k, f]
            east = jnp.where(last_column, 0.0, pltpu.roll(x, columns - 1, 1))
            west = jnp.where(first_column, 0.0, pltpu.roll(x, 1, 1))
            north = jnp.where(last_row, 0.0, pltpu.roll(x, rows - 1, 0))
            south = jnp.where(first_row, 0.0, pltpu.roll(x, 1, 0))
            along = 0.5 * (east - west)
            cross = 0.5 * (north - south)
            advect = (
                x
                + diffusion_rate * (east + west + north + south - 4.0 * x)
                + flow_along * along
                + flow_cross * cross
            )
            centers.append(x)
            advects.append(advect)
            alongs.append(along)
            crosses.append(cross)
        diverge = alongs[2] + crosses[3]
        buoy_along = thermal_coef * alongs[0] - haline_coef * alongs[1]
        buoy_cross = thermal_coef * crosses[0] - haline_coef * crosses[1]
        hor_ref[k * fields + 0] = mask_inv * (advects[0] - thermal_coef * couple_rate * diverge)
        hor_ref[k * fields + 1] = mask_inv * (advects[1] + haline_coef * couple_rate * diverge)
        hor_ref[k * fields + 2] = mask_inv * (advects[2] + coriolis * centers[3] + couple_rate * buoy_along)
        hor_ref[k * fields + 3] = mask_inv * (advects[3] - coriolis * centers[2] + couple_rate * buoy_cross)
        return upper, ratio

    zero = jnp.zeros(shape, jnp.float32)
    lax.fori_loop(0, levels, level, (zero, zero))
    copies = local_copies(local_hbm, (hor_ref, coef_ref, weight_ref), sems, False)
    for copy in copies:
        copy.start()
    for copy in copies:
        copy.wait()


def local_copies(local_hbm, refs, sems, inward):
    copies, at = [], 0
    for i, ref in enumerate(refs):
        part = local_hbm.at[pl.ds(at, ref.shape[0])]
        source, target = (part, ref) if inward else (ref, part)
        copies.append(pltpu.make_async_copy(source, target, sems.at[i]))
        at += ref.shape[0]
    return copies


def local_scratch(levels, fields, rows, columns):
    planes = levels * fields
    return [
        pltpu.VMEM((planes, rows, columns), jnp.float32),
        pltpu.VMEM((3 * levels, rows, columns), jnp.float32),
        pltpu.VMEM((2 * planes // rows + 1, rows, columns), jnp.float32),
    ]


def local_part(adjoint, flow, land_mask, mixing):
    levels, fields, rows, columns = adjoint.shape
    vmem = pl.BlockSpec(memory_space=pltpu.VMEM)
    return pl.pallas_call(
        local_kernel,
        out_shape=jax.ShapeDtypeStruct((LOCAL_PLANES, rows, columns), jnp.float32),
        in_specs=[vmem] * 4,
        out_specs=pl.BlockSpec(memory_space=pltpu.HBM),
        scratch_shapes=local_scratch(*adjoint.shape) + [pltpu.SemaphoreType.DMA((3,))],
        compiler_params=pltpu.CompilerParams(vmem_limit_bytes=WIDE_VMEM_BYTES),
        cost_estimate=pl.CostEstimate(flops=1000, bytes_accessed=100000, transcendentals=0),
        name="local_part",
    )(adjoint, flow, land_mask, mixing)


def turned_edge(edge, code):
    planes = edge.shape[1]
    cosine = jnp.where(code == 0, 1.0, 0.0) - jnp.where(code == 2, 1.0, 0.0)
    sine = jnp.where(code == 1, 1.0, 0.0) - jnp.where(code == 3, 1.0, 0.0)
    field = lax.broadcasted_iota(jnp.int32, edge.shape, 1) & 3
    zonal = cosine * edge - sine * pltpu.roll(edge, planes - 1, 1)
    meridional = sine * pltpu.roll(edge, 1, 1) + cosine * edge
    return jnp.where(field == 2, zonal, jnp.where(field == 3, meridional, edge))


def edge_term(edge, weight, sign, axis, vector):
    planes = edge.shape[axis]
    field = lax.broadcasted_iota(jnp.int32, edge.shape, axis) & 3
    ahead = lambda n: pltpu.roll(edge, planes - n, axis)
    behind = lambda n: pltpu.roll(edge, n, axis)
    thermal = sign * 0.5 * thermal_coef * couple_rate
    haline = sign * 0.5 * haline_coef * couple_rate
    other = thermal * behind(vector) - haline * behind(vector - 1)
    mixed = jnp.where(field == 0, -thermal * ahead(vector), 0.0)
    mixed = jnp.where(field == 1, haline * ahead(vector - 1), mixed)
    mixed = jnp.where(field == vector, other, mixed)
    return weight * edge + mixed


def start_with_edges(
    acc, own_code, next_code, north_ref, south_ref, east_ref, west_ref, weight_ref
):
    rows, planes, columns = acc.shape
    row_planes = planes // rows
    weight_north = weight_ref[0:row_planes].reshape(planes, columns)
    weight_south = weight_ref[row_planes : 2 * row_planes].reshape(planes, columns)
    weight_east = weight_ref[2 * row_planes, :, 0:planes]
    weight_west = weight_ref[2 * row_planes, :, planes : 2 * planes]
    east = turned_edge(east_ref[...].astype(jnp.float32), (4 - next_code) & 3)
    west = turned_edge(west_ref[...].astype(jnp.float32), own_code)
    fill = jnp.zeros((LANES - rows, planes), jnp.float32)
    tall = lambda line: jnp.transpose(jnp.concatenate([line, fill], axis=0))
    east = tall(edge_term(east, weight_east, 1.0, 1, 2))
    west = tall(edge_term(west, weight_west, -1.0, 1, 2))
    north = edge_term(north_ref[...].astype(jnp.float32), weight_north, 1.0, 0, 3)
    south = edge_term(south_ref[...].astype(jnp.float32), weight_south, -1.0, 0, 3)
    lane = lax.broadcasted_iota(jnp.int32, (planes, LANES), 1)
    blank = jnp.zeros((planes, columns - 2 * LANES), jnp.float32)
    for c in range(rows):
        first = jnp.where(lane == 0, jnp.broadcast_to(west[:, c : c + 1], lane.shape), 0.0)
        last = jnp.where(lane == LANES - 1, jnp.broadcast_to(east[:, c : c + 1], lane.shape), 0.0)
        line = jnp.concatenate([first, blank, last], axis=1) if blank.shape[1] else (
            jnp.concatenate([first, last], axis=1)
        )
        if c == 0:
            line = line + south
        if c == rows - 1:
            line = line + north
        acc[c] = line


GATHER_BLOCKS = 3


def lane_order(head_f, line_ref, capacity):
    tiles = head_f.shape[0]
    pitch = capacity + HEAD_ROWS
    lane = lax.broadcasted_iota(jnp.int32, (1, LANES), 1)
    for t in range(tiles * pitch // LANES):
        line = jnp.zeros((1, LANES), jnp.float32)
        for source in range(tiles):
            start = source * pitch - t * LANES
            if start < LANES and start + capacity > 0:
                inside = (lane >= start) & (lane < start + capacity)
                line = jnp.where(inside, head_f[source : source + 1, :], line)
        line_ref[:, t * LANES : (t + 1) * LANES] = line


def finish_kernel(
    seam_ref, got_ref, heads_ref, north_ref, south_ref, east_ref, west_ref, local_hbm,
    out_hbm, acc, out_ref, hor_ref, coef_ref, weight_ref,
    head_f, row_line, column_line, sems, out_sems,
):
    slots, width = got_ref.shape
    tiles, pairs = heads_ref.shape[0], heads_ref.shape[1]
    capacity = slots // tiles - HEAD_ROWS
    levels, fields, rows, columns = out_ref.shape
    depth = slots // GATHER_BLOCKS
    copies = local_copies(local_hbm, (hor_ref, coef_ref, weight_ref), sems, True)
    for copy in copies[::-1]:
        copy.start()
    along_rank = lax.axis_index("along")
    own_code = seam_ref[along_rank]
    next_code = seam_ref[lax.rem(along_rank + 1, seam_ref.shape[0])]
    copies[2].wait()
    start_with_edges(
        acc, own_code, next_code, north_ref, south_ref, east_ref, west_ref, weight_ref
    )

    heads = heads_ref[:, pairs - 1].astype(jnp.float32)
    for i, line_ref in enumerate((row_line, column_line)):
        head_f[i] = heads[:, i, :]
        lane_order(head_f.at[i], line_ref, capacity)
    column_id = lax.broadcasted_iota(jnp.int32, (columns, depth), 0).astype(jnp.float32)
    zero = jnp.zeros((width, depth), jnp.bfloat16)

    def gather(i, carried):
        span = pl.ds(pl.multiple_of(i * depth, depth), depth)
        turned = jnp.transpose(got_ref[span, :])
        onehot = (column_id == column_line[:, span]).astype(jnp.float32).astype(jnp.bfloat16)
        row_wide = jnp.broadcast_to(row_line[:, span], (width, depth)).astype(jnp.bfloat16)
        masked = jnp.concatenate(
            [jnp.where(row_wide == (c + 1), turned, zero) for c in range(rows)], axis=0
        )
        part = lax.dot_general(
            masked, onehot, (((1,), (1,)), ((), ())), preferred_element_type=jnp.float32
        )
        acc[...] += part.reshape(rows, width, columns)
        return carried

    lax.fori_loop(0, GATHER_BLOCKS, gather, 0)

    copies[0].wait()
    copies[1].wait()

    def forward(q, previous):
        forcing = jnp.swapaxes(acc[:, pl.ds(pl.multiple_of(q * 8, 8), 8), :], 0, 1)
        state = list(previous)
        for i in range(8 // fields):
            k = q * (8 // fields) + i
            mask_inv, lower_inv = coef_ref[k], coef_ref[levels + k]
            for f in range(fields):
                state[f] = (
                    hor_ref[k * fields + f] + mask_inv * forcing[i * fields + f] + lower_inv * state[f]
                )
                out_ref[k, f] = state[f]
        return tuple(state)

    zero = jnp.zeros((rows, columns), jnp.float32)
    last = lax.fori_loop(0, levels * fields // 8, forward, (zero,) * fields)

    def backward(step, below):
        k = levels - 2 - step
        ratio = coef_ref[2 * levels + k]
        here = []
        for f in range(fields):
            here.append(out_ref[k, f] - ratio * below[f])
            out_ref[k, f] = here[f]
        return tuple(here)

    below = last
    out_copies = []
    part = levels // PARTS
    done = 0
    for i in range(PARTS):
        steps = part - 1 if i == 0 else part
        below = lax.fori_loop(done, done + steps, backward, below)
        done += steps
        span = pl.ds(levels - (i + 1) * part, part)
        copy = pltpu.make_async_copy(out_ref.at[span], out_hbm.at[span], out_sems.at[i])
        copy.start()
        out_copies.append(copy)
    for copy in out_copies:
        copy.wait()


def finish(seam_code, got, halos, local, tiles, shape):
    slots, width = got.shape
    heads = got.reshape(tiles, slots // tiles // HEAD_ROWS, HEAD_ROWS, width)
    levels, fields, rows, columns = shape
    vmem = pl.BlockSpec(memory_space=pltpu.VMEM)
    hbm = pl.BlockSpec(memory_space=pltpu.HBM)
    return pl.pallas_call(
        finish_kernel,
        out_shape=jax.ShapeDtypeStruct(shape, jnp.float32),
        in_specs=[pl.BlockSpec(memory_space=pltpu.SMEM)] + [vmem] * 6 + [hbm],
        out_specs=hbm,
        scratch_shapes=[
            pltpu.VMEM((rows, levels * fields, columns), jnp.float32),
            pltpu.VMEM(shape, jnp.float32),
        ]
        + local_scratch(*shape)
        + [
            pltpu.VMEM((2, tiles, LANES), jnp.float32),
            pltpu.VMEM((1, slots), jnp.float32),
            pltpu.VMEM((1, slots), jnp.float32),
            pltpu.SemaphoreType.DMA((3,)),
            pltpu.SemaphoreType.DMA((PARTS,)),
        ],
        compiler_params=pltpu.CompilerParams(vmem_limit_bytes=LAST_VMEM_BYTES),
        name="finish",
    )(seam_code, got, heads, *halos, local)


def per_device(adjoint, flow, land_mask, mixing, seam_code, obs_misfit, obs_owner, obs_cell):
    levels, fields, rows, columns = adjoint.shape
    along_count = lax.axis_size("along")
    cross_count = lax.axis_size("cross")
    devices = along_count * cross_count
    capacity = 2 * obs_misfit.shape[0] // devices
    packed = pack_rows(obs_owner, obs_cell, obs_misfit, devices, capacity)
    packed, adjoint = lax.optimization_barrier((packed, adjoint))
    slots, width = packed.shape
    pairs = packed.reshape(slots // HEAD_ROWS, HEAD_ROWS, width)
    got = lax.all_to_all(pairs, ("along", "cross"), split_axis=0, concat_axis=0, tiled=True)
    got = got.reshape(slots, width)

    ring_up = [(i, (i + 1) % along_count) for i in range(along_count)]
    ring_down = [(target, source) for source, target in ring_up]
    line_up = [(i, i + 1) for i in range(cross_count - 1)]
    line_down = [(target, source) for source, target in line_up]
    first_row, last_row, first_column, last_column = edges(adjoint)
    west = lax.ppermute(last_column, "along", ring_up)
    east = lax.ppermute(first_column, "along", ring_down)
    south = lax.ppermute(last_row, "cross", line_up)
    north = lax.ppermute(first_row, "cross", line_down)
    local = local_part(adjoint, flow, land_mask, mixing)
    return finish(seam_code, got, (north, south, east, west), local, devices, adjoint.shape)


def solution(mesh):
    return jax.shard_map(
        per_device,
        mesh=mesh,
        in_specs=(
            P(None, None, "cross", "along"),
            P(None, None, "cross", "along"),
            P(None, "cross", "along"),
            P(None, "cross", "along"),
            P(),
            P(("along", "cross"), None),
            P(("along", "cross"), None),
            P(("along", "cross")),
        ),
        out_specs=P(None, None, "cross", "along"),
        check_vma=False,
    )
```

```python
import functools

import jax
import jax.numpy as jnp
from jax import lax
from jax.experimental import pallas as pl
from jax.experimental.pallas import tpu as pltpu
from jax.sharding import PartitionSpec as P

diffusion_rate = 0.15
coriolis = 0.3
couple_rate = 0.3
thermal_coef = 0.8
haline_coef = 0.6

LANES = 128
HEAD_ROWS = 2
PARTS = 4
LAST_VMEM_BYTES = 44 * 1024 * 1024
LOCAL_VMEM_BYTES = 50 * 1024 * 1024
LOCAL_PLANES = 1536
WIDE_VMEM_BYTES = 61 * 1024 * 1024


def pack_kernel(
    owner_hbm, cell_hbm, rows_hbm, out_hbm,
    owner_ref, cell_ref, rows_ref, out_ref, stage, rows_f, slot_v, slot_s, sems, out_sems,
    *, tiles,
):
    block_rows = out_ref.shape[0] // tiles
    capacity = block_rows - HEAD_ROWS
    blocks = owner_ref.shape[0]
    half = blocks // 2
    owner_copy = pltpu.make_async_copy(owner_hbm, owner_ref, sems.at[0])
    cell_copy = pltpu.make_async_copy(cell_hbm, cell_ref, sems.at[1])
    rows_copy = pltpu.make_async_copy(rows_hbm, rows_ref, sems.at[2])
    owner_copy.start()
    cell_copy.start()
    rows_copy.start()
    tile_id = lax.broadcasted_iota(jnp.int32, (tiles, LANES), 0)
    low = lax.broadcasted_iota(jnp.int32, (LANES, 2 * LANES), 0)
    high = lax.broadcasted_iota(jnp.int32, (LANES, 2 * LANES), 1)
    count_with = ((low <= high) | (high >= LANES)).astype(jnp.float32).astype(jnp.bfloat16)
    device = lax.axis_index("along") * lax.axis_size("cross") + lax.axis_index("cross")
    place = lax.broadcasted_iota(jnp.int32, (LANES, LANES), 0) - device * block_rows
    place = (place & (LANES - 1)).astype(jnp.float32)
    carry = jnp.zeros((tiles, LANES), jnp.float32)
    total = jnp.zeros((tiles, 2 * LANES), jnp.float32)
    owner_copy.wait()
    cell_copy.wait()
    slot_copies = []
    for b in range(blocks):
        owner = owner_ref[b : b + 1, :]
        cell = cell_ref[b : b + 1, :]
        hit = (tile_id == owner).astype(jnp.float32)
        hit_narrow = hit.astype(jnp.bfloat16)
        counts = jnp.dot(hit_narrow, count_with, preferred_element_type=jnp.float32)
        rank = jnp.sum((counts[:, :LANES] + carry) * hit, axis=0, keepdims=True) - 1.0
        carry = carry + counts[:, LANES:]
        slot_v[b : b + 1, :] = owner * block_rows + rank.astype(jnp.int32)
        row_part = ((cell >> 8) + 1).astype(jnp.float32)
        column_part = (cell & 255).astype(jnp.float32)
        here = place == rank
        values = jnp.concatenate(
            [jnp.where(here, row_part, 0.0), jnp.where(here, column_part, 0.0)], axis=0
        ).astype(jnp.bfloat16)
        total = total + lax.dot_general(
            hit_narrow, values, (((1,), (1,)), ((), ())), preferred_element_type=jnp.float32
        )
        if (b + 1) % half == 0:
            span = pl.ds(b + 1 - half, half)
            copy = pltpu.make_async_copy(
                slot_v.at[span], slot_s.at[span], sems.at[3 + len(slot_copies)]
            )
            copy.start()
            slot_copies.append(copy)
    stage[pl.ds(capacity, tiles, stride=block_rows), :] = total[:, :LANES]
    stage[pl.ds(capacity + 1, tiles, stride=block_rows), :] = total[:, LANES:]
    rows_copy.wait()
    rows_f[...] = rows_ref[...].astype(jnp.float32)

    def scatter(b, carried):
        base = pl.multiple_of(b * LANES, LANES)
        for j in range(LANES):
            stage[pl.ds(slot_s[b, j], 1), :] = rows_f[pl.ds(base + j, 1), :]
        return carried

    for i, copy in enumerate(slot_copies):
        copy.wait()
        lax.fori_loop(i * half, (i + 1) * half, scatter, 0)

    step = out_ref.shape[0] // PARTS
    piece = capacity

    def narrow(i, carried):
        span = pl.ds(pl.multiple_of(i * piece, piece), piece)
        out_ref[span, :] = stage[span, :].astype(jnp.bfloat16)
        return carried

    out_copies = []
    for i in range(PARTS):
        lax.fori_loop(i * step // piece, (i + 1) * step // piece, narrow, 0, unroll=3)
        span = pl.ds(i * step, step)
        copy = pltpu.make_async_copy(out_ref.at[span], out_hbm.at[span], out_sems.at[i])
        copy.start()
        out_copies.append(copy)
    for copy in out_copies:
        copy.wait()


def pack_rows(obs_owner, obs_cell, obs_misfit, tiles, capacity):
    obs_rows, width = obs_misfit.shape
    blocks = obs_rows // LANES
    slots = tiles * (capacity + HEAD_ROWS)
    hbm = pl.BlockSpec(memory_space=pltpu.HBM)
    return pl.pallas_call(
        functools.partial(pack_kernel, tiles=tiles),
        out_shape=jax.ShapeDtypeStruct((slots, width), jnp.bfloat16),
        in_specs=[hbm] * 3,
        out_specs=hbm,
        scratch_shapes=[
            pltpu.VMEM((blocks, LANES), jnp.int32),
            pltpu.VMEM((blocks, LANES), jnp.int32),
            pltpu.VMEM((obs_rows, width), jnp.bfloat16),
            pltpu.VMEM((slots, width), jnp.bfloat16),
            pltpu.VMEM((slots, width), jnp.float32),
            pltpu.VMEM((obs_rows, width), jnp.float32),
            pltpu.VMEM((blocks, LANES), jnp.int32),
            pltpu.SMEM((blocks, LANES), jnp.int32),
            pltpu.SemaphoreType.DMA((5,)),
            pltpu.SemaphoreType.DMA((PARTS,)),
        ],
        compiler_params=pltpu.CompilerParams(vmem_limit_bytes=WIDE_VMEM_BYTES),
        name="pack_rows",
    )(obs_owner.reshape(blocks, LANES), obs_cell.reshape(blocks, LANES), obs_misfit)


def edge_kernel(adj_ref, north_ref, south_ref, east_ref, west_ref):
    planes, rows, columns = adj_ref.shape
    north_ref[...] = adj_ref[:, 0, :].astype(jnp.bfloat16)
    south_ref[...] = adj_ref[:, rows - 1, :].astype(jnp.bfloat16)
    row = lax.broadcasted_iota(jnp.int32, (rows, LANES), 0)
    lane = lax.broadcasted_iota(jnp.int32, (rows, LANES), 1)
    for ref, start, at in ((east_ref, 0, 0), (west_ref, columns - LANES, LANES - 1)):
        line = jnp.zeros((rows, planes), jnp.float32)
        for r in range(rows):
            pick = ((lane == at) & (row == r)).astype(jnp.float32).astype(jnp.bfloat16)
            side = adj_ref[:, r, start : start + LANES].astype(jnp.bfloat16)
            line = line + lax.dot_general(
                pick, side, (((1,), (1,)), ((), ())), preferred_element_type=jnp.float32
            )
        ref[...] = line.astype(jnp.bfloat16)


def edges(adjoint):
    levels, fields, rows, columns = adjoint.shape
    planes = levels * fields
    vmem = pl.BlockSpec(memory_space=pltpu.VMEM)
    side = jax.ShapeDtypeStruct((rows, planes), jnp.bfloat16)
    row = jax.ShapeDtypeStruct((planes, columns), jnp.bfloat16)
    return pl.pallas_call(
        edge_kernel,
        out_shape=(row, row, side, side),
        in_specs=[vmem],
        out_specs=(vmem,) * 4,
        compiler_params=pltpu.CompilerParams(vmem_limit_bytes=WIDE_VMEM_BYTES),
        cost_estimate=pl.CostEstimate(flops=1000, bytes_accessed=100000, transcendentals=0),
        name="edges",
    )(adjoint.reshape(planes, rows, columns))


def local_kernel(
    adj_ref, flow_ref, mask_ref, mix_ref, local_hbm, weight_ref, hor_ref, coef_ref, sems,
):
    levels, fields, rows, columns = adj_ref.shape
    planes = levels * fields
    shape = (rows, columns)
    lane = lax.broadcasted_iota(jnp.int32, shape, 1)
    sub = lax.broadcasted_iota(jnp.int32, shape, 0)
    last_column, first_column = lane == columns - 1, lane == 0
    last_row, first_row = sub == rows - 1, sub == 0

    row = lax.broadcasted_iota(jnp.int32, (rows, LANES), 0)
    short_lane = lax.broadcasted_iota(jnp.int32, (rows, LANES), 1)
    repeat = (
        lax.broadcasted_iota(jnp.int32, (levels, planes), 1) // fields
        == lax.broadcasted_iota(jnp.int32, (levels, planes), 0)
    ).astype(jnp.float32)
    row_planes = planes // rows
    for place, start, at, half in ((0, columns - LANES, LANES - 1, 0.5), (planes, 0, 0, -0.5)):
        line = jnp.zeros((rows, levels), jnp.float32)
        for r in range(rows):
            pick = ((short_lane == at) & (row == r)).astype(jnp.float32)
            line = line + lax.dot_general(
                pick,
                flow_ref[:, 0, r, start : start + LANES],
                (((1,), (1,)), ((), ())),
                precision=lax.Precision.HIGHEST,
                preferred_element_type=jnp.float32,
            )
        line = jnp.dot(
            line, repeat, precision=lax.Precision.HIGHEST, preferred_element_type=jnp.float32
        )
        weight_ref[2 * row_planes, :, place : place + planes] = diffusion_rate + half * line

    def level(k, state):
        lower, ratio_prev = state
        mask = mask_ref[k].astype(jnp.float32)
        below = jnp.minimum(k + 1, levels - 1)
        mask_below = mask_ref[below].astype(jnp.float32)
        mix = mix_ref[jnp.minimum(k, levels - 2)]
        upper = jnp.where(k < levels - 1, mix * mask * mask_below, 0.0)
        inverse = 1.0 / (1.0 + lower + upper + lower * ratio_prev)
        ratio = -upper * inverse
        mask_inv = mask * inverse
        coef_ref[k] = mask_inv
        coef_ref[levels + k] = lower * inverse
        coef_ref[2 * levels + k] = ratio
        flow_along, flow_cross = flow_ref[k, 0], flow_ref[k, 1]
        north_weight = diffusion_rate + 0.5 * flow_cross[rows - 1 : rows, :]
        south_weight = diffusion_rate - 0.5 * flow_cross[0:1, :]
        centers, advects, alongs, crosses = [], [], [], []
        for f in range(fields):
            at = k * fields + f
            weight_ref[at // rows, pl.ds(at % rows, 1), :] = north_weight
            weight_ref[row_planes + at // rows, pl.ds(at % rows, 1), :] = south_weight
            x = adj_ref[k, f]
            east = jnp.where(last_column, 0.0, pltpu.roll(x, columns - 1, 1))
            west = jnp.where(first_column, 0.0, pltpu.roll(x, 1, 1))
            north = jnp.where(last_row, 0.0, pltpu.roll(x, rows - 1, 0))
            south = jnp.where(first_row, 0.0, pltpu.roll(x, 1, 0))
            along = 0.5 * (east - west)
            cross = 0.5 * (north - south)
            advect = (
                x
                + diffusion_rate * (east + west + north + south - 4.0 * x)
                + flow_along * along
                + flow_cross * cross
            )
            centers.append(x)
            advects.append(advect)
            alongs.append(along)
            crosses.append(cross)
        diverge = alongs[2] + crosses[3]
        buoy_along = thermal_coef * alongs[0] - haline_coef * alongs[1]
        buoy_cross = thermal_coef * crosses[0] - haline_coef * crosses[1]
        hor_ref[k * fields + 0] = mask_inv * (advects[0] - thermal_coef * couple_rate * diverge)
        hor_ref[k * fields + 1] = mask_inv * (advects[1] + haline_coef * couple_rate * diverge)
        hor_ref[k * fields + 2] = mask_inv * (advects[2] + coriolis * centers[3] + couple_rate * buoy_along)
        hor_ref[k * fields + 3] = mask_inv * (advects[3] - coriolis * centers[2] + couple_rate * buoy_cross)
        return upper, ratio

    zero = jnp.zeros(shape, jnp.float32)
    lax.fori_loop(0, levels, level, (zero, zero))
    copies = local_copies(local_hbm, (hor_ref, coef_ref), sems, False)
    for copy in copies:
        copy.start()
    for copy in copies:
        copy.wait()


def local_copies(local_hbm, refs, sems, inward):
    copies, at = [], 0
    for i, ref in enumerate(refs):
        part = local_hbm.at[pl.ds(at, ref.shape[0])]
        source, target = (part, ref) if inward else (ref, part)
        copies.append(pltpu.make_async_copy(source, target, sems.at[i]))
        at += ref.shape[0]
    return copies


def local_scratch(levels, fields, rows, columns):
    planes = levels * fields
    return [
        pltpu.VMEM((planes, rows, columns), jnp.float32),
        pltpu.VMEM((3 * levels, rows, columns), jnp.float32),
    ]


def local_part(adjoint, flow, land_mask, mixing):
    levels, fields, rows, columns = adjoint.shape
    vmem = pl.BlockSpec(memory_space=pltpu.VMEM)
    return pl.pallas_call(
        local_kernel,
        out_shape=(
            jax.ShapeDtypeStruct((LOCAL_PLANES, rows, columns), jnp.float32),
            jax.ShapeDtypeStruct((2 * levels * fields // rows + 1, rows, columns), jnp.float32),
        ),
        in_specs=[vmem] * 4,
        out_specs=(pl.BlockSpec(memory_space=pltpu.HBM), vmem),
        scratch_shapes=local_scratch(*adjoint.shape) + [pltpu.SemaphoreType.DMA((2,))],
        compiler_params=pltpu.CompilerParams(vmem_limit_bytes=LOCAL_VMEM_BYTES),
        cost_estimate=pl.CostEstimate(flops=1000, bytes_accessed=100000, transcendentals=0),
        name="local_part",
    )(adjoint, flow, land_mask, mixing)


def turned_edge(edge, code):
    planes = edge.shape[1]
    cosine = jnp.where(code == 0, 1.0, 0.0) - jnp.where(code == 2, 1.0, 0.0)
    sine = jnp.where(code == 1, 1.0, 0.0) - jnp.where(code == 3, 1.0, 0.0)
    field = lax.broadcasted_iota(jnp.int32, edge.shape, 1) & 3
    zonal = cosine * edge - sine * pltpu.roll(edge, planes - 1, 1)
    meridional = sine * pltpu.roll(edge, 1, 1) + cosine * edge
    return jnp.where(field == 2, zonal, jnp.where(field == 3, meridional, edge))


def edge_term(edge, weight, sign, axis, vector):
    planes = edge.shape[axis]
    field = lax.broadcasted_iota(jnp.int32, edge.shape, axis) & 3
    ahead = lambda n: pltpu.roll(edge, planes - n, axis)
    behind = lambda n: pltpu.roll(edge, n, axis)
    thermal = sign * 0.5 * thermal_coef * couple_rate
    haline = sign * 0.5 * haline_coef * couple_rate
    other = thermal * behind(vector) - haline * behind(vector - 1)
    mixed = jnp.where(field == 0, -thermal * ahead(vector), 0.0)
    mixed = jnp.where(field == 1, haline * ahead(vector - 1), mixed)
    mixed = jnp.where(field == vector, other, mixed)
    return weight * edge + mixed


def start_with_edges(
    acc, own_code, next_code, north_ref, south_ref, east_ref, west_ref, weight_ref
):
    rows, planes, columns = acc.shape
    row_planes = planes // rows
    weight_north = weight_ref[0:row_planes].reshape(planes, columns)
    weight_south = weight_ref[row_planes : 2 * row_planes].reshape(planes, columns)
    weight_east = weight_ref[2 * row_planes, :, 0:planes]
    weight_west = weight_ref[2 * row_planes, :, planes : 2 * planes]
    east = turned_edge(east_ref[...].astype(jnp.float32), (4 - next_code) & 3)
    west = turned_edge(west_ref[...].astype(jnp.float32), own_code)
    fill = jnp.zeros((LANES - rows, planes), jnp.float32)
    tall = lambda line: jnp.transpose(jnp.concatenate([line, fill], axis=0))
    east = tall(edge_term(east, weight_east, 1.0, 1, 2))
    west = tall(edge_term(west, weight_west, -1.0, 1, 2))
    north = edge_term(north_ref[...].astype(jnp.float32), weight_north, 1.0, 0, 3)
    south = edge_term(south_ref[...].astype(jnp.float32), weight_south, -1.0, 0, 3)
    lane = lax.broadcasted_iota(jnp.int32, (planes, LANES), 1)
    blank = jnp.zeros((planes, columns - 2 * LANES), jnp.float32)
    for c in range(rows):
        first = jnp.where(lane == 0, jnp.broadcast_to(west[:, c : c + 1], lane.shape), 0.0)
        last = jnp.where(lane == LANES - 1, jnp.broadcast_to(east[:, c : c + 1], lane.shape), 0.0)
        line = jnp.concatenate([first, blank, last], axis=1) if blank.shape[1] else (
            jnp.concatenate([first, last], axis=1)
        )
        if c == 0:
            line = line + south
        if c == rows - 1:
            line = line + north
        acc[c] = line


GATHER_BLOCKS = 1


def lane_order(head_f, line_ref, capacity):
    tiles = head_f.shape[0]
    pitch = capacity + HEAD_ROWS
    lane = lax.broadcasted_iota(jnp.int32, (1, LANES), 1)
    for t in range(tiles * pitch // LANES):
        line = jnp.zeros((1, LANES), jnp.float32)
        for source in range(tiles):
            start = source * pitch - t * LANES
            if start < LANES and start + capacity > 0:
                inside = (lane >= start) & (lane < start + capacity)
                line = jnp.where(inside, head_f[source : source + 1, :], line)
        line_ref[:, t * LANES : (t + 1) * LANES] = line


def finish_kernel(
    seam_ref, got_ref, heads_ref, north_ref, south_ref, east_ref, west_ref, weight_ref, local_hbm,
    out_hbm, acc, out_ref, hor_ref, coef_ref,
    head_f, row_line, column_line, sems, out_sems,
):
    slots, width = got_ref.shape
    tiles, pairs = heads_ref.shape[0], heads_ref.shape[1]
    capacity = slots // tiles - HEAD_ROWS
    levels, fields, rows, columns = out_ref.shape
    depth = slots // GATHER_BLOCKS
    copies = local_copies(local_hbm, (hor_ref, coef_ref), sems, True)
    for copy in copies:
        copy.start()
    along_rank = lax.axis_index("along")
    own_code = seam_ref[along_rank]
    next_code = seam_ref[lax.rem(along_rank + 1, seam_ref.shape[0])]
    start_with_edges(
        acc, own_code, next_code, north_ref, south_ref, east_ref, west_ref, weight_ref
    )

    heads = heads_ref[:, pairs - 1].astype(jnp.float32)
    for i, line_ref in enumerate((row_line, column_line)):
        head_f[i] = heads[:, i, :]
        lane_order(head_f.at[i], line_ref, capacity)
    column_id = lax.broadcasted_iota(jnp.int32, (columns, depth), 0).astype(jnp.float32)
    zero = jnp.zeros((width, depth), jnp.bfloat16)

    def gather(i, carried):
        span = pl.ds(pl.multiple_of(i * depth, depth), depth)
        turned = jnp.transpose(got_ref[span, :])
        onehot = (column_id == column_line[:, span]).astype(jnp.float32).astype(jnp.bfloat16)
        row_wide = jnp.broadcast_to(row_line[:, span], (width, depth)).astype(jnp.bfloat16)
        masked = jnp.concatenate(
            [jnp.where(row_wide == (c + 1), turned, zero) for c in range(rows)], axis=0
        )
        part = lax.dot_general(
            masked, onehot, (((1,), (1,)), ((), ())), preferred_element_type=jnp.float32
        )
        acc[...] += part.reshape(rows, width, columns)
        return carried

    lax.fori_loop(0, GATHER_BLOCKS, gather, 0)

    copies[0].wait()
    copies[1].wait()

    def forward(q, previous):
        forcing = jnp.swapaxes(acc[:, pl.ds(pl.multiple_of(q * 8, 8), 8), :], 0, 1)
        state = list(previous)
        for i in range(8 // fields):
            k = q * (8 // fields) + i
            mask_inv, lower_inv = coef_ref[k], coef_ref[levels + k]
            for f in range(fields):
                state[f] = (
                    hor_ref[k * fields + f] + mask_inv * forcing[i * fields + f] + lower_inv * state[f]
                )
                out_ref[k, f] = state[f]
        return tuple(state)

    zero = jnp.zeros((rows, columns), jnp.float32)
    last = lax.fori_loop(0, levels * fields // 8, forward, (zero,) * fields)

    def backward(step, below):
        k = levels - 2 - step
        ratio = coef_ref[2 * levels + k]
        here = []
        for f in range(fields):
            here.append(out_ref[k, f] - ratio * below[f])
            out_ref[k, f] = here[f]
        return tuple(here)

    below = last
    out_copies = []
    part = levels // PARTS
    done = 0
    for i in range(PARTS):
        steps = part - 1 if i == 0 else part
        below = lax.fori_loop(done, done + steps, backward, below)
        done += steps
        span = pl.ds(levels - (i + 1) * part, part)
        copy = pltpu.make_async_copy(out_ref.at[span], out_hbm.at[span], out_sems.at[i])
        copy.start()
        out_copies.append(copy)
    for copy in out_copies:
        copy.wait()


def finish(seam_code, got, halos, weight, local, tiles, shape):
    slots, width = got.shape
    heads = got.reshape(tiles, slots // tiles // HEAD_ROWS, HEAD_ROWS, width)
    levels, fields, rows, columns = shape
    vmem = pl.BlockSpec(memory_space=pltpu.VMEM)
    hbm = pl.BlockSpec(memory_space=pltpu.HBM)
    return pl.pallas_call(
        finish_kernel,
        out_shape=jax.ShapeDtypeStruct(shape, jnp.float32),
        in_specs=[pl.BlockSpec(memory_space=pltpu.SMEM)] + [vmem] * 7 + [hbm],
        out_specs=hbm,
        scratch_shapes=[
            pltpu.VMEM((rows, levels * fields, columns), jnp.float32),
            pltpu.VMEM(shape, jnp.float32),
        ]
        + local_scratch(*shape)
        + [
            pltpu.VMEM((2, tiles, LANES), jnp.float32),
            pltpu.VMEM((1, slots), jnp.float32),
            pltpu.VMEM((1, slots), jnp.float32),
            pltpu.SemaphoreType.DMA((2,)),
            pltpu.SemaphoreType.DMA((PARTS,)),
        ],
        compiler_params=pltpu.CompilerParams(vmem_limit_bytes=LAST_VMEM_BYTES),
        name="finish",
    )(seam_code, got, heads, *halos, weight, local)


def per_device(adjoint, flow, land_mask, mixing, seam_code, obs_misfit, obs_owner, obs_cell):
    levels, fields, rows, columns = adjoint.shape
    along_count = lax.axis_size("along")
    cross_count = lax.axis_size("cross")
    devices = along_count * cross_count
    capacity = 2 * obs_misfit.shape[0] // devices
    packed = pack_rows(obs_owner, obs_cell, obs_misfit, devices, capacity)
    packed, adjoint = lax.optimization_barrier((packed, adjoint))
    slots, width = packed.shape
    pairs = packed.reshape(slots // HEAD_ROWS, HEAD_ROWS, width)
    got = lax.all_to_all(pairs, ("along", "cross"), split_axis=0, concat_axis=0, tiled=True)
    got = got.reshape(slots, width)

    ring_up = [(i, (i + 1) % along_count) for i in range(along_count)]
    ring_down = [(target, source) for source, target in ring_up]
    line_up = [(i, i + 1) for i in range(cross_count - 1)]
    line_down = [(target, source) for source, target in line_up]
    first_row, last_row, first_column, last_column = edges(adjoint)
    west = lax.ppermute(last_column, "along", ring_up)
    east = lax.ppermute(first_column, "along", ring_down)
    south = lax.ppermute(last_row, "cross", line_up)
    north = lax.ppermute(first_row, "cross", line_down)
    local, weight = local_part(adjoint, flow, land_mask, mixing)
    halos = (north, south, east, west)
    return finish(seam_code, got, halos, weight, local, devices, adjoint.shape)


def solution(mesh):
    return jax.shard_map(
        per_device,
        mesh=mesh,
        in_specs=(
            P(None, None, "cross", "along"),
            P(None, None, "cross", "along"),
            P(None, "cross", "along"),
            P(None, "cross", "along"),
            P(),
            P(("along", "cross"), None),
            P(("along", "cross"), None),
            P(("along", "cross")),
        ),
        out_specs=P(None, None, "cross", "along"),
        check_vma=False,
    )
```

```python
import functools

import jax
import jax.numpy as jnp
from jax import lax
from jax.experimental import pallas as pl
from jax.experimental.pallas import tpu as pltpu
from jax.sharding import PartitionSpec as P

diffusion_rate = 0.15
coriolis = 0.3
couple_rate = 0.3
thermal_coef = 0.8
haline_coef = 0.6

LANES = 128
HEAD_ROWS = 2
PARTS = 4
LAST_VMEM_BYTES = 44 * 1024 * 1024
LOCAL_VMEM_BYTES = 50 * 1024 * 1024
LOCAL_PLANES = 1536
WIDE_VMEM_BYTES = 61 * 1024 * 1024


def pack_kernel(
    owner_hbm, cell_hbm, rows_hbm, out_hbm,
    owner_ref, cell_ref, rows_ref, out_ref, stage, rows_f, slot_v, slot_s, sems, out_sems,
    *, tiles,
):
    block_rows = out_ref.shape[0] // tiles
    capacity = block_rows - HEAD_ROWS
    blocks = owner_ref.shape[0]
    half = blocks // 2
    owner_copy = pltpu.make_async_copy(owner_hbm, owner_ref, sems.at[0])
    cell_copy = pltpu.make_async_copy(cell_hbm, cell_ref, sems.at[1])
    rows_copy = pltpu.make_async_copy(rows_hbm, rows_ref, sems.at[2])
    owner_copy.start()
    cell_copy.start()
    rows_copy.start()
    tile_id = lax.broadcasted_iota(jnp.int32, (tiles, LANES), 0)
    low = lax.broadcasted_iota(jnp.int32, (LANES, 2 * LANES), 0)
    high = lax.broadcasted_iota(jnp.int32, (LANES, 2 * LANES), 1)
    count_with = ((low <= high) | (high >= LANES)).astype(jnp.float32).astype(jnp.bfloat16)
    device = lax.axis_index("along") * lax.axis_size("cross") + lax.axis_index("cross")
    place = lax.broadcasted_iota(jnp.int32, (LANES, LANES), 0) - device * block_rows
    place = (place & (LANES - 1)).astype(jnp.float32)
    carry = jnp.zeros((tiles, LANES), jnp.float32)
    total = jnp.zeros((tiles, 2 * LANES), jnp.float32)
    owner_copy.wait()
    cell_copy.wait()
    slot_copies = []
    for b in range(blocks):
        owner = owner_ref[b : b + 1, :]
        cell = cell_ref[b : b + 1, :]
        hit = (tile_id == owner).astype(jnp.float32)
        hit_narrow = hit.astype(jnp.bfloat16)
        counts = jnp.dot(hit_narrow, count_with, preferred_element_type=jnp.float32)
        rank = jnp.sum((counts[:, :LANES] + carry) * hit, axis=0, keepdims=True) - 1.0
        carry = carry + counts[:, LANES:]
        slot_v[b : b + 1, :] = owner * block_rows + rank.astype(jnp.int32)
        row_part = ((cell >> 8) + 1).astype(jnp.float32)
        column_part = (cell & 255).astype(jnp.float32)
        here = place == rank
        values = jnp.concatenate(
            [jnp.where(here, row_part, 0.0), jnp.where(here, column_part, 0.0)], axis=0
        ).astype(jnp.bfloat16)
        total = total + lax.dot_general(
            hit_narrow, values, (((1,), (1,)), ((), ())), preferred_element_type=jnp.float32
        )
        if (b + 1) % half == 0:
            span = pl.ds(b + 1 - half, half)
            copy = pltpu.make_async_copy(
                slot_v.at[span], slot_s.at[span], sems.at[3 + len(slot_copies)]
            )
            copy.start()
            slot_copies.append(copy)
    stage[pl.ds(capacity, tiles, stride=block_rows), :] = total[:, :LANES]
    stage[pl.ds(capacity + 1, tiles, stride=block_rows), :] = total[:, LANES:]
    rows_copy.wait()
    rows_f[...] = rows_ref[...].astype(jnp.float32)

    def scatter(b, carried):
        base = pl.multiple_of(b * LANES, LANES)
        for j in range(LANES):
            stage[pl.ds(slot_s[b, j], 1), :] = rows_f[pl.ds(base + j, 1), :]
        return carried

    for i, copy in enumerate(slot_copies):
        copy.wait()
        lax.fori_loop(i * half, (i + 1) * half, scatter, 0)

    step = out_ref.shape[0] // PARTS
    piece = capacity

    def narrow(i, carried):
        span = pl.ds(pl.multiple_of(i * piece, piece), piece)
        out_ref[span, :] = stage[span, :].astype(jnp.bfloat16)
        return carried

    out_copies = []
    for i in range(PARTS):
        lax.fori_loop(i * step // piece, (i + 1) * step // piece, narrow, 0, unroll=3)
        span = pl.ds(i * step, step)
        copy = pltpu.make_async_copy(out_ref.at[span], out_hbm.at[span], out_sems.at[i])
        copy.start()
        out_copies.append(copy)
    for copy in out_copies:
        copy.wait()


def pack_rows(obs_owner, obs_cell, obs_misfit, tiles, capacity):
    obs_rows, width = obs_misfit.shape
    blocks = obs_rows // LANES
    slots = tiles * (capacity + HEAD_ROWS)
    hbm = pl.BlockSpec(memory_space=pltpu.HBM)
    return pl.pallas_call(
        functools.partial(pack_kernel, tiles=tiles),
        out_shape=jax.ShapeDtypeStruct((slots, width), jnp.bfloat16),
        in_specs=[hbm] * 3,
        out_specs=hbm,
        scratch_shapes=[
            pltpu.VMEM((blocks, LANES), jnp.int32),
            pltpu.VMEM((blocks, LANES), jnp.int32),
            pltpu.VMEM((obs_rows, width), jnp.bfloat16),
            pltpu.VMEM((slots, width), jnp.bfloat16),
            pltpu.VMEM((slots, width), jnp.float32),
            pltpu.VMEM((obs_rows, width), jnp.float32),
            pltpu.VMEM((blocks, LANES), jnp.int32),
            pltpu.SMEM((blocks, LANES), jnp.int32),
            pltpu.SemaphoreType.DMA((5,)),
            pltpu.SemaphoreType.DMA((PARTS,)),
        ],
        compiler_params=pltpu.CompilerParams(vmem_limit_bytes=WIDE_VMEM_BYTES),
        name="pack_rows",
    )(obs_owner.reshape(blocks, LANES), obs_cell.reshape(blocks, LANES), obs_misfit)


def edge_kernel(adj_ref, north_ref, south_ref, east_ref, west_ref):
    planes, rows, columns = adj_ref.shape
    north_ref[...] = adj_ref[:, 0, :].astype(jnp.bfloat16)
    south_ref[...] = adj_ref[:, rows - 1, :].astype(jnp.bfloat16)
    row = lax.broadcasted_iota(jnp.int32, (rows, LANES), 0)
    lane = lax.broadcasted_iota(jnp.int32, (rows, LANES), 1)
    for ref, start, at in ((east_ref, 0, 0), (west_ref, columns - LANES, LANES - 1)):
        line = jnp.zeros((rows, planes), jnp.float32)
        for r in range(rows):
            pick = ((lane == at) & (row == r)).astype(jnp.float32).astype(jnp.bfloat16)
            side = adj_ref[:, r, start : start + LANES].astype(jnp.bfloat16)
            line = line + lax.dot_general(
                pick, side, (((1,), (1,)), ((), ())), preferred_element_type=jnp.float32
            )
        ref[...] = line.astype(jnp.bfloat16)


def edges(adjoint):
    levels, fields, rows, columns = adjoint.shape
    planes = levels * fields
    vmem = pl.BlockSpec(memory_space=pltpu.VMEM)
    side = jax.ShapeDtypeStruct((rows, planes), jnp.bfloat16)
    row = jax.ShapeDtypeStruct((planes, columns), jnp.bfloat16)
    return pl.pallas_call(
        edge_kernel,
        out_shape=(row, row, side, side),
        in_specs=[vmem],
        out_specs=(vmem,) * 4,
        compiler_params=pltpu.CompilerParams(vmem_limit_bytes=WIDE_VMEM_BYTES),
        cost_estimate=pl.CostEstimate(flops=1000, bytes_accessed=100000, transcendentals=0),
        name="edges",
    )(adjoint.reshape(planes, rows, columns))


def local_kernel(
    adj_ref, flow_ref, mask_ref, mix_ref, local_hbm, weight_ref, hor_ref, coef_ref, sems,
):
    levels, fields, rows, columns = adj_ref.shape
    planes = levels * fields
    shape = (rows, columns)
    lane = lax.broadcasted_iota(jnp.int32, shape, 1)
    sub = lax.broadcasted_iota(jnp.int32, shape, 0)
    last_column, first_column = lane == columns - 1, lane == 0
    last_row, first_row = sub == rows - 1, sub == 0

    row = lax.broadcasted_iota(jnp.int32, (rows, LANES), 0)
    short_lane = lax.broadcasted_iota(jnp.int32, (rows, LANES), 1)
    repeat = (
        lax.broadcasted_iota(jnp.int32, (levels, planes), 1) // fields
        == lax.broadcasted_iota(jnp.int32, (levels, planes), 0)
    ).astype(jnp.float32)
    row_planes = planes // rows
    for place, start, at, half in ((0, columns - LANES, LANES - 1, 0.5), (planes, 0, 0, -0.5)):
        line = jnp.zeros((rows, levels), jnp.float32)
        for r in range(rows):
            pick = ((short_lane == at) & (row == r)).astype(jnp.float32)
            line = line + lax.dot_general(
                pick,
                flow_ref[:, 0, r, start : start + LANES],
                (((1,), (1,)), ((), ())),
                precision=lax.Precision.HIGHEST,
                preferred_element_type=jnp.float32,
            )
        line = jnp.dot(
            line, repeat, precision=lax.Precision.HIGHEST, preferred_element_type=jnp.float32
        )
        weight_ref[2 * row_planes, :, place : place + planes] = diffusion_rate + half * line

    def level(k, state):
        lower, ratio_prev = state
        mask = mask_ref[k].astype(jnp.float32)
        below = jnp.minimum(k + 1, levels - 1)
        mask_below = mask_ref[below].astype(jnp.float32)
        mix = mix_ref[jnp.minimum(k, levels - 2)]
        upper = jnp.where(k < levels - 1, mix * mask * mask_below, 0.0)
        inverse = 1.0 / (1.0 + lower + upper + lower * ratio_prev)
        ratio = -upper * inverse
        mask_inv = mask * inverse
        coef_ref[k] = mask_inv
        coef_ref[levels + k] = lower * inverse
        coef_ref[2 * levels + k] = ratio
        flow_along, flow_cross = flow_ref[k, 0], flow_ref[k, 1]
        north_weight = diffusion_rate + 0.5 * flow_cross[rows - 1 : rows, :]
        south_weight = diffusion_rate - 0.5 * flow_cross[0:1, :]
        centers, advects, alongs, crosses = [], [], [], []
        for f in range(fields):
            at = k * fields + f
            weight_ref[at // rows, pl.ds(at % rows, 1), :] = north_weight
            weight_ref[row_planes + at // rows, pl.ds(at % rows, 1), :] = south_weight
            x = adj_ref[k, f]
            east = jnp.where(last_column, 0.0, pltpu.roll(x, columns - 1, 1))
            west = jnp.where(first_column, 0.0, pltpu.roll(x, 1, 1))
            north = jnp.where(last_row, 0.0, pltpu.roll(x, rows - 1, 0))
            south = jnp.where(first_row, 0.0, pltpu.roll(x, 1, 0))
            along = 0.5 * (east - west)
            cross = 0.5 * (north - south)
            advect = (
                x
                + diffusion_rate * (east + west + north + south - 4.0 * x)
                + flow_along * along
                + flow_cross * cross
            )
            centers.append(x)
            advects.append(advect)
            alongs.append(along)
            crosses.append(cross)
        diverge = alongs[2] + crosses[3]
        buoy_along = thermal_coef * alongs[0] - haline_coef * alongs[1]
        buoy_cross = thermal_coef * crosses[0] - haline_coef * crosses[1]
        hor_ref[k * fields + 0] = mask_inv * (advects[0] - thermal_coef * couple_rate * diverge)
        hor_ref[k * fields + 1] = mask_inv * (advects[1] + haline_coef * couple_rate * diverge)
        hor_ref[k * fields + 2] = mask_inv * (advects[2] + coriolis * centers[3] + couple_rate * buoy_along)
        hor_ref[k * fields + 3] = mask_inv * (advects[3] - coriolis * centers[2] + couple_rate * buoy_cross)
        return upper, ratio

    zero = jnp.zeros(shape, jnp.float32)
    lax.fori_loop(0, levels, level, (zero, zero))
    copies = local_copies(local_hbm, (hor_ref, coef_ref), sems, False)
    for copy in copies:
        copy.start()
    for copy in copies:
        copy.wait()


def local_copies(local_hbm, refs, sems, inward):
    copies, at = [], 0
    for i, ref in enumerate(refs):
        part = local_hbm.at[pl.ds(at, ref.shape[0])]
        source, target = (part, ref) if inward else (ref, part)
        copies.append(pltpu.make_async_copy(source, target, sems.at[i]))
        at += ref.shape[0]
    return copies


def local_scratch(levels, fields, rows, columns):
    planes = levels * fields
    return [
        pltpu.VMEM((planes, rows, columns), jnp.float32),
        pltpu.VMEM((3 * levels, rows, columns), jnp.float32),
    ]


def local_part(adjoint, flow, land_mask, mixing):
    levels, fields, rows, columns = adjoint.shape
    vmem = pl.BlockSpec(memory_space=pltpu.VMEM)
    return pl.pallas_call(
        local_kernel,
        out_shape=(
            jax.ShapeDtypeStruct((LOCAL_PLANES, rows, columns), jnp.float32),
            jax.ShapeDtypeStruct((2 * levels * fields // rows + 1, rows, columns), jnp.float32),
        ),
        in_specs=[vmem] * 4,
        out_specs=(pl.BlockSpec(memory_space=pltpu.HBM), vmem),
        scratch_shapes=local_scratch(*adjoint.shape) + [pltpu.SemaphoreType.DMA((2,))],
        compiler_params=pltpu.CompilerParams(vmem_limit_bytes=LOCAL_VMEM_BYTES),
        cost_estimate=pl.CostEstimate(flops=1000, bytes_accessed=100000, transcendentals=0),
        name="local_part",
    )(adjoint, flow, land_mask, mixing)


def turned_edge(edge, code):
    planes = edge.shape[1]
    cosine = jnp.where(code == 0, 1.0, 0.0) - jnp.where(code == 2, 1.0, 0.0)
    sine = jnp.where(code == 1, 1.0, 0.0) - jnp.where(code == 3, 1.0, 0.0)
    field = lax.broadcasted_iota(jnp.int32, edge.shape, 1) & 3
    zonal = cosine * edge - sine * pltpu.roll(edge, planes - 1, 1)
    meridional = sine * pltpu.roll(edge, 1, 1) + cosine * edge
    return jnp.where(field == 2, zonal, jnp.where(field == 3, meridional, edge))


def edge_term(edge, weight, sign, axis, vector):
    planes = edge.shape[axis]
    field = lax.broadcasted_iota(jnp.int32, edge.shape, axis) & 3
    ahead = lambda n: pltpu.roll(edge, planes - n, axis)
    behind = lambda n: pltpu.roll(edge, n, axis)
    thermal = sign * 0.5 * thermal_coef * couple_rate
    haline = sign * 0.5 * haline_coef * couple_rate
    other = thermal * behind(vector) - haline * behind(vector - 1)
    mixed = jnp.where(field == 0, -thermal * ahead(vector), 0.0)
    mixed = jnp.where(field == 1, haline * ahead(vector - 1), mixed)
    mixed = jnp.where(field == vector, other, mixed)
    return weight * edge + mixed


def start_with_edges(
    acc, own_code, next_code, north_ref, south_ref, east_ref, west_ref, weight_ref
):
    rows, planes, columns = acc.shape
    row_planes = planes // rows
    weight_north = weight_ref[0:row_planes].reshape(planes, columns)
    weight_south = weight_ref[row_planes : 2 * row_planes].reshape(planes, columns)
    weight_east = weight_ref[2 * row_planes, :, 0:planes]
    weight_west = weight_ref[2 * row_planes, :, planes : 2 * planes]
    east = turned_edge(east_ref[...].astype(jnp.float32), (4 - next_code) & 3)
    west = turned_edge(west_ref[...].astype(jnp.float32), own_code)
    fill = jnp.zeros((LANES - rows, planes), jnp.float32)
    tall = lambda line: jnp.transpose(jnp.concatenate([line, fill], axis=0))
    east = tall(edge_term(east, weight_east, 1.0, 1, 2))
    west = tall(edge_term(west, weight_west, -1.0, 1, 2))
    north = edge_term(north_ref[...].astype(jnp.float32), weight_north, 1.0, 0, 3)
    south = edge_term(south_ref[...].astype(jnp.float32), weight_south, -1.0, 0, 3)
    lane = lax.broadcasted_iota(jnp.int32, (planes, LANES), 1)
    blank = jnp.zeros((planes, columns - 2 * LANES), jnp.float32)
    for c in range(rows):
        first = jnp.where(lane == 0, jnp.broadcast_to(west[:, c : c + 1], lane.shape), 0.0)
        last = jnp.where(lane == LANES - 1, jnp.broadcast_to(east[:, c : c + 1], lane.shape), 0.0)
        line = jnp.concatenate([first, blank, last], axis=1) if blank.shape[1] else (
            jnp.concatenate([first, last], axis=1)
        )
        if c == 0:
            line = line + south
        if c == rows - 1:
            line = line + north
        acc[c] = line


GATHER_BLOCKS = 1
ROW_PARTS = 2


def lane_order(head_f, line_ref, capacity):
    tiles = head_f.shape[0]
    pitch = capacity + HEAD_ROWS
    lane = lax.broadcasted_iota(jnp.int32, (1, LANES), 1)
    for t in range(tiles * pitch // LANES):
        line = jnp.zeros((1, LANES), jnp.float32)
        for source in range(tiles):
            start = source * pitch - t * LANES
            if start < LANES and start + capacity > 0:
                inside = (lane >= start) & (lane < start + capacity)
                line = jnp.where(inside, head_f[source : source + 1, :], line)
        line_ref[:, t * LANES : (t + 1) * LANES] = line


def finish_kernel(
    seam_ref, got_ref, heads_ref, north_ref, south_ref, east_ref, west_ref, weight_ref, local_hbm,
    out_hbm, acc, out_ref, hor_ref, coef_ref,
    head_f, row_line, column_line, sems, out_sems,
):
    slots, width = got_ref.shape
    tiles, pairs = heads_ref.shape[0], heads_ref.shape[1]
    capacity = slots // tiles - HEAD_ROWS
    levels, fields, rows, columns = out_ref.shape
    depth = slots // GATHER_BLOCKS
    copies = local_copies(local_hbm, (hor_ref, coef_ref), sems, True)
    for copy in copies:
        copy.start()
    along_rank = lax.axis_index("along")
    own_code = seam_ref[along_rank]
    next_code = seam_ref[lax.rem(along_rank + 1, seam_ref.shape[0])]
    start_with_edges(
        acc, own_code, next_code, north_ref, south_ref, east_ref, west_ref, weight_ref
    )

    heads = heads_ref[:, pairs - 1].astype(jnp.float32)
    for i, line_ref in enumerate((row_line, column_line)):
        head_f[i] = heads[:, i, :]
        lane_order(head_f.at[i], line_ref, capacity)
    column_id = lax.broadcasted_iota(jnp.int32, (columns, depth), 0).astype(jnp.float32)
    column_id = column_id.astype(jnp.bfloat16)
    zero = jnp.zeros((width, depth), jnp.bfloat16)

    def gather(i, carried):
        span = pl.ds(pl.multiple_of(i * depth, depth), depth)
        turned = jnp.transpose(got_ref[span, :])
        column_wide = jnp.broadcast_to(column_line[:, span], (columns, depth)).astype(jnp.bfloat16)
        onehot = jnp.where(
            column_id == column_wide, jnp.ones((), jnp.bfloat16), jnp.zeros((), jnp.bfloat16)
        )
        row_wide = jnp.broadcast_to(row_line[:, span], (width, depth)).astype(jnp.bfloat16)
        for start in range(0, rows, rows // ROW_PARTS):
            some = range(start, start + rows // ROW_PARTS)
            masked = jnp.concatenate(
                [jnp.where(row_wide == (c + 1), turned, zero) for c in some], axis=0
            )
            part = lax.dot_general(
                masked, onehot, (((1,), (1,)), ((), ())), preferred_element_type=jnp.float32
            )
            acc[start : start + rows // ROW_PARTS] += part.reshape(rows // ROW_PARTS, width, columns)
        return carried

    lax.fori_loop(0, GATHER_BLOCKS, gather, 0)

    copies[0].wait()
    copies[1].wait()

    def forward(q, previous):
        forcing = jnp.swapaxes(acc[:, pl.ds(pl.multiple_of(q * 8, 8), 8), :], 0, 1)
        state = list(previous)
        for i in range(8 // fields):
            k = q * (8 // fields) + i
            mask_inv, lower_inv = coef_ref[k], coef_ref[levels + k]
            for f in range(fields):
                state[f] = (
                    hor_ref[k * fields + f] + mask_inv * forcing[i * fields + f] + lower_inv * state[f]
                )
                out_ref[k, f] = state[f]
        return tuple(state)

    zero = jnp.zeros((rows, columns), jnp.float32)
    last = lax.fori_loop(0, levels * fields // 8, forward, (zero,) * fields)

    def backward(step, below):
        k = levels - 2 - step
        ratio = coef_ref[2 * levels + k]
        here = []
        for f in range(fields):
            here.append(out_ref[k, f] - ratio * below[f])
            out_ref[k, f] = here[f]
        return tuple(here)

    below = last
    out_copies = []
    part = levels // PARTS
    done = 0
    for i in range(PARTS):
        steps = part - 1 if i == 0 else part
        below = lax.fori_loop(done, done + steps, backward, below)
        done += steps
        span = pl.ds(levels - (i + 1) * part, part)
        copy = pltpu.make_async_copy(out_ref.at[span], out_hbm.at[span], out_sems.at[i])
        copy.start()
        out_copies.append(copy)
    for copy in out_copies:
        copy.wait()


def finish(seam_code, got, halos, weight, local, tiles, shape):
    slots, width = got.shape
    heads = got.reshape(tiles, slots // tiles // HEAD_ROWS, HEAD_ROWS, width)
    levels, fields, rows, columns = shape
    vmem = pl.BlockSpec(memory_space=pltpu.VMEM)
    hbm = pl.BlockSpec(memory_space=pltpu.HBM)
    return pl.pallas_call(
        finish_kernel,
        out_shape=jax.ShapeDtypeStruct(shape, jnp.float32),
        in_specs=[pl.BlockSpec(memory_space=pltpu.SMEM)] + [vmem] * 7 + [hbm],
        out_specs=hbm,
        scratch_shapes=[
            pltpu.VMEM((rows, levels * fields, columns), jnp.float32),
            pltpu.VMEM(shape, jnp.float32),
        ]
        + local_scratch(*shape)
        + [
            pltpu.VMEM((2, tiles, LANES), jnp.float32),
            pltpu.VMEM((1, slots), jnp.float32),
            pltpu.VMEM((1, slots), jnp.float32),
            pltpu.SemaphoreType.DMA((2,)),
            pltpu.SemaphoreType.DMA((PARTS,)),
        ],
        compiler_params=pltpu.CompilerParams(vmem_limit_bytes=LAST_VMEM_BYTES),
        name="finish",
    )(seam_code, got, heads, *halos, weight, local)


def per_device(adjoint, flow, land_mask, mixing, seam_code, obs_misfit, obs_owner, obs_cell):
    levels, fields, rows, columns = adjoint.shape
    along_count = lax.axis_size("along")
    cross_count = lax.axis_size("cross")
    devices = along_count * cross_count
    capacity = 2 * obs_misfit.shape[0] // devices
    packed = pack_rows(obs_owner, obs_cell, obs_misfit, devices, capacity)
    packed, adjoint = lax.optimization_barrier((packed, adjoint))
    slots, width = packed.shape
    pairs = packed.reshape(slots // HEAD_ROWS, HEAD_ROWS, width)
    got = lax.all_to_all(pairs, ("along", "cross"), split_axis=0, concat_axis=0, tiled=True)
    got = got.reshape(slots, width)

    ring_up = [(i, (i + 1) % along_count) for i in range(along_count)]
    ring_down = [(target, source) for source, target in ring_up]
    line_up = [(i, i + 1) for i in range(cross_count - 1)]
    line_down = [(target, source) for source, target in line_up]
    first_row, last_row, first_column, last_column = edges(adjoint)
    west = lax.ppermute(last_column, "along", ring_up)
    east = lax.ppermute(first_column, "along", ring_down)
    south = lax.ppermute(last_row, "cross", line_up)
    north = lax.ppermute(first_row, "cross", line_down)
    local, weight = local_part(adjoint, flow, land_mask, mixing)
    halos = (north, south, east, west)
    return finish(seam_code, got, halos, weight, local, devices, adjoint.shape)


def solution(mesh):
    return jax.shard_map(
        per_device,
        mesh=mesh,
        in_specs=(
            P(None, None, "cross", "along"),
            P(None, None, "cross", "along"),
            P(None, "cross", "along"),
            P(None, "cross", "along"),
            P(),
            P(("along", "cross"), None),
            P(("along", "cross"), None),
            P(("along", "cross")),
        ),
        out_specs=P(None, None, "cross", "along"),
        check_vma=False,
    )
```

```python
import functools

import jax
import jax.numpy as jnp
from jax import lax
from jax.experimental import pallas as pl
from jax.experimental.pallas import tpu as pltpu
from jax.sharding import PartitionSpec as P

diffusion_rate = 0.15
coriolis = 0.3
couple_rate = 0.3
thermal_coef = 0.8
haline_coef = 0.6

LANES = 128
HEAD_ROWS = 2
PARTS = 4
LAST_VMEM_BYTES = 44 * 1024 * 1024
LOCAL_VMEM_BYTES = 50 * 1024 * 1024
LOCAL_PLANES = 1536
WIDE_VMEM_BYTES = 61 * 1024 * 1024


def pack_kernel(
    owner_hbm, cell_hbm, rows_hbm, out_hbm,
    owner_ref, cell_ref, rows_ref, out_ref, stage, rows_f, slot_v, slot_s, sems, out_sems,
    *, tiles,
):
    block_rows = out_ref.shape[0] // tiles
    capacity = block_rows - HEAD_ROWS
    blocks = owner_ref.shape[0]
    half = blocks // 2
    owner_copy = pltpu.make_async_copy(owner_hbm, owner_ref, sems.at[0])
    cell_copy = pltpu.make_async_copy(cell_hbm, cell_ref, sems.at[1])
    rows_copy = pltpu.make_async_copy(rows_hbm, rows_ref, sems.at[2])
    owner_copy.start()
    cell_copy.start()
    rows_copy.start()
    tile_id = lax.broadcasted_iota(jnp.int32, (tiles, LANES), 0)
    low = lax.broadcasted_iota(jnp.int32, (LANES, 2 * LANES), 0)
    high = lax.broadcasted_iota(jnp.int32, (LANES, 2 * LANES), 1)
    count_with = ((low <= high) | (high >= LANES)).astype(jnp.float32).astype(jnp.bfloat16)
    device = lax.axis_index("along") * lax.axis_size("cross") + lax.axis_index("cross")
    place = lax.broadcasted_iota(jnp.int32, (LANES, LANES), 0) - device * block_rows
    place = (place & (LANES - 1)).astype(jnp.float32)
    carry = jnp.zeros((tiles, LANES), jnp.float32)
    total = jnp.zeros((tiles, 2 * LANES), jnp.float32)
    owner_copy.wait()
    cell_copy.wait()
    slot_copies = []
    for b in range(blocks):
        owner = owner_ref[b : b + 1, :]
        cell = cell_ref[b : b + 1, :]
        hit = (tile_id == owner).astype(jnp.float32)
        hit_narrow = hit.astype(jnp.bfloat16)
        counts = jnp.dot(hit_narrow, count_with, preferred_element_type=jnp.float32)
        rank = jnp.sum((counts[:, :LANES] + carry) * hit, axis=0, keepdims=True) - 1.0
        carry = carry + counts[:, LANES:]
        slot_v[b : b + 1, :] = owner * block_rows + rank.astype(jnp.int32)
        row_part = ((cell >> 8) + 1).astype(jnp.float32)
        column_part = (cell & 255).astype(jnp.float32)
        here = place == rank
        values = jnp.concatenate(
            [jnp.where(here, row_part, 0.0), jnp.where(here, column_part, 0.0)], axis=0
        ).astype(jnp.bfloat16)
        total = total + lax.dot_general(
            hit_narrow, values, (((1,), (1,)), ((), ())), preferred_element_type=jnp.float32
        )
        if (b + 1) % half == 0:
            span = pl.ds(b + 1 - half, half)
            copy = pltpu.make_async_copy(
                slot_v.at[span], slot_s.at[span], sems.at[3 + len(slot_copies)]
            )
            copy.start()
            slot_copies.append(copy)
    stage[pl.ds(capacity, tiles, stride=block_rows), :] = total[:, :LANES]
    stage[pl.ds(capacity + 1, tiles, stride=block_rows), :] = total[:, LANES:]
    rows_copy.wait()
    rows_f[...] = rows_ref[...].astype(jnp.float32)

    def scatter(b, carried):
        base = pl.multiple_of(b * LANES, LANES)
        for j in range(LANES):
            stage[pl.ds(slot_s[b, j], 1), :] = rows_f[pl.ds(base + j, 1), :]
        return carried

    for i, copy in enumerate(slot_copies):
        copy.wait()
        lax.fori_loop(i * half, (i + 1) * half, scatter, 0)

    step = out_ref.shape[0] // PARTS
    piece = capacity

    def narrow(i, carried):
        span = pl.ds(pl.multiple_of(i * piece, piece), piece)
        out_ref[span, :] = stage[span, :].astype(jnp.bfloat16)
        return carried

    out_copies = []
    for i in range(PARTS):
        lax.fori_loop(i * step // piece, (i + 1) * step // piece, narrow, 0, unroll=3)
        span = pl.ds(i * step, step)
        copy = pltpu.make_async_copy(out_ref.at[span], out_hbm.at[span], out_sems.at[i])
        copy.start()
        out_copies.append(copy)
    for copy in out_copies:
        copy.wait()


def pack_rows(obs_owner, obs_cell, obs_misfit, tiles, capacity):
    obs_rows, width = obs_misfit.shape
    blocks = obs_rows // LANES
    slots = tiles * (capacity + HEAD_ROWS)
    hbm = pl.BlockSpec(memory_space=pltpu.HBM)
    return pl.pallas_call(
        functools.partial(pack_kernel, tiles=tiles),
        out_shape=jax.ShapeDtypeStruct((slots, width), jnp.bfloat16),
        in_specs=[hbm] * 3,
        out_specs=hbm,
        scratch_shapes=[
            pltpu.VMEM((blocks, LANES), jnp.int32),
            pltpu.VMEM((blocks, LANES), jnp.int32),
            pltpu.VMEM((obs_rows, width), jnp.bfloat16),
            pltpu.VMEM((slots, width), jnp.bfloat16),
            pltpu.VMEM((slots, width), jnp.float32),
            pltpu.VMEM((obs_rows, width), jnp.float32),
            pltpu.VMEM((blocks, LANES), jnp.int32),
            pltpu.SMEM((blocks, LANES), jnp.int32),
            pltpu.SemaphoreType.DMA((5,)),
            pltpu.SemaphoreType.DMA((PARTS,)),
        ],
        compiler_params=pltpu.CompilerParams(vmem_limit_bytes=WIDE_VMEM_BYTES),
        name="pack_rows",
    )(obs_owner.reshape(blocks, LANES), obs_cell.reshape(blocks, LANES), obs_misfit)


def edge_kernel(adj_ref, north_ref, south_ref, east_ref, west_ref):
    planes, rows, columns = adj_ref.shape
    north_ref[...] = adj_ref[:, 0, :].astype(jnp.bfloat16)
    south_ref[...] = adj_ref[:, rows - 1, :].astype(jnp.bfloat16)
    row = lax.broadcasted_iota(jnp.int32, (rows, LANES), 0)
    lane = lax.broadcasted_iota(jnp.int32, (rows, LANES), 1)
    for ref, start, at in ((east_ref, 0, 0), (west_ref, columns - LANES, LANES - 1)):
        line = jnp.zeros((rows, planes), jnp.float32)
        for r in range(rows):
            pick = ((lane == at) & (row == r)).astype(jnp.float32).astype(jnp.bfloat16)
            side = adj_ref[:, r, start : start + LANES].astype(jnp.bfloat16)
            line = line + lax.dot_general(
                pick, side, (((1,), (1,)), ((), ())), preferred_element_type=jnp.float32
            )
        ref[...] = line.astype(jnp.bfloat16)


def edges(adjoint):
    levels, fields, rows, columns = adjoint.shape
    planes = levels * fields
    vmem = pl.BlockSpec(memory_space=pltpu.VMEM)
    side = jax.ShapeDtypeStruct((rows, planes), jnp.bfloat16)
    row = jax.ShapeDtypeStruct((planes, columns), jnp.bfloat16)
    return pl.pallas_call(
        edge_kernel,
        out_shape=(row, row, side, side),
        in_specs=[vmem],
        out_specs=(vmem,) * 4,
        compiler_params=pltpu.CompilerParams(vmem_limit_bytes=WIDE_VMEM_BYTES),
        cost_estimate=pl.CostEstimate(flops=1000, bytes_accessed=100000, transcendentals=0),
        name="edges",
    )(adjoint.reshape(planes, rows, columns))


def local_kernel(
    seam_ref, adj_ref, flow_ref, mask_ref, mix_ref, local_hbm, weight_ref, hor_ref, coef_ref, sems,
):
    levels, fields, rows, columns = adj_ref.shape
    planes = levels * fields
    shape = (rows, columns)
    lane = lax.broadcasted_iota(jnp.int32, shape, 1)
    sub = lax.broadcasted_iota(jnp.int32, shape, 0)
    last_column, first_column = lane == columns - 1, lane == 0
    last_row, first_row = sub == rows - 1, sub == 0

    row = lax.broadcasted_iota(jnp.int32, (rows, LANES), 0)
    short_lane = lax.broadcasted_iota(jnp.int32, (rows, LANES), 1)
    repeat = (
        lax.broadcasted_iota(jnp.int32, (levels, planes), 1) // fields
        == lax.broadcasted_iota(jnp.int32, (levels, planes), 0)
    ).astype(jnp.float32)
    row_planes = planes // rows
    along_rank = lax.axis_index("along")
    own_code = seam_ref[along_rank]
    next_code = seam_ref[lax.rem(along_rank + 1, seam_ref.shape[0])]
    for place, code in ((0, (4 - next_code) & 3), (planes, own_code)):
        weight_ref[2 * row_planes + 1, :, place : place + planes] = jnp.full(
            (rows, planes), code.astype(jnp.float32)
        )
    for place, start, at, half in ((0, columns - LANES, LANES - 1, 0.5), (planes, 0, 0, -0.5)):
        line = jnp.zeros((rows, levels), jnp.float32)
        for r in range(rows):
            pick = ((short_lane == at) & (row == r)).astype(jnp.float32)
            line = line + lax.dot_general(
                pick,
                flow_ref[:, 0, r, start : start + LANES],
                (((1,), (1,)), ((), ())),
                precision=lax.Precision.HIGHEST,
                preferred_element_type=jnp.float32,
            )
        line = jnp.dot(
            line, repeat, precision=lax.Precision.HIGHEST, preferred_element_type=jnp.float32
        )
        weight_ref[2 * row_planes, :, place : place + planes] = diffusion_rate + half * line

    def level(k, state):
        lower, ratio_prev = state
        mask = mask_ref[k].astype(jnp.float32)
        below = jnp.minimum(k + 1, levels - 1)
        mask_below = mask_ref[below].astype(jnp.float32)
        mix = mix_ref[jnp.minimum(k, levels - 2)]
        upper = jnp.where(k < levels - 1, mix * mask * mask_below, 0.0)
        inverse = 1.0 / (1.0 + lower + upper + lower * ratio_prev)
        ratio = -upper * inverse
        mask_inv = mask * inverse
        coef_ref[k] = mask_inv
        coef_ref[levels + k] = lower * inverse
        coef_ref[2 * levels + k] = ratio
        flow_along, flow_cross = flow_ref[k, 0], flow_ref[k, 1]
        north_weight = diffusion_rate + 0.5 * flow_cross[rows - 1 : rows, :]
        south_weight = diffusion_rate - 0.5 * flow_cross[0:1, :]
        centers, advects, alongs, crosses = [], [], [], []
        for f in range(fields):
            at = k * fields + f
            weight_ref[at // rows, pl.ds(at % rows, 1), :] = north_weight
            weight_ref[row_planes + at // rows, pl.ds(at % rows, 1), :] = south_weight
            x = adj_ref[k, f]
            east = jnp.where(last_column, 0.0, pltpu.roll(x, columns - 1, 1))
            west = jnp.where(first_column, 0.0, pltpu.roll(x, 1, 1))
            north = jnp.where(last_row, 0.0, pltpu.roll(x, rows - 1, 0))
            south = jnp.where(first_row, 0.0, pltpu.roll(x, 1, 0))
            along = 0.5 * (east - west)
            cross = 0.5 * (north - south)
            advect = (
                x
                + diffusion_rate * (east + west + north + south - 4.0 * x)
                + flow_along * along
                + flow_cross * cross
            )
            centers.append(x)
            advects.append(advect)
            alongs.append(along)
            crosses.append(cross)
        diverge = alongs[2] + crosses[3]
        buoy_along = thermal_coef * alongs[0] - haline_coef * alongs[1]
        buoy_cross = thermal_coef * crosses[0] - haline_coef * crosses[1]
        hor_ref[k * fields + 0] = mask_inv * (advects[0] - thermal_coef * couple_rate * diverge)
        hor_ref[k * fields + 1] = mask_inv * (advects[1] + haline_coef * couple_rate * diverge)
        hor_ref[k * fields + 2] = mask_inv * (advects[2] + coriolis * centers[3] + couple_rate * buoy_along)
        hor_ref[k * fields + 3] = mask_inv * (advects[3] - coriolis * centers[2] + couple_rate * buoy_cross)
        return upper, ratio

    zero = jnp.zeros(shape, jnp.float32)
    lax.fori_loop(0, levels, level, (zero, zero))
    copies = local_copies(local_hbm, (hor_ref, coef_ref), sems, False)
    for copy in copies:
        copy.start()
    for copy in copies:
        copy.wait()


def local_copies(local_hbm, refs, sems, inward):
    copies, at = [], 0
    for i, ref in enumerate(refs):
        part = local_hbm.at[pl.ds(at, ref.shape[0])]
        source, target = (part, ref) if inward else (ref, part)
        copies.append(pltpu.make_async_copy(source, target, sems.at[i]))
        at += ref.shape[0]
    return copies


def local_scratch(levels, fields, rows, columns):
    planes = levels * fields
    return [
        pltpu.VMEM((planes, rows, columns), jnp.float32),
        pltpu.VMEM((3 * levels, rows, columns), jnp.float32),
    ]


def local_part(seam_code, adjoint, flow, land_mask, mixing):
    levels, fields, rows, columns = adjoint.shape
    vmem = pl.BlockSpec(memory_space=pltpu.VMEM)
    return pl.pallas_call(
        local_kernel,
        out_shape=(
            jax.ShapeDtypeStruct((LOCAL_PLANES, rows, columns), jnp.float32),
            jax.ShapeDtypeStruct((2 * levels * fields // rows + 2, rows, columns), jnp.float32),
        ),
        in_specs=[pl.BlockSpec(memory_space=pltpu.SMEM)] + [vmem] * 4,
        out_specs=(pl.BlockSpec(memory_space=pltpu.HBM), vmem),
        scratch_shapes=local_scratch(*adjoint.shape) + [pltpu.SemaphoreType.DMA((2,))],
        compiler_params=pltpu.CompilerParams(vmem_limit_bytes=LOCAL_VMEM_BYTES),
        cost_estimate=pl.CostEstimate(flops=1000, bytes_accessed=100000, transcendentals=0),
        name="local_part",
    )(seam_code, adjoint, flow, land_mask, mixing)


def turned_edge(edge, code):
    planes = edge.shape[1]
    cosine = jnp.where(code == 0, 1.0, 0.0) - jnp.where(code == 2, 1.0, 0.0)
    sine = jnp.where(code == 1, 1.0, 0.0) - jnp.where(code == 3, 1.0, 0.0)
    field = lax.broadcasted_iota(jnp.int32, edge.shape, 1) & 3
    zonal = cosine * edge - sine * pltpu.roll(edge, planes - 1, 1)
    meridional = sine * pltpu.roll(edge, 1, 1) + cosine * edge
    return jnp.where(field == 2, zonal, jnp.where(field == 3, meridional, edge))


def edge_term(edge, weight, sign, axis, vector):
    planes = edge.shape[axis]
    field = lax.broadcasted_iota(jnp.int32, edge.shape, axis) & 3
    ahead = lambda n: pltpu.roll(edge, planes - n, axis)
    behind = lambda n: pltpu.roll(edge, n, axis)
    thermal = sign * 0.5 * thermal_coef * couple_rate
    haline = sign * 0.5 * haline_coef * couple_rate
    other = thermal * behind(vector) - haline * behind(vector - 1)
    mixed = jnp.where(field == 0, -thermal * ahead(vector), 0.0)
    mixed = jnp.where(field == 1, haline * ahead(vector - 1), mixed)
    mixed = jnp.where(field == vector, other, mixed)
    return weight * edge + mixed


def start_with_edges(
    acc, north_ref, south_ref, east_ref, west_ref, weight_ref
):
    rows, planes, columns = acc.shape
    row_planes = planes // rows
    weight_north = weight_ref[0:row_planes].reshape(planes, columns)
    weight_south = weight_ref[row_planes : 2 * row_planes].reshape(planes, columns)
    weight_east = weight_ref[2 * row_planes, :, 0:planes]
    weight_west = weight_ref[2 * row_planes, :, planes : 2 * planes]
    east = turned_edge(east_ref[...].astype(jnp.float32), weight_ref[2 * row_planes + 1, :, 0:planes])
    west = turned_edge(
        west_ref[...].astype(jnp.float32), weight_ref[2 * row_planes + 1, :, planes : 2 * planes]
    )
    fill = jnp.zeros((LANES - rows, planes), jnp.float32)
    tall = lambda line: jnp.transpose(jnp.concatenate([line, fill], axis=0))
    east = tall(edge_term(east, weight_east, 1.0, 1, 2))
    west = tall(edge_term(west, weight_west, -1.0, 1, 2))
    north = edge_term(north_ref[...].astype(jnp.float32), weight_north, 1.0, 0, 3)
    south = edge_term(south_ref[...].astype(jnp.float32), weight_south, -1.0, 0, 3)
    lane = lax.broadcasted_iota(jnp.int32, (planes, LANES), 1)
    blank = jnp.zeros((planes, columns - 2 * LANES), jnp.float32)
    for c in range(rows):
        first = jnp.where(lane == 0, jnp.broadcast_to(west[:, c : c + 1], lane.shape), 0.0)
        last = jnp.where(lane == LANES - 1, jnp.broadcast_to(east[:, c : c + 1], lane.shape), 0.0)
        line = jnp.concatenate([first, blank, last], axis=1) if blank.shape[1] else (
            jnp.concatenate([first, last], axis=1)
        )
        if c == 0:
            line = line + south
        if c == rows - 1:
            line = line + north
        acc[c] = line


GATHER_BLOCKS = 1
ROW_PARTS = 2


def lane_order(head_f, line_ref, capacity):
    tiles = head_f.shape[0]
    pitch = capacity + HEAD_ROWS
    lane = lax.broadcasted_iota(jnp.int32, (1, LANES), 1)
    for t in range(tiles * pitch // LANES):
        line = jnp.zeros((1, LANES), jnp.float32)
        for source in range(tiles):
            start = source * pitch - t * LANES
            if start < LANES and start + capacity > 0:
                inside = (lane >= start) & (lane < start + capacity)
                line = jnp.where(inside, head_f[source : source + 1, :], line)
        line_ref[:, t * LANES : (t + 1) * LANES] = line


def finish_kernel(
    got_ref, heads_ref, north_ref, south_ref, east_ref, west_ref, weight_ref, local_hbm,
    out_hbm, acc, out_ref, hor_ref, coef_ref,
    head_f, row_line, column_line, sems, out_sems,
):
    slots, width = got_ref.shape
    tiles, pairs = heads_ref.shape[0], heads_ref.shape[1]
    capacity = slots // tiles - HEAD_ROWS
    levels, fields, rows, columns = out_ref.shape
    depth = slots // GATHER_BLOCKS
    copies = local_copies(local_hbm, (hor_ref, coef_ref), sems, True)
    for copy in copies:
        copy.start()
    start_with_edges(
        acc, north_ref, south_ref, east_ref, west_ref, weight_ref
    )

    heads = heads_ref[:, pairs - 1].astype(jnp.float32)
    for i, line_ref in enumerate((row_line, column_line)):
        head_f[i] = heads[:, i, :]
        lane_order(head_f.at[i], line_ref, capacity)
    column_id = lax.broadcasted_iota(jnp.int32, (columns, depth), 0).astype(jnp.float32)
    column_id = column_id.astype(jnp.bfloat16)
    zero = jnp.zeros((width, depth), jnp.bfloat16)

    def gather(i, carried):
        span = pl.ds(pl.multiple_of(i * depth, depth), depth)
        turned = jnp.transpose(got_ref[span, :])
        column_wide = jnp.broadcast_to(column_line[:, span], (columns, depth)).astype(jnp.bfloat16)
        onehot = jnp.where(
            column_id == column_wide, jnp.ones((), jnp.bfloat16), jnp.zeros((), jnp.bfloat16)
        )
        row_wide = jnp.broadcast_to(row_line[:, span], (width, depth)).astype(jnp.bfloat16)
        for start in range(0, rows, rows // ROW_PARTS):
            some = range(start, start + rows // ROW_PARTS)
            masked = jnp.concatenate(
                [jnp.where(row_wide == (c + 1), turned, zero) for c in some], axis=0
            )
            part = lax.dot_general(
                masked, onehot, (((1,), (1,)), ((), ())), preferred_element_type=jnp.float32
            )
            acc[start : start + rows // ROW_PARTS] += part.reshape(rows // ROW_PARTS, width, columns)
        return carried

    lax.fori_loop(0, GATHER_BLOCKS, gather, 0)

    copies[0].wait()
    copies[1].wait()

    def forward(q, previous):
        forcing = jnp.swapaxes(acc[:, pl.ds(pl.multiple_of(q * 8, 8), 8), :], 0, 1)
        state = list(previous)
        for i in range(8 // fields):
            k = q * (8 // fields) + i
            mask_inv, lower_inv = coef_ref[k], coef_ref[levels + k]
            for f in range(fields):
                state[f] = (
                    hor_ref[k * fields + f] + mask_inv * forcing[i * fields + f] + lower_inv * state[f]
                )
                out_ref[k, f] = state[f]
        return tuple(state)

    zero = jnp.zeros((rows, columns), jnp.float32)
    last = lax.fori_loop(0, levels * fields // 8, forward, (zero,) * fields)

    def backward(step, below):
        k = levels - 2 - step
        ratio = coef_ref[2 * levels + k]
        here = []
        for f in range(fields):
            here.append(out_ref[k, f] - ratio * below[f])
            out_ref[k, f] = here[f]
        return tuple(here)

    below = last
    out_copies = []
    part = levels // PARTS
    done = 0
    for i in range(PARTS):
        steps = part - 1 if i == 0 else part
        below = lax.fori_loop(done, done + steps, backward, below)
        done += steps
        span = pl.ds(levels - (i + 1) * part, part)
        copy = pltpu.make_async_copy(out_ref.at[span], out_hbm.at[span], out_sems.at[i])
        copy.start()
        out_copies.append(copy)
    for copy in out_copies:
        copy.wait()


def finish(got, halos, weight, local, tiles, shape):
    slots, width = got.shape
    heads = got.reshape(tiles, slots // tiles // HEAD_ROWS, HEAD_ROWS, width)
    levels, fields, rows, columns = shape
    vmem = pl.BlockSpec(memory_space=pltpu.VMEM)
    hbm = pl.BlockSpec(memory_space=pltpu.HBM)
    return pl.pallas_call(
        finish_kernel,
        out_shape=jax.ShapeDtypeStruct(shape, jnp.float32),
        in_specs=[vmem] * 7 + [hbm],
        out_specs=hbm,
        scratch_shapes=[
            pltpu.VMEM((rows, levels * fields, columns), jnp.float32),
            pltpu.VMEM(shape, jnp.float32),
        ]
        + local_scratch(*shape)
        + [
            pltpu.VMEM((2, tiles, LANES), jnp.float32),
            pltpu.VMEM((1, slots), jnp.float32),
            pltpu.VMEM((1, slots), jnp.float32),
            pltpu.SemaphoreType.DMA((2,)),
            pltpu.SemaphoreType.DMA((PARTS,)),
        ],
        compiler_params=pltpu.CompilerParams(vmem_limit_bytes=LAST_VMEM_BYTES),
        name="finish",
    )(got, heads, *halos, weight, local)


def per_device(adjoint, flow, land_mask, mixing, seam_code, obs_misfit, obs_owner, obs_cell):
    levels, fields, rows, columns = adjoint.shape
    along_count = lax.axis_size("along")
    cross_count = lax.axis_size("cross")
    devices = along_count * cross_count
    capacity = 2 * obs_misfit.shape[0] // devices
    packed = pack_rows(obs_owner, obs_cell, obs_misfit, devices, capacity)
    packed, adjoint = lax.optimization_barrier((packed, adjoint))
    slots, width = packed.shape
    pairs = packed.reshape(slots // HEAD_ROWS, HEAD_ROWS, width)
    got = lax.all_to_all(pairs, ("along", "cross"), split_axis=0, concat_axis=0, tiled=True)
    got = got.reshape(slots, width)

    ring_up = [(i, (i + 1) % along_count) for i in range(along_count)]
    ring_down = [(target, source) for source, target in ring_up]
    line_up = [(i, i + 1) for i in range(cross_count - 1)]
    line_down = [(target, source) for source, target in line_up]
    first_row, last_row, first_column, last_column = edges(adjoint)
    west = lax.ppermute(last_column, "along", ring_up)
    east = lax.ppermute(first_column, "along", ring_down)
    south = lax.ppermute(last_row, "cross", line_up)
    north = lax.ppermute(first_row, "cross", line_down)
    local, weight = local_part(seam_code, adjoint, flow, land_mask, mixing)
    halos = (north, south, east, west)
    return finish(got, halos, weight, local, devices, adjoint.shape)


def solution(mesh):
    return jax.shard_map(
        per_device,
        mesh=mesh,
        in_specs=(
            P(None, None, "cross", "along"),
            P(None, None, "cross", "along"),
            P(None, "cross", "along"),
            P(None, "cross", "along"),
            P(),
            P(("along", "cross"), None),
            P(("along", "cross"), None),
            P(("along", "cross")),
        ),
        out_specs=P(None, None, "cross", "along"),
        check_vma=False,
    )
```

```python
import functools

import jax
import jax.numpy as jnp
from jax import lax
from jax.experimental import pallas as pl
from jax.experimental.pallas import tpu as pltpu
from jax.sharding import PartitionSpec as P

diffusion_rate = 0.15
coriolis = 0.3
couple_rate = 0.3
thermal_coef = 0.8
haline_coef = 0.6

LANES = 128
HEAD_ROWS = 2
PARTS = 4
LAST_VMEM_BYTES = 44 * 1024 * 1024
LOCAL_VMEM_BYTES = 50 * 1024 * 1024
LOCAL_PLANES = 1536
WIDE_VMEM_BYTES = 61 * 1024 * 1024


def pack_kernel(
    owner_hbm, cell_hbm, rows_hbm, out_hbm,
    owner_ref, cell_ref, rows_ref, out_ref, stage, rows_f, slot_v, slot_s, sems, out_sems,
    *, tiles,
):
    block_rows = out_ref.shape[0] // tiles
    capacity = block_rows - HEAD_ROWS
    blocks = owner_ref.shape[0]
    half = blocks // 2
    owner_copy = pltpu.make_async_copy(owner_hbm, owner_ref, sems.at[0])
    cell_copy = pltpu.make_async_copy(cell_hbm, cell_ref, sems.at[1])
    rows_copy = pltpu.make_async_copy(rows_hbm, rows_ref, sems.at[2])
    owner_copy.start()
    cell_copy.start()
    rows_copy.start()
    tile_id = lax.broadcasted_iota(jnp.int32, (tiles, LANES), 0)
    low = lax.broadcasted_iota(jnp.int32, (LANES, 2 * LANES), 0)
    high = lax.broadcasted_iota(jnp.int32, (LANES, 2 * LANES), 1)
    count_with = ((low <= high) | (high >= LANES)).astype(jnp.float32).astype(jnp.bfloat16)
    device = lax.axis_index("along") * lax.axis_size("cross") + lax.axis_index("cross")
    place = lax.broadcasted_iota(jnp.int32, (LANES, LANES), 0) - device * block_rows
    place = (place & (LANES - 1)).astype(jnp.float32)
    carry = jnp.zeros((tiles, LANES), jnp.float32)
    total = jnp.zeros((tiles, 2 * LANES), jnp.float32)
    owner_copy.wait()
    cell_copy.wait()
    slot_copies = []
    for b in range(blocks):
        owner = owner_ref[b : b + 1, :]
        cell = cell_ref[b : b + 1, :]
        hit = (tile_id == owner).astype(jnp.float32)
        hit_narrow = hit.astype(jnp.bfloat16)
        counts = jnp.dot(hit_narrow, count_with, preferred_element_type=jnp.float32)
        rank = jnp.sum((counts[:, :LANES] + carry) * hit, axis=0, keepdims=True) - 1.0
        carry = carry + counts[:, LANES:]
        slot_v[b : b + 1, :] = owner * block_rows + rank.astype(jnp.int32)
        row_part = ((cell >> 8) + 1).astype(jnp.float32)
        column_part = (cell & 255).astype(jnp.float32)
        here = place == rank
        values = jnp.concatenate(
            [jnp.where(here, row_part, 0.0), jnp.where(here, column_part, 0.0)], axis=0
        ).astype(jnp.bfloat16)
        total = total + lax.dot_general(
            hit_narrow, values, (((1,), (1,)), ((), ())), preferred_element_type=jnp.float32
        )
        if (b + 1) % half == 0:
            span = pl.ds(b + 1 - half, half)
            copy = pltpu.make_async_copy(
                slot_v.at[span], slot_s.at[span], sems.at[3 + len(slot_copies)]
            )
            copy.start()
            slot_copies.append(copy)
    stage[pl.ds(capacity, tiles, stride=block_rows), :] = total[:, :LANES]
    stage[pl.ds(capacity + 1, tiles, stride=block_rows), :] = total[:, LANES:]
    rows_copy.wait()
    rows_f[...] = rows_ref[...].astype(jnp.float32)

    def scatter(b, carried):
        base = pl.multiple_of(b * LANES, LANES)
        for j in range(LANES):
            stage[pl.ds(slot_s[b, j], 1), :] = rows_f[pl.ds(base + j, 1), :]
        return carried

    for i, copy in enumerate(slot_copies):
        copy.wait()
        lax.fori_loop(i * half, (i + 1) * half, scatter, 0)

    step = out_ref.shape[0] // PARTS
    piece = capacity

    def narrow(i, carried):
        span = pl.ds(pl.multiple_of(i * piece, piece), piece)
        out_ref[span, :] = stage[span, :].astype(jnp.bfloat16)
        return carried

    out_copies = []
    for i in range(PARTS):
        lax.fori_loop(i * step // piece, (i + 1) * step // piece, narrow, 0, unroll=3)
        span = pl.ds(i * step, step)
        copy = pltpu.make_async_copy(out_ref.at[span], out_hbm.at[span], out_sems.at[i])
        copy.start()
        out_copies.append(copy)
    for copy in out_copies:
        copy.wait()


def pack_rows(obs_owner, obs_cell, obs_misfit, tiles, capacity):
    obs_rows, width = obs_misfit.shape
    blocks = obs_rows // LANES
    slots = tiles * (capacity + HEAD_ROWS)
    hbm = pl.BlockSpec(memory_space=pltpu.HBM)
    return pl.pallas_call(
        functools.partial(pack_kernel, tiles=tiles),
        out_shape=jax.ShapeDtypeStruct((slots, width), jnp.bfloat16),
        in_specs=[hbm] * 3,
        out_specs=hbm,
        scratch_shapes=[
            pltpu.VMEM((blocks, LANES), jnp.int32),
            pltpu.VMEM((blocks, LANES), jnp.int32),
            pltpu.VMEM((obs_rows, width), jnp.bfloat16),
            pltpu.VMEM((slots, width), jnp.bfloat16),
            pltpu.VMEM((slots, width), jnp.float32),
            pltpu.VMEM((obs_rows, width), jnp.float32),
            pltpu.VMEM((blocks, LANES), jnp.int32),
            pltpu.SMEM((blocks, LANES), jnp.int32),
            pltpu.SemaphoreType.DMA((5,)),
            pltpu.SemaphoreType.DMA((PARTS,)),
        ],
        compiler_params=pltpu.CompilerParams(vmem_limit_bytes=WIDE_VMEM_BYTES),
        name="pack_rows",
    )(obs_owner.reshape(blocks, LANES), obs_cell.reshape(blocks, LANES), obs_misfit)


def edge_kernel(adj_ref, north_ref, south_ref, east_ref, west_ref):
    planes, rows, columns = adj_ref.shape
    north_ref[...] = adj_ref[:, 0, :].astype(jnp.bfloat16)
    south_ref[...] = adj_ref[:, rows - 1, :].astype(jnp.bfloat16)
    row = lax.broadcasted_iota(jnp.int32, (rows, LANES), 0)
    lane = lax.broadcasted_iota(jnp.int32, (rows, LANES), 1)
    for ref, start, at in ((east_ref, 0, 0), (west_ref, columns - LANES, LANES - 1)):
        line = jnp.zeros((rows, planes), jnp.float32)
        for r in range(rows):
            pick = ((lane == at) & (row == r)).astype(jnp.float32).astype(jnp.bfloat16)
            side = adj_ref[:, r, start : start + LANES].astype(jnp.bfloat16)
            line = line + lax.dot_general(
                pick, side, (((1,), (1,)), ((), ())), preferred_element_type=jnp.float32
            )
        ref[...] = line.astype(jnp.bfloat16)


def edges(adjoint):
    levels, fields, rows, columns = adjoint.shape
    planes = levels * fields
    vmem = pl.BlockSpec(memory_space=pltpu.VMEM)
    side = jax.ShapeDtypeStruct((rows, planes), jnp.bfloat16)
    row = jax.ShapeDtypeStruct((planes, columns), jnp.bfloat16)
    return pl.pallas_call(
        edge_kernel,
        out_shape=(row, row, side, side),
        in_specs=[vmem],
        out_specs=(vmem,) * 4,
        compiler_params=pltpu.CompilerParams(vmem_limit_bytes=WIDE_VMEM_BYTES),
        cost_estimate=pl.CostEstimate(flops=1000, bytes_accessed=100000, transcendentals=0),
        name="edges",
    )(adjoint.reshape(planes, rows, columns))


def local_kernel(
    adj_ref, flow_ref, mask_ref, mix_ref, local_hbm, weight_ref, hor_ref, coef_ref, sems,
):
    levels, fields, rows, columns = adj_ref.shape
    planes = levels * fields
    shape = (rows, columns)
    lane = lax.broadcasted_iota(jnp.int32, shape, 1)
    sub = lax.broadcasted_iota(jnp.int32, shape, 0)
    last_column, first_column = lane == columns - 1, lane == 0
    last_row, first_row = sub == rows - 1, sub == 0

    row = lax.broadcasted_iota(jnp.int32, (rows, LANES), 0)
    short_lane = lax.broadcasted_iota(jnp.int32, (rows, LANES), 1)
    repeat = (
        lax.broadcasted_iota(jnp.int32, (levels, planes), 1) // fields
        == lax.broadcasted_iota(jnp.int32, (levels, planes), 0)
    ).astype(jnp.float32)
    row_planes = planes // rows
    for place, start, at, half in ((0, columns - LANES, LANES - 1, 0.5), (planes, 0, 0, -0.5)):
        line = jnp.zeros((rows, levels), jnp.float32)
        for r in range(rows):
            pick = ((short_lane == at) & (row == r)).astype(jnp.float32)
            line = line + lax.dot_general(
                pick,
                flow_ref[:, 0, r, start : start + LANES],
                (((1,), (1,)), ((), ())),
                precision=lax.Precision.HIGHEST,
                preferred_element_type=jnp.float32,
            )
        line = jnp.dot(
            line, repeat, precision=lax.Precision.HIGHEST, preferred_element_type=jnp.float32
        )
        weight_ref[2 * row_planes, :, place : place + planes] = diffusion_rate + half * line

    def level(k, state):
        lower, ratio_prev = state
        mask = mask_ref[k].astype(jnp.float32)
        below = jnp.minimum(k + 1, levels - 1)
        mask_below = mask_ref[below].astype(jnp.float32)
        mix = mix_ref[jnp.minimum(k, levels - 2)]
        upper = jnp.where(k < levels - 1, mix * mask * mask_below, 0.0)
        inverse = 1.0 / (1.0 + lower + upper + lower * ratio_prev)
        ratio = -upper * inverse
        mask_inv = mask * inverse
        coef_ref[k] = mask_inv
        coef_ref[levels + k] = lower * inverse
        coef_ref[2 * levels + k] = ratio
        flow_along, flow_cross = flow_ref[k, 0], flow_ref[k, 1]
        north_weight = diffusion_rate + 0.5 * flow_cross[rows - 1 : rows, :]
        south_weight = diffusion_rate - 0.5 * flow_cross[0:1, :]
        centers, advects, alongs, crosses = [], [], [], []
        for f in range(fields):
            at = k * fields + f
            weight_ref[at // rows, pl.ds(at % rows, 1), :] = north_weight
            weight_ref[row_planes + at // rows, pl.ds(at % rows, 1), :] = south_weight
            x = adj_ref[k, f]
            east = jnp.where(last_column, 0.0, pltpu.roll(x, columns - 1, 1))
            west = jnp.where(first_column, 0.0, pltpu.roll(x, 1, 1))
            north = jnp.where(last_row, 0.0, pltpu.roll(x, rows - 1, 0))
            south = jnp.where(first_row, 0.0, pltpu.roll(x, 1, 0))
            along = 0.5 * (east - west)
            cross = 0.5 * (north - south)
            advect = (
                x
                + diffusion_rate * (east + west + north + south - 4.0 * x)
                + flow_along * along
                + flow_cross * cross
            )
            centers.append(x)
            advects.append(advect)
            alongs.append(along)
            crosses.append(cross)
        diverge = alongs[2] + crosses[3]
        buoy_along = thermal_coef * alongs[0] - haline_coef * alongs[1]
        buoy_cross = thermal_coef * crosses[0] - haline_coef * crosses[1]
        hor_ref[k * fields + 0] = mask_inv * (advects[0] - thermal_coef * couple_rate * diverge)
        hor_ref[k * fields + 1] = mask_inv * (advects[1] + haline_coef * couple_rate * diverge)
        hor_ref[k * fields + 2] = mask_inv * (advects[2] + coriolis * centers[3] + couple_rate * buoy_along)
        hor_ref[k * fields + 3] = mask_inv * (advects[3] - coriolis * centers[2] + couple_rate * buoy_cross)
        return upper, ratio

    zero = jnp.zeros(shape, jnp.float32)
    lax.fori_loop(0, levels, level, (zero, zero))
    copies = local_copies(local_hbm, (hor_ref, coef_ref), sems, False)
    for copy in copies:
        copy.start()
    for copy in copies:
        copy.wait()


def local_copies(local_hbm, refs, sems, inward):
    copies, at = [], 0
    for i, ref in enumerate(refs):
        part = local_hbm.at[pl.ds(at, ref.shape[0])]
        source, target = (part, ref) if inward else (ref, part)
        copies.append(pltpu.make_async_copy(source, target, sems.at[i]))
        at += ref.shape[0]
    return copies


def local_scratch(levels, fields, rows, columns):
    planes = levels * fields
    return [
        pltpu.VMEM((planes, rows, columns), jnp.float32),
        pltpu.VMEM((3 * levels, rows, columns), jnp.float32),
    ]


def local_part(adjoint, flow, land_mask, mixing):
    levels, fields, rows, columns = adjoint.shape
    vmem = pl.BlockSpec(memory_space=pltpu.VMEM)
    return pl.pallas_call(
        local_kernel,
        out_shape=(
            jax.ShapeDtypeStruct((LOCAL_PLANES, rows, columns), jnp.float32),
            jax.ShapeDtypeStruct((2 * levels * fields // rows + 1, rows, columns), jnp.float32),
        ),
        in_specs=[vmem] * 4,
        out_specs=(pl.BlockSpec(memory_space=pltpu.HBM), vmem),
        scratch_shapes=local_scratch(*adjoint.shape) + [pltpu.SemaphoreType.DMA((2,))],
        compiler_params=pltpu.CompilerParams(vmem_limit_bytes=LOCAL_VMEM_BYTES),
        cost_estimate=pl.CostEstimate(flops=1000, bytes_accessed=100000, transcendentals=0),
        name="local_part",
    )(adjoint, flow, land_mask, mixing)


def turned_edge(edge, code):
    planes = edge.shape[1]
    cosine = jnp.where(code == 0, 1.0, 0.0) - jnp.where(code == 2, 1.0, 0.0)
    sine = jnp.where(code == 1, 1.0, 0.0) - jnp.where(code == 3, 1.0, 0.0)
    field = lax.broadcasted_iota(jnp.int32, edge.shape, 1) & 3
    zonal = cosine * edge - sine * pltpu.roll(edge, planes - 1, 1)
    meridional = sine * pltpu.roll(edge, 1, 1) + cosine * edge
    return jnp.where(field == 2, zonal, jnp.where(field == 3, meridional, edge))


def edge_term(edge, weight, sign, axis, vector):
    planes = edge.shape[axis]
    field = lax.broadcasted_iota(jnp.int32, edge.shape, axis) & 3
    ahead = lambda n: pltpu.roll(edge, planes - n, axis)
    behind = lambda n: pltpu.roll(edge, n, axis)
    thermal = sign * 0.5 * thermal_coef * couple_rate
    haline = sign * 0.5 * haline_coef * couple_rate
    other = thermal * behind(vector) - haline * behind(vector - 1)
    mixed = jnp.where(field == 0, -thermal * ahead(vector), 0.0)
    mixed = jnp.where(field == 1, haline * ahead(vector - 1), mixed)
    mixed = jnp.where(field == vector, other, mixed)
    return weight * edge + mixed


def start_with_edges(
    acc, own_code, next_code, north_ref, south_ref, east_ref, west_ref, weight_ref
):
    rows, planes, columns = acc.shape
    row_planes = planes // rows
    weight_north = weight_ref[0:row_planes].reshape(planes, columns)
    weight_south = weight_ref[row_planes : 2 * row_planes].reshape(planes, columns)
    weight_east = weight_ref[2 * row_planes, :, 0:planes]
    weight_west = weight_ref[2 * row_planes, :, planes : 2 * planes]
    east = turned_edge(east_ref[...].astype(jnp.float32), (4 - next_code) & 3)
    west = turned_edge(west_ref[...].astype(jnp.float32), own_code)
    fill = jnp.zeros((LANES - rows, planes), jnp.float32)
    tall = lambda line: jnp.transpose(jnp.concatenate([line, fill], axis=0))
    east = tall(edge_term(east, weight_east, 1.0, 1, 2))
    west = tall(edge_term(west, weight_west, -1.0, 1, 2))
    north = edge_term(north_ref[...].astype(jnp.float32), weight_north, 1.0, 0, 3)
    south = edge_term(south_ref[...].astype(jnp.float32), weight_south, -1.0, 0, 3)
    lane = lax.broadcasted_iota(jnp.int32, (planes, LANES), 1)
    blank = jnp.zeros((planes, columns - 2 * LANES), jnp.float32)
    for c in range(rows):
        first = jnp.where(lane == 0, jnp.broadcast_to(west[:, c : c + 1], lane.shape), 0.0)
        last = jnp.where(lane == LANES - 1, jnp.broadcast_to(east[:, c : c + 1], lane.shape), 0.0)
        line = jnp.concatenate([first, blank, last], axis=1) if blank.shape[1] else (
            jnp.concatenate([first, last], axis=1)
        )
        if c == 0:
            line = line + south
        if c == rows - 1:
            line = line + north
        acc[c] = line


GATHER_BLOCKS = 1
ROW_PARTS = 4


def lane_order(head_f, line_ref, capacity):
    tiles = head_f.shape[0]
    pitch = capacity + HEAD_ROWS
    lane = lax.broadcasted_iota(jnp.int32, (1, LANES), 1)
    for t in range(tiles * pitch // LANES):
        line = jnp.zeros((1, LANES), jnp.float32)
        for source in range(tiles):
            start = source * pitch - t * LANES
            if start < LANES and start + capacity > 0:
                inside = (lane >= start) & (lane < start + capacity)
                line = jnp.where(inside, head_f[source : source + 1, :], line)
        line_ref[:, t * LANES : (t + 1) * LANES] = line


def finish_kernel(
    seam_ref, got_ref, heads_ref, north_ref, south_ref, east_ref, west_ref, weight_ref, local_hbm,
    out_hbm, acc, out_ref, hor_ref, coef_ref,
    head_f, row_line, column_line, sems, out_sems,
):
    slots, width = got_ref.shape
    tiles, pairs = heads_ref.shape[0], heads_ref.shape[1]
    capacity = slots // tiles - HEAD_ROWS
    levels, fields, rows, columns = out_ref.shape
    depth = slots // GATHER_BLOCKS
    copies = local_copies(local_hbm, (hor_ref, coef_ref), sems, True)
    for copy in copies:
        copy.start()
    along_rank = lax.axis_index("along")
    own_code = seam_ref[along_rank]
    next_code = seam_ref[lax.rem(along_rank + 1, seam_ref.shape[0])]
    start_with_edges(
        acc, own_code, next_code, north_ref, south_ref, east_ref, west_ref, weight_ref
    )

    heads = heads_ref[:, pairs - 1].astype(jnp.float32)
    for i, line_ref in enumerate((row_line, column_line)):
        head_f[i] = heads[:, i, :]
        lane_order(head_f.at[i], line_ref, capacity)
    column_id = lax.broadcasted_iota(jnp.int32, (columns, depth), 0).astype(jnp.float32)
    column_id = column_id.astype(jnp.bfloat16)
    zero = jnp.zeros((width, depth), jnp.bfloat16)

    def gather(i, carried):
        span = pl.ds(pl.multiple_of(i * depth, depth), depth)
        turned = jnp.transpose(got_ref[span, :])
        column_wide = jnp.broadcast_to(column_line[:, span], (columns, depth)).astype(jnp.bfloat16)
        onehot = jnp.where(
            column_id == column_wide, jnp.ones((), jnp.bfloat16), jnp.zeros((), jnp.bfloat16)
        )
        row_wide = jnp.broadcast_to(row_line[:, span], (width, depth)).astype(jnp.bfloat16)
        for start in range(0, rows, rows // ROW_PARTS):
            some = range(start, start + rows // ROW_PARTS)
            masked = jnp.concatenate(
                [jnp.where(row_wide == (c + 1), turned, zero) for c in some], axis=0
            )
            part = lax.dot_general(
                masked, onehot, (((1,), (1,)), ((), ())), preferred_element_type=jnp.float32
            )
            acc[start : start + rows // ROW_PARTS] += part.reshape(rows // ROW_PARTS, width, columns)
        return carried

    lax.fori_loop(0, GATHER_BLOCKS, gather, 0)

    copies[0].wait()
    copies[1].wait()

    def forward(q, previous):
        forcing = jnp.swapaxes(acc[:, pl.ds(pl.multiple_of(q * 8, 8), 8), :], 0, 1)
        state = list(previous)
        for i in range(8 // fields):
            k = q * (8 // fields) + i
            mask_inv, lower_inv = coef_ref[k], coef_ref[levels + k]
            for f in range(fields):
                state[f] = (
                    hor_ref[k * fields + f] + mask_inv * forcing[i * fields + f] + lower_inv * state[f]
                )
                out_ref[k, f] = state[f]
        return tuple(state)

    zero = jnp.zeros((rows, columns), jnp.float32)
    last = lax.fori_loop(0, levels * fields // 8, forward, (zero,) * fields)

    def backward(step, below):
        k = levels - 2 - step
        ratio = coef_ref[2 * levels + k]
        here = []
        for f in range(fields):
            here.append(out_ref[k, f] - ratio * below[f])
            out_ref[k, f] = here[f]
        return tuple(here)

    below = last
    out_copies = []
    part = levels // PARTS
    done = 0
    for i in range(PARTS):
        steps = part - 1 if i == 0 else part
        below = lax.fori_loop(done, done + steps, backward, below)
        done += steps
        span = pl.ds(levels - (i + 1) * part, part)
        copy = pltpu.make_async_copy(out_ref.at[span], out_hbm.at[span], out_sems.at[i])
        copy.start()
        out_copies.append(copy)
    for copy in out_copies:
        copy.wait()


def finish(seam_code, got, halos, weight, local, tiles, shape):
    slots, width = got.shape
    heads = got.reshape(tiles, slots // tiles // HEAD_ROWS, HEAD_ROWS, width)
    levels, fields, rows, columns = shape
    vmem = pl.BlockSpec(memory_space=pltpu.VMEM)
    hbm = pl.BlockSpec(memory_space=pltpu.HBM)
    return pl.pallas_call(
        finish_kernel,
        out_shape=jax.ShapeDtypeStruct(shape, jnp.float32),
        in_specs=[pl.BlockSpec(memory_space=pltpu.SMEM)] + [vmem] * 7 + [hbm],
        out_specs=hbm,
        scratch_shapes=[
            pltpu.VMEM((rows, levels * fields, columns), jnp.float32),
            pltpu.VMEM(shape, jnp.float32),
        ]
        + local_scratch(*shape)
        + [
            pltpu.VMEM((2, tiles, LANES), jnp.float32),
            pltpu.VMEM((1, slots), jnp.float32),
            pltpu.VMEM((1, slots), jnp.float32),
            pltpu.SemaphoreType.DMA((2,)),
            pltpu.SemaphoreType.DMA((PARTS,)),
        ],
        compiler_params=pltpu.CompilerParams(vmem_limit_bytes=LAST_VMEM_BYTES),
        name="finish",
    )(seam_code, got, heads, *halos, weight, local)


def per_device(adjoint, flow, land_mask, mixing, seam_code, obs_misfit, obs_owner, obs_cell):
    levels, fields, rows, columns = adjoint.shape
    along_count = lax.axis_size("along")
    cross_count = lax.axis_size("cross")
    devices = along_count * cross_count
    capacity = 2 * obs_misfit.shape[0] // devices
    packed = pack_rows(obs_owner, obs_cell, obs_misfit, devices, capacity)
    packed, adjoint = lax.optimization_barrier((packed, adjoint))
    slots, width = packed.shape
    pairs = packed.reshape(slots // HEAD_ROWS, HEAD_ROWS, width)
    got = lax.all_to_all(pairs, ("along", "cross"), split_axis=0, concat_axis=0, tiled=True)
    got = got.reshape(slots, width)

    ring_up = [(i, (i + 1) % along_count) for i in range(along_count)]
    ring_down = [(target, source) for source, target in ring_up]
    line_up = [(i, i + 1) for i in range(cross_count - 1)]
    line_down = [(target, source) for source, target in line_up]
    first_row, last_row, first_column, last_column = edges(adjoint)
    west = lax.ppermute(last_column, "along", ring_up)
    east = lax.ppermute(first_column, "along", ring_down)
    south = lax.ppermute(last_row, "cross", line_up)
    north = lax.ppermute(first_row, "cross", line_down)
    local, weight = local_part(adjoint, flow, land_mask, mixing)
    halos = (north, south, east, west)
    return finish(seam_code, got, halos, weight, local, devices, adjoint.shape)


def solution(mesh):
    return jax.shard_map(
        per_device,
        mesh=mesh,
        in_specs=(
            P(None, None, "cross", "along"),
            P(None, None, "cross", "along"),
            P(None, "cross", "along"),
            P(None, "cross", "along"),
            P(),
            P(("along", "cross"), None),
            P(("along", "cross"), None),
            P(("along", "cross")),
        ),
        out_specs=P(None, None, "cross", "along"),
        check_vma=False,
    )
```

```python
import functools

import jax
import jax.numpy as jnp
from jax import lax
from jax.experimental import pallas as pl
from jax.experimental.pallas import tpu as pltpu
from jax.sharding import PartitionSpec as P

diffusion_rate = 0.15
coriolis = 0.3
couple_rate = 0.3
thermal_coef = 0.8
haline_coef = 0.6

LANES = 128
HEAD_ROWS = 2
PARTS = 4
LAST_VMEM_BYTES = 44 * 1024 * 1024
LOCAL_VMEM_BYTES = 50 * 1024 * 1024
LOCAL_PLANES = 1536
WIDE_VMEM_BYTES = 61 * 1024 * 1024


def pack_kernel(
    owner_hbm, cell_hbm, rows_hbm, out_hbm,
    owner_ref, cell_ref, rows_ref, out_ref, stage, rows_f, slot_v, slot_s, sems, out_sems,
    *, tiles,
):
    block_rows = out_ref.shape[0] // tiles
    capacity = block_rows - HEAD_ROWS
    blocks = owner_ref.shape[0]
    half = blocks // 2
    owner_copy = pltpu.make_async_copy(owner_hbm, owner_ref, sems.at[0])
    cell_copy = pltpu.make_async_copy(cell_hbm, cell_ref, sems.at[1])
    rows_copy = pltpu.make_async_copy(rows_hbm, rows_ref, sems.at[2])
    owner_copy.start()
    cell_copy.start()
    rows_copy.start()
    tile_id = lax.broadcasted_iota(jnp.int32, (tiles, LANES), 0)
    low = lax.broadcasted_iota(jnp.int32, (LANES, 2 * LANES), 0)
    high = lax.broadcasted_iota(jnp.int32, (LANES, 2 * LANES), 1)
    count_with = ((low <= high) | (high >= LANES)).astype(jnp.float32).astype(jnp.bfloat16)
    device = lax.axis_index("along") * lax.axis_size("cross") + lax.axis_index("cross")
    place = lax.broadcasted_iota(jnp.int32, (LANES, LANES), 0) - device * block_rows
    place = (place & (LANES - 1)).astype(jnp.float32)
    carry = jnp.zeros((tiles, LANES), jnp.float32)
    total = jnp.zeros((tiles, 2 * LANES), jnp.float32)
    owner_copy.wait()
    cell_copy.wait()
    slot_copies = []
    for b in range(blocks):
        owner = owner_ref[b : b + 1, :]
        cell = cell_ref[b : b + 1, :]
        hit = (tile_id == owner).astype(jnp.float32)
        hit_narrow = hit.astype(jnp.bfloat16)
        counts = jnp.dot(hit_narrow, count_with, preferred_element_type=jnp.float32)
        rank = jnp.sum((counts[:, :LANES] + carry) * hit, axis=0, keepdims=True) - 1.0
        carry = carry + counts[:, LANES:]
        slot_v[b : b + 1, :] = owner * block_rows + rank.astype(jnp.int32)
        row_part = ((cell >> 8) + 1).astype(jnp.float32)
        column_part = (cell & 255).astype(jnp.float32)
        here = place == rank
        values = jnp.concatenate(
            [jnp.where(here, row_part, 0.0), jnp.where(here, column_part, 0.0)], axis=0
        ).astype(jnp.bfloat16)
        total = total + lax.dot_general(
            hit_narrow, values, (((1,), (1,)), ((), ())), preferred_element_type=jnp.float32
        )
        if (b + 1) % half == 0:
            span = pl.ds(b + 1 - half, half)
            copy = pltpu.make_async_copy(
                slot_v.at[span], slot_s.at[span], sems.at[3 + len(slot_copies)]
            )
            copy.start()
            slot_copies.append(copy)
    stage[pl.ds(capacity, tiles, stride=block_rows), :] = total[:, :LANES]
    stage[pl.ds(capacity + 1, tiles, stride=block_rows), :] = total[:, LANES:]
    rows_copy.wait()
    rows_f[...] = rows_ref[...].astype(jnp.float32)

    def scatter(b, carried):
        base = pl.multiple_of(b * LANES, LANES)
        for j in range(LANES):
            stage[pl.ds(slot_s[b, j], 1), :] = rows_f[pl.ds(base + j, 1), :]
        return carried

    for i, copy in enumerate(slot_copies):
        copy.wait()
        lax.fori_loop(i * half, (i + 1) * half, scatter, 0)

    step = out_ref.shape[0] // PARTS
    piece = capacity

    def narrow(i, carried):
        span = pl.ds(pl.multiple_of(i * piece, piece), piece)
        out_ref[span, :] = stage[span, :].astype(jnp.bfloat16)
        return carried

    out_copies = []
    for i in range(PARTS):
        lax.fori_loop(i * step // piece, (i + 1) * step // piece, narrow, 0, unroll=3)
        span = pl.ds(i * step, step)
        copy = pltpu.make_async_copy(out_ref.at[span], out_hbm.at[span], out_sems.at[i])
        copy.start()
        out_copies.append(copy)
    for copy in out_copies:
        copy.wait()


def pack_rows(obs_owner, obs_cell, obs_misfit, tiles, capacity):
    obs_rows, width = obs_misfit.shape
    blocks = obs_rows // LANES
    slots = tiles * (capacity + HEAD_ROWS)
    hbm = pl.BlockSpec(memory_space=pltpu.HBM)
    return pl.pallas_call(
        functools.partial(pack_kernel, tiles=tiles),
        out_shape=jax.ShapeDtypeStruct((slots, width), jnp.bfloat16),
        in_specs=[hbm] * 3,
        out_specs=hbm,
        scratch_shapes=[
            pltpu.VMEM((blocks, LANES), jnp.int32),
            pltpu.VMEM((blocks, LANES), jnp.int32),
            pltpu.VMEM((obs_rows, width), jnp.bfloat16),
            pltpu.VMEM((slots, width), jnp.bfloat16),
            pltpu.VMEM((slots, width), jnp.float32),
            pltpu.VMEM((obs_rows, width), jnp.float32),
            pltpu.VMEM((blocks, LANES), jnp.int32),
            pltpu.SMEM((blocks, LANES), jnp.int32),
            pltpu.SemaphoreType.DMA((5,)),
            pltpu.SemaphoreType.DMA((PARTS,)),
        ],
        compiler_params=pltpu.CompilerParams(vmem_limit_bytes=WIDE_VMEM_BYTES),
        name="pack_rows",
    )(obs_owner.reshape(blocks, LANES), obs_cell.reshape(blocks, LANES), obs_misfit)


def edge_kernel(adj_ref, north_ref, south_ref, east_ref, west_ref):
    planes, rows, columns = adj_ref.shape
    north_ref[...] = adj_ref[:, 0, :].astype(jnp.bfloat16)
    south_ref[...] = adj_ref[:, rows - 1, :].astype(jnp.bfloat16)
    row = lax.broadcasted_iota(jnp.int32, (rows, LANES), 0)
    lane = lax.broadcasted_iota(jnp.int32, (rows, LANES), 1)
    for ref, start, at in ((east_ref, 0, 0), (west_ref, columns - LANES, LANES - 1)):
        line = jnp.zeros((rows, planes), jnp.float32)
        for r in range(rows):
            pick = ((lane == at) & (row == r)).astype(jnp.float32).astype(jnp.bfloat16)
            side = adj_ref[:, r, start : start + LANES].astype(jnp.bfloat16)
            line = line + lax.dot_general(
                pick, side, (((1,), (1,)), ((), ())), preferred_element_type=jnp.float32
            )
        ref[...] = line.astype(jnp.bfloat16)


def edges(adjoint):
    levels, fields, rows, columns = adjoint.shape
    planes = levels * fields
    vmem = pl.BlockSpec(memory_space=pltpu.VMEM)
    side = jax.ShapeDtypeStruct((rows, planes), jnp.bfloat16)
    row = jax.ShapeDtypeStruct((planes, columns), jnp.bfloat16)
    return pl.pallas_call(
        edge_kernel,
        out_shape=(row, row, side, side),
        in_specs=[vmem],
        out_specs=(vmem,) * 4,
        compiler_params=pltpu.CompilerParams(vmem_limit_bytes=WIDE_VMEM_BYTES),
        cost_estimate=pl.CostEstimate(flops=1000, bytes_accessed=100000, transcendentals=0),
        name="edges",
    )(adjoint.reshape(planes, rows, columns))


def local_kernel(
    adj_ref, flow_ref, mask_ref, mix_ref, local_hbm, weight_ref, hor_ref, coef_ref, sems,
):
    levels, fields, rows, columns = adj_ref.shape
    planes = levels * fields
    shape = (rows, columns)
    lane = lax.broadcasted_iota(jnp.int32, shape, 1)
    sub = lax.broadcasted_iota(jnp.int32, shape, 0)
    last_column, first_column = lane == columns - 1, lane == 0
    last_row, first_row = sub == rows - 1, sub == 0

    row = lax.broadcasted_iota(jnp.int32, (rows, LANES), 0)
    short_lane = lax.broadcasted_iota(jnp.int32, (rows, LANES), 1)
    repeat = (
        lax.broadcasted_iota(jnp.int32, (levels, planes), 1) // fields
        == lax.broadcasted_iota(jnp.int32, (levels, planes), 0)
    ).astype(jnp.float32)
    row_planes = planes // rows
    for place, start, at, half in ((0, columns - LANES, LANES - 1, 0.5), (planes, 0, 0, -0.5)):
        line = jnp.zeros((rows, levels), jnp.float32)
        for r in range(rows):
            pick = ((short_lane == at) & (row == r)).astype(jnp.float32)
            line = line + lax.dot_general(
                pick,
                flow_ref[:, 0, r, start : start + LANES],
                (((1,), (1,)), ((), ())),
                precision=lax.Precision.HIGHEST,
                preferred_element_type=jnp.float32,
            )
        line = jnp.dot(
            line, repeat, precision=lax.Precision.HIGHEST, preferred_element_type=jnp.float32
        )
        weight_ref[2 * row_planes, :, place : place + planes] = diffusion_rate + half * line

    def level(k, state):
        lower, ratio_prev = state
        mask = mask_ref[k].astype(jnp.float32)
        below = jnp.minimum(k + 1, levels - 1)
        mask_below = mask_ref[below].astype(jnp.float32)
        mix = mix_ref[jnp.minimum(k, levels - 2)]
        upper = jnp.where(k < levels - 1, mix * mask * mask_below, 0.0)
        inverse = 1.0 / (1.0 + lower + upper + lower * ratio_prev)
        ratio = -upper * inverse
        mask_inv = mask * inverse
        coef_ref[k] = mask_inv
        coef_ref[levels + k] = lower * inverse
        coef_ref[2 * levels + k] = ratio
        flow_along, flow_cross = flow_ref[k, 0], flow_ref[k, 1]
        north_weight = diffusion_rate + 0.5 * flow_cross[rows - 1 : rows, :]
        south_weight = diffusion_rate - 0.5 * flow_cross[0:1, :]
        centers, advects, alongs, crosses = [], [], [], []
        for f in range(fields):
            at = k * fields + f
            weight_ref[at // rows, pl.ds(at % rows, 1), :] = north_weight
            weight_ref[row_planes + at // rows, pl.ds(at % rows, 1), :] = south_weight
            x = adj_ref[k, f]
            east = jnp.where(last_column, 0.0, pltpu.roll(x, columns - 1, 1))
            west = jnp.where(first_column, 0.0, pltpu.roll(x, 1, 1))
            north = jnp.where(last_row, 0.0, pltpu.roll(x, rows - 1, 0))
            south = jnp.where(first_row, 0.0, pltpu.roll(x, 1, 0))
            along = 0.5 * (east - west)
            cross = 0.5 * (north - south)
            advect = (
                x
                + diffusion_rate * (east + west + north + south - 4.0 * x)
                + flow_along * along
                + flow_cross * cross
            )
            centers.append(x)
            advects.append(advect)
            alongs.append(along)
            crosses.append(cross)
        diverge = alongs[2] + crosses[3]
        buoy_along = thermal_coef * alongs[0] - haline_coef * alongs[1]
        buoy_cross = thermal_coef * crosses[0] - haline_coef * crosses[1]
        hor_ref[k * fields + 0] = mask_inv * (advects[0] - thermal_coef * couple_rate * diverge)
        hor_ref[k * fields + 1] = mask_inv * (advects[1] + haline_coef * couple_rate * diverge)
        hor_ref[k * fields + 2] = mask_inv * (advects[2] + coriolis * centers[3] + couple_rate * buoy_along)
        hor_ref[k * fields + 3] = mask_inv * (advects[3] - coriolis * centers[2] + couple_rate * buoy_cross)
        return upper, ratio

    zero = jnp.zeros(shape, jnp.float32)
    lax.fori_loop(0, levels, level, (zero, zero))
    copies = local_copies(local_hbm, (hor_ref, coef_ref), sems, False)
    for copy in copies:
        copy.start()
    for copy in copies:
        copy.wait()


def local_copies(local_hbm, refs, sems, inward):
    copies, at = [], 0
    for i, ref in enumerate(refs):
        part = local_hbm.at[pl.ds(at, ref.shape[0])]
        source, target = (part, ref) if inward else (ref, part)
        copies.append(pltpu.make_async_copy(source, target, sems.at[i]))
        at += ref.shape[0]
    return copies


def local_scratch(levels, fields, rows, columns):
    planes = levels * fields
    return [
        pltpu.VMEM((planes, rows, columns), jnp.float32),
        pltpu.VMEM((3 * levels, rows, columns), jnp.float32),
    ]


def local_part(adjoint, flow, land_mask, mixing):
    levels, fields, rows, columns = adjoint.shape
    vmem = pl.BlockSpec(memory_space=pltpu.VMEM)
    return pl.pallas_call(
        local_kernel,
        out_shape=(
            jax.ShapeDtypeStruct((LOCAL_PLANES, rows, columns), jnp.float32),
            jax.ShapeDtypeStruct((2 * levels * fields // rows + 1, rows, columns), jnp.float32),
        ),
        in_specs=[vmem] * 4,
        out_specs=(pl.BlockSpec(memory_space=pltpu.HBM), vmem),
        scratch_shapes=local_scratch(*adjoint.shape) + [pltpu.SemaphoreType.DMA((2,))],
        compiler_params=pltpu.CompilerParams(vmem_limit_bytes=LOCAL_VMEM_BYTES),
        cost_estimate=pl.CostEstimate(flops=1000, bytes_accessed=100000, transcendentals=0),
        name="local_part",
    )(adjoint, flow, land_mask, mixing)


def turned_edge(edge, code):
    planes = edge.shape[1]
    cosine = jnp.where(code == 0, 1.0, 0.0) - jnp.where(code == 2, 1.0, 0.0)
    sine = jnp.where(code == 1, 1.0, 0.0) - jnp.where(code == 3, 1.0, 0.0)
    field = lax.broadcasted_iota(jnp.int32, edge.shape, 1) & 3
    zonal = cosine * edge - sine * pltpu.roll(edge, planes - 1, 1)
    meridional = sine * pltpu.roll(edge, 1, 1) + cosine * edge
    return jnp.where(field == 2, zonal, jnp.where(field == 3, meridional, edge))


def edge_term(edge, weight, sign, axis, vector):
    planes = edge.shape[axis]
    field = lax.broadcasted_iota(jnp.int32, edge.shape, axis) & 3
    ahead = lambda n: pltpu.roll(edge, planes - n, axis)
    behind = lambda n: pltpu.roll(edge, n, axis)
    thermal = sign * 0.5 * thermal_coef * couple_rate
    haline = sign * 0.5 * haline_coef * couple_rate
    other = thermal * behind(vector) - haline * behind(vector - 1)
    mixed = jnp.where(field == 0, -thermal * ahead(vector), 0.0)
    mixed = jnp.where(field == 1, haline * ahead(vector - 1), mixed)
    mixed = jnp.where(field == vector, other, mixed)
    return weight * edge + mixed


def start_with_edges(
    acc, own_code, next_code, north_ref, south_ref, east_ref, west_ref, weight_ref
):
    rows, planes, columns = acc.shape
    row_planes = planes // rows
    weight_north = weight_ref[0:row_planes].reshape(planes, columns)
    weight_south = weight_ref[row_planes : 2 * row_planes].reshape(planes, columns)
    weight_east = weight_ref[2 * row_planes, :, 0:planes]
    weight_west = weight_ref[2 * row_planes, :, planes : 2 * planes]
    east = turned_edge(east_ref[...].astype(jnp.float32), (4 - next_code) & 3)
    west = turned_edge(west_ref[...].astype(jnp.float32), own_code)
    fill = jnp.zeros((LANES - rows, planes), jnp.float32)
    tall = lambda line: jnp.transpose(jnp.concatenate([line, fill], axis=0))
    east = tall(edge_term(east, weight_east, 1.0, 1, 2))
    west = tall(edge_term(west, weight_west, -1.0, 1, 2))
    north = edge_term(north_ref[...].astype(jnp.float32), weight_north, 1.0, 0, 3)
    south = edge_term(south_ref[...].astype(jnp.float32), weight_south, -1.0, 0, 3)
    lane = lax.broadcasted_iota(jnp.int32, (planes, LANES), 1)
    blank = jnp.zeros((planes, columns - 2 * LANES), jnp.float32)
    for c in range(rows):
        first = jnp.where(lane == 0, jnp.broadcast_to(west[:, c : c + 1], lane.shape), 0.0)
        last = jnp.where(lane == LANES - 1, jnp.broadcast_to(east[:, c : c + 1], lane.shape), 0.0)
        line = jnp.concatenate([first, blank, last], axis=1) if blank.shape[1] else (
            jnp.concatenate([first, last], axis=1)
        )
        if c == 0:
            line = line + south
        if c == rows - 1:
            line = line + north
        acc[c] = line


GATHER_BLOCKS = 1
ROW_PARTS = 8


def lane_order(head_f, line_ref, capacity):
    tiles = head_f.shape[0]
    pitch = capacity + HEAD_ROWS
    lane = lax.broadcasted_iota(jnp.int32, (1, LANES), 1)
    for t in range(tiles * pitch // LANES):
        line = jnp.zeros((1, LANES), jnp.float32)
        for source in range(tiles):
            start = source * pitch - t * LANES
            if start < LANES and start + capacity > 0:
                inside = (lane >= start) & (lane < start + capacity)
                line = jnp.where(inside, head_f[source : source + 1, :], line)
        line_ref[:, t * LANES : (t + 1) * LANES] = line


def finish_kernel(
    seam_ref, got_ref, heads_ref, north_ref, south_ref, east_ref, west_ref, weight_ref, local_hbm,
    out_hbm, acc, out_ref, hor_ref, coef_ref,
    head_f, row_line, column_line, sems, out_sems,
):
    slots, width = got_ref.shape
    tiles, pairs = heads_ref.shape[0], heads_ref.shape[1]
    capacity = slots // tiles - HEAD_ROWS
    levels, fields, rows, columns = out_ref.shape
    depth = slots // GATHER_BLOCKS
    copies = local_copies(local_hbm, (hor_ref, coef_ref), sems, True)
    for copy in copies:
        copy.start()
    along_rank = lax.axis_index("along")
    own_code = seam_ref[along_rank]
    next_code = seam_ref[lax.rem(along_rank + 1, seam_ref.shape[0])]
    start_with_edges(
        acc, own_code, next_code, north_ref, south_ref, east_ref, west_ref, weight_ref
    )

    heads = heads_ref[:, pairs - 1].astype(jnp.float32)
    for i, line_ref in enumerate((row_line, column_line)):
        head_f[i] = heads[:, i, :]
        lane_order(head_f.at[i], line_ref, capacity)
    column_id = lax.broadcasted_iota(jnp.int32, (columns, depth), 0).astype(jnp.float32)
    column_id = column_id.astype(jnp.bfloat16)
    zero = jnp.zeros((width, depth), jnp.bfloat16)

    def gather(i, carried):
        span = pl.ds(pl.multiple_of(i * depth, depth), depth)
        turned = jnp.transpose(got_ref[span, :])
        column_wide = jnp.broadcast_to(column_line[:, span], (columns, depth)).astype(jnp.bfloat16)
        onehot = jnp.where(
            column_id == column_wide, jnp.ones((), jnp.bfloat16), jnp.zeros((), jnp.bfloat16)
        )
        row_wide = jnp.broadcast_to(row_line[:, span], (width, depth)).astype(jnp.bfloat16)
        for start in range(0, rows, rows // ROW_PARTS):
            some = range(start, start + rows // ROW_PARTS)
            masked = jnp.concatenate(
                [jnp.where(row_wide == (c + 1), turned, zero) for c in some], axis=0
            )
            part = lax.dot_general(
                masked, onehot, (((1,), (1,)), ((), ())), preferred_element_type=jnp.float32
            )
            acc[start : start + rows // ROW_PARTS] += part.reshape(rows // ROW_PARTS, width, columns)
        return carried

    lax.fori_loop(0, GATHER_BLOCKS, gather, 0)

    copies[0].wait()
    copies[1].wait()

    def forward(q, previous):
        forcing = jnp.swapaxes(acc[:, pl.ds(pl.multiple_of(q * 8, 8), 8), :], 0, 1)
        state = list(previous)
        for i in range(8 // fields):
            k = q * (8 // fields) + i
            mask_inv, lower_inv = coef_ref[k], coef_ref[levels + k]
            for f in range(fields):
                state[f] = (
                    hor_ref[k * fields + f] + mask_inv * forcing[i * fields + f] + lower_inv * state[f]
                )
                out_ref[k, f] = state[f]
        return tuple(state)

    zero = jnp.zeros((rows, columns), jnp.float32)
    last = lax.fori_loop(0, levels * fields // 8, forward, (zero,) * fields)

    def backward(step, below):
        k = levels - 2 - step
        ratio = coef_ref[2 * levels + k]
        here = []
        for f in range(fields):
            here.append(out_ref[k, f] - ratio * below[f])
            out_ref[k, f] = here[f]
        return tuple(here)

    below = last
    out_copies = []
    part = levels // PARTS
    done = 0
    for i in range(PARTS):
        steps = part - 1 if i == 0 else part
        below = lax.fori_loop(done, done + steps, backward, below)
        done += steps
        span = pl.ds(levels - (i + 1) * part, part)
        copy = pltpu.make_async_copy(out_ref.at[span], out_hbm.at[span], out_sems.at[i])
        copy.start()
        out_copies.append(copy)
    for copy in out_copies:
        copy.wait()


def finish(seam_code, got, halos, weight, local, tiles, shape):
    slots, width = got.shape
    heads = got.reshape(tiles, slots // tiles // HEAD_ROWS, HEAD_ROWS, width)
    levels, fields, rows, columns = shape
    vmem = pl.BlockSpec(memory_space=pltpu.VMEM)
    hbm = pl.BlockSpec(memory_space=pltpu.HBM)
    return pl.pallas_call(
        finish_kernel,
        out_shape=jax.ShapeDtypeStruct(shape, jnp.float32),
        in_specs=[pl.BlockSpec(memory_space=pltpu.SMEM)] + [vmem] * 7 + [hbm],
        out_specs=hbm,
        scratch_shapes=[
            pltpu.VMEM((rows, levels * fields, columns), jnp.float32),
            pltpu.VMEM(shape, jnp.float32),
        ]
        + local_scratch(*shape)
        + [
            pltpu.VMEM((2, tiles, LANES), jnp.float32),
            pltpu.VMEM((1, slots), jnp.float32),
            pltpu.VMEM((1, slots), jnp.float32),
            pltpu.SemaphoreType.DMA((2,)),
            pltpu.SemaphoreType.DMA((PARTS,)),
        ],
        compiler_params=pltpu.CompilerParams(vmem_limit_bytes=LAST_VMEM_BYTES),
        name="finish",
    )(seam_code, got, heads, *halos, weight, local)


def per_device(adjoint, flow, land_mask, mixing, seam_code, obs_misfit, obs_owner, obs_cell):
    levels, fields, rows, columns = adjoint.shape
    along_count = lax.axis_size("along")
    cross_count = lax.axis_size("cross")
    devices = along_count * cross_count
    capacity = 2 * obs_misfit.shape[0] // devices
    packed = pack_rows(obs_owner, obs_cell, obs_misfit, devices, capacity)
    packed, adjoint = lax.optimization_barrier((packed, adjoint))
    slots, width = packed.shape
    pairs = packed.reshape(slots // HEAD_ROWS, HEAD_ROWS, width)
    got = lax.all_to_all(pairs, ("along", "cross"), split_axis=0, concat_axis=0, tiled=True)
    got = got.reshape(slots, width)

    ring_up = [(i, (i + 1) % along_count) for i in range(along_count)]
    ring_down = [(target, source) for source, target in ring_up]
    line_up = [(i, i + 1) for i in range(cross_count - 1)]
    line_down = [(target, source) for source, target in line_up]
    first_row, last_row, first_column, last_column = edges(adjoint)
    west = lax.ppermute(last_column, "along", ring_up)
    east = lax.ppermute(first_column, "along", ring_down)
    south = lax.ppermute(last_row, "cross", line_up)
    north = lax.ppermute(first_row, "cross", line_down)
    local, weight = local_part(adjoint, flow, land_mask, mixing)
    halos = (north, south, east, west)
    return finish(seam_code, got, halos, weight, local, devices, adjoint.shape)


def solution(mesh):
    return jax.shard_map(
        per_device,
        mesh=mesh,
        in_specs=(
            P(None, None, "cross", "along"),
            P(None, None, "cross", "along"),
            P(None, "cross", "along"),
            P(None, "cross", "along"),
            P(),
            P(("along", "cross"), None),
            P(("along", "cross"), None),
            P(("along", "cross")),
        ),
        out_specs=P(None, None, "cross", "along"),
        check_vma=False,
    )
```
